128 devices in a mesh: dp: 32 (over x_lo, y, z), tensor: 4 (over x_hi, core).
Axes of the slice: x: 4 (x_hi: 2, x_lo: 2; x = x_hi * 2 + x_lo), y: 4, z: 4, core: 2. Of those that a mesh axis runs over, the one named last changes fastest.
Arguments:
- tokens: bfloat16 [8192, 1024], P('dp')
- segments: int32 [8192], P('dp'), may hold values from 0 to 4, as said below
- routes: int32 [8192], P('dp'), may hold values from 0 to 1, as said below
- slot_table: int32 [32, 2, 128], P('dp'), may hold values from 0 to 256, as said below
- ln_gain: bfloat16 [1024], replicated, may hold values from 0.5 to 1.5
- ln_shift: bfloat16 [1024], replicated, may hold values from -1 to 1
- qkv_proj: bfloat16 [3, 1024, 1024], P(None, None, 'tensor'), may hold values from -0.25 to 0.25
- qv_bias: bfloat16 [2, 1024], P(None, 'tensor'), may hold values from -1.5 to 1.5
- out_proj: bfloat16 [1024, 1024], P('tensor'), may hold values from -0.375 to 0.375
- out_bias: bfloat16 [1024], replicated, may hold values from -1 to 1
- centroids: bfloat16 [2, 1024], replicated, may hold values from -0.0625 to 0.0625
- ffn_gain: bfloat16 [2, 2, 1024], replicated, may hold values from 0.5 to 1.5
- ffn_shift: bfloat16 [2, 2, 1024], replicated, may hold values from -1 to 1
- up_proj: bfloat16 [2, 2, 1024, 4096], P(None, None, None, 'tensor'), may hold values from -0.1875 to 0.1875
- up_bias: bfloat16 [2, 2, 4096], P(None, None, 'tensor'), may hold values from -1 to 1
- down_proj: bfloat16 [2, 2, 4096, 1024], P(None, None, 'tensor'), may hold values from -0.125 to 0.125
- down_bias: bfloat16 [2, 2, 1024], replicated, may hold values from -0.5 to 0.5
- cotangent: bfloat16 [8192, 1024], P('dp'), may hold values from -6 to 6
Outputs:
- result: bfloat16 [8192, 1024], P('dp')
- tokens_grad: bfloat16 [8192, 1024], P('dp')
- ln_gain_grad: float32 [1024], P('dp')
- ln_shift_grad: float32 [1024], P('dp')
- qkv_proj_grad: float32 [3, 1024, 1024], P(None, 'dp', 'tensor')
- qv_bias_grad: float32 [2, 1024], P(None, 'tensor')
- out_proj_grad: float32 [1024, 1024], P('tensor', 'dp')
- out_bias_grad: float32 [1024], P('dp')
- centroids_grad: float32 [2, 1024], P(None, 'dp')
- ffn_gain_grad: float32 [2, 2, 1024], P(None, None, 'dp')
- ffn_shift_grad: float32 [2, 2, 1024], P(None, None, 'dp')
- up_proj_grad: float32 [2, 2, 1024, 4096], P(None, None, 'dp', 'tensor')
- up_bias_grad: float32 [2, 2, 4096], P(None, None, 'tensor')
- down_proj_grad: float32 [2, 2, 4096, 1024], P(None, None, 'tensor', 'dp')
- down_bias_grad: float32 [2, 2, 1024], P(None, None, 'dp')
- rms_values: float32 [4], replicated
The draws below stay inside these ranges and needn't reach their ends.
Inputs may be any that keep to these rules, and one draw needn't show every extreme that they name: `segments`: within each pack of 256 tokens the valid tokens come first, numbered from 1 upward and never falling; the rest of the pack is padding, numbered 0. The share of valid tokens falls along the packs from nearly all of the first to about a third of the last. A pack holds at most 4 documents, and the first pack holds 4. `routes`: the route of a valid token is the expert of its slot; that of padding is arbitrary. slot_table[p, e, c] is the position within pack p of the c-th valid token of that pack routed to e, in order of position, or 256 where fewer tokens are routed to e; every valid token stands in exactly one slot, padding in none; in the first pack one expert fills all 128 slots.
All inputs are finite; a program needn't handle non-finite values.
Results may differ from the reference program's by a relative error of at most 0.014.
The reference program's roundings to bfloat16 on the way count: a program that leaves them out, or rounds other values in their place, can miss the bound.
Values sent between devices are 32-bit elements; how exact they have to be, the bound alone decides.
A program may use at most 256 MiB of HBM per device.

```python
import jax
import jax.numpy as jnp
from jax import lax

D = 1024
H = 16
HD = 64
FF = 4096
E = 2
TOK_DEV = 256
CAP = 128
PACKS = 32
TOKENS = 8192


def draw_tokens(key, part):
    row_key, column_key, base_key = jax.random.split(key, 3)
    pack_of_row = jnp.arange(TOKENS, dtype=jnp.int32) // TOK_DEV
    level = pack_of_row.astype(jnp.float32) / max(PACKS - 1, 1)
    row_scale = jnp.exp(jax.random.uniform(row_key, (TOKENS, 1), minval=-1.15, maxval=1.15))
    column_scale = jnp.exp(jax.random.uniform(column_key, (1, D), minval=-0.55, maxval=0.55))
    noise = jax.random.normal(base_key, (TOKENS, D))
    pack_scale = jnp.exp2(level)
    return (noise * row_scale * column_scale * pack_scale[:, None] / 1.6).astype(jnp.bfloat16)


def route_tables(key):

    def one_pack(pack_index):
        pack_key = jax.random.fold_in(key, 7001 + pack_index)
        pack_keys = jax.random.split(pack_key, 6)
        position = jnp.arange(TOK_DEV, dtype=jnp.int32)
        padding_cut = 2 * TOK_DEV * pack_index // (3 * max(PACKS - 1, 1))
        live_count = TOK_DEV - padding_cut - jax.random.randint(pack_keys[0], (), 0, TOK_DEV // 16 + 1)
        is_live = position < live_count
        random_starts = jax.random.randint(pack_keys[1], (TOK_DEV,), 0, 128) == 0
        quarter_starts = position % (TOK_DEV // 4) == 0
        starts = (random_starts | quarter_starts) & (position > 0)
        segment_ids = jnp.where(is_live, jnp.minimum(1 + jnp.cumsum(starts.astype(jnp.int32)), 4), 0)
        shuffled = jax.random.permutation(pack_keys[2], TOK_DEV).astype(jnp.int32)
        ranking = jnp.where(is_live, shuffled, TOK_DEV + position)
        ordering = jnp.argsort(ranking)
        token_rank = jnp.zeros((TOK_DEV,), jnp.int32).at[ordering].set(position)
        busiest = jax.random.randint(pack_keys[3], (), 0, E)
        others = (busiest + 1 + jax.random.randint(pack_keys[4], (TOK_DEV,), 0, E - 1)) % E
        routed = jnp.where(token_rank < CAP, busiest, others)
        route_ids = jnp.where(is_live, routed, jax.random.randint(pack_keys[5], (TOK_DEV,), 0, E))
        member = (route_ids[:, None] == jnp.arange(E, dtype=jnp.int32)[None, :]) & is_live[:, None]
        within = jnp.cumsum(member.astype(jnp.int32), axis=0) - 1
        slot_place = jnp.sum(jnp.where(member, within, 0), axis=1)
        target = jnp.where(is_live, route_ids * CAP + slot_place, E * CAP)
        table = jnp.full((E * CAP,), TOK_DEV, jnp.int32).at[target].set(position, mode='drop')
        return (segment_ids.astype(jnp.int32), route_ids.astype(jnp.int32), table.reshape(E, CAP))
    return jax.vmap(one_pack)(jnp.arange(PACKS, dtype=jnp.int32))


def draw_segments(key, part):
    segment_ids, route_ids, table = route_tables(key)
    return segment_ids.reshape(TOKENS)


def draw_routes(key, part):
    segment_ids, route_ids, table = route_tables(key)
    return route_ids.reshape(TOKENS)


def draw_slot_table(key, part):
    segment_ids, route_ids, table = route_tables(key)
    return table


def with_spikes(values, own_key, source, target, blocks, factor):
    owner, partner = [(jnp.arange(values.shape[dim]) // (values.shape[dim] // blocks)).reshape([-1 if axis == dim else 1 for axis in range(values.ndim)]) for dim in (source, target)]
    chosen = jax.random.permutation(own_key, blocks)[partner]
    strong = (owner == chosen) | (owner == (partner + blocks // 2) % blocks)
    return jnp.where(strong, factor * values, values)


def level_of(rng, extent, shards, least, high):
    level = 1.0
    for dim, parts in shards:
        heights = jax.random.uniform(jax.random.fold_in(jax.random.fold_in(rng, 6), dim), (parts,), jnp.float32, least / len(shards), high / len(shards))
        level = level * jnp.repeat(jnp.exp(heights), extent[dim] // parts).reshape((-1,) + (1,) * (len(extent) - 1 - dim))
    return level


def bell_draw(rng, dims, scale, limit, shards=(), held_as=jnp.bfloat16):
    level = level_of(rng, dims, shards, -0.22, 0.18) if shards else 1.0
    entries = jax.random.normal(rng, dims, jnp.float32) * scale * level
    return jnp.minimum(jnp.maximum(entries, -limit), limit).astype(held_as)


def noise_with(stream_key, shape, deviation, most, pieces, heavy, kind=jnp.bfloat16):
    array = deviation * jax.random.normal(stream_key, shape, jnp.float32)
    if pieces:
        array = array * level_of(stream_key, shape, pieces, -0.22, 0.18)
    return jnp.clip(with_spikes(array, jax.random.fold_in(stream_key, 3), *heavy), -most, most).astype(kind)


def setup_inputs(seed: int = 0) -> dict:
    key_list = jax.random.split(jax.random.key(seed), 19)
    tokens = draw_tokens(jax.random.fold_in(key_list[18], 71), 0)
    segments = draw_segments(jax.random.fold_in(key_list[18], 71), 0)
    routes = draw_routes(jax.random.fold_in(key_list[18], 71), 0)
    slot_table = draw_slot_table(jax.random.fold_in(key_list[18], 71), 0)
    ln_gain = jnp.clip(1.0 + 0.1 * jax.random.normal(key_list[4], (D,), jnp.float32), 0.5, 1.5).astype(jnp.bfloat16)
    ln_shift = bell_draw(key_list[5], (D,), 0.2, 1.0)
    qkv_proj = bell_draw(key_list[6], (3, D, H * HD), (D // 2) ** -0.5, 0.25, ((2, 4),))
    qv_bias = bell_draw(key_list[7], (2, H * HD), 0.3, 1.5, ((1, 4),))
    out_proj = bell_draw(key_list[8], (H * HD, D), (H * HD // 4) ** -0.5, 0.375, ((0, 4),))
    out_bias = bell_draw(key_list[9], (D,), 0.2, 1.0)
    centroids = bell_draw(key_list[10], (E, D), (8 * D) ** -0.5, 0.0625)
    ffn_gain = jnp.clip(1.0 + 0.1 * jax.random.normal(key_list[11], (E, 2, D), jnp.float32), 0.5, 1.5).astype(jnp.bfloat16)
    ffn_shift = bell_draw(key_list[12], (E, 2, D), 0.2, 1.0)
    up_proj = bell_draw(key_list[13], (E, 2, D, FF), D ** -0.5, 0.1875, ((3, 4),))
    up_bias = bell_draw(key_list[14], (E, 2, FF), 0.2, 1.0, ((2, 4),))
    down_proj = bell_draw(key_list[15], (E, 2, FF, D), (FF // 2) ** -0.5, 0.125, ((2, 4),))
    down_bias = bell_draw(key_list[16], (E, 2, D), 0.1, 0.5)
    cotangent = noise_with(key_list[17], (TOKENS, D), 1.0, 6.0, ((0, 32),), (0, 1, 32, 2.75))
    return dict(tokens=tokens, segments=segments, routes=routes, slot_table=slot_table, ln_gain=ln_gain, ln_shift=ln_shift, qkv_proj=qkv_proj, qv_bias=qv_bias, out_proj=out_proj, out_bias=out_bias, centroids=centroids, ffn_gain=ffn_gain, ffn_shift=ffn_shift, up_proj=up_proj, up_bias=up_bias, down_proj=down_proj, down_bias=down_bias, cotangent=cotangent)


@jax.custom_vjp
def low(v):
    return lax.optimization_barrier(v.astype(jnp.bfloat16)).astype(jnp.float32)

@jax.custom_vjp
def low_back(v):
    return v

def low_keep(v):
    return (low(v), None)

def low_pass(kept, grad):
    return (grad,)

def back_keep(v):
    return (v, None)

def back_low(kept, grad):
    return (low(grad),)
low.defvjp(low_keep, low_pass)
low_back.defvjp(back_keep, back_low)
norm_eps = 1e-05
highest = lax.Precision.HIGHEST

def dot_high(left, right):
    return jnp.dot(left, right, precision=highest)

def layer_norm(inputs, norm_gain, norm_shift):
    center = inputs - lax.optimization_barrier(jnp.mean(inputs, axis=-1, keepdims=True))
    spread = lax.optimization_barrier(jnp.mean(center * center, axis=-1, keepdims=True))
    return center * lax.rsqrt(spread + norm_eps) * norm_gain + norm_shift

def pack_forward(params, tokens, segments, routes, slot_table):
    ln_gain, ln_shift, qkv_proj, qv_bias, out_proj, out_bias, centroids, ffn_gain, ffn_shift, up_proj, up_bias, down_proj, down_bias = params
    length = tokens.shape[0]
    position = jnp.arange(length, dtype=jnp.int32)
    is_valid = (segments != 0).astype(jnp.float32)
    normed = low(layer_norm(tokens, ln_gain, ln_shift))
    query_low = low(low_back(dot_high(normed, qkv_proj[0]) + qv_bias[0])).reshape(length, H, HD)
    keyed_low = low(low_back(dot_high(normed, qkv_proj[1]))).reshape(length, H, HD)
    value_low = low(low_back(dot_high(normed, qkv_proj[2]) + qv_bias[1])).reshape(length, H, HD)
    scores = low_back(jnp.einsum('qhd,khd->hqk', query_low, keyed_low, precision=highest) * HD ** (-0.5))
    allowed = (segments[:, None] == segments[None, :]) & (position[None, :] <= position[:, None]) & (segments[:, None] != 0)
    masked = jnp.where(allowed[None], scores, -1e+30)
    row_top = lax.optimization_barrier(jnp.max(masked, axis=-1, keepdims=True))
    exponent = jnp.where(allowed[None], jnp.exp(masked - row_top), 0.0)
    row_total = lax.optimization_barrier(jnp.sum(exponent, axis=-1, keepdims=True)) + (1.0 - is_valid)[None, :, None]
    attn_probs = low(exponent / row_total)
    attn_mixed = jnp.einsum('hqk,khd->qhd', attn_probs, value_low, precision=highest).reshape(length, H * HD)
    attn_mixed = low(low_back(attn_mixed))
    branch = low_back(dot_high(attn_mixed, out_proj) + out_bias)
    hidden = tokens + branch
    route_hot = (routes[:, None] == jnp.arange(E, dtype=jnp.int32)[None, :]).astype(jnp.float32)
    logits = lax.optimization_barrier(jnp.sum(hidden * dot_high(route_hot, centroids), axis=-1))
    gating = jax.nn.sigmoid(logits) * is_valid
    flat_slots = slot_table.reshape(-1)
    dispatch = (flat_slots[:, None] == position[None, :]).astype(jnp.float32)
    filled = (flat_slots < length).astype(jnp.float32)[:, None]
    expert_rows = dot_high(dispatch, hidden)
    row_sums = []
    for sublayer in range(2):
        current = expert_rows.reshape(E, CAP, D)
        normed_e = low(layer_norm(current, ffn_gain[:, sublayer][:, None, :], ffn_shift[:, sublayer][:, None, :]))
        pre_act = low_back(jnp.einsum('ecd,edf->ecf', normed_e, up_proj[:, sublayer], precision=highest) + up_bias[:, sublayer][:, None, :])
        act_low = low(jax.nn.gelu(pre_act, approximate=True))
        branch_out = low_back(jnp.einsum('ecf,efd->ecd', act_low, down_proj[:, sublayer], precision=highest) + down_bias[:, sublayer][:, None, :])
        expert_rows = (current + branch_out).reshape(E * CAP, D)
        row_sums.append(jnp.sum(expert_rows * expert_rows * filled))
    combined = dot_high(dispatch.T, expert_rows)
    result = hidden + gating[:, None] * combined
    valid_col = is_valid[:, None]
    stat_sums = jnp.stack([jnp.sum(hidden * hidden * valid_col), row_sums[0], row_sums[1], jnp.sum(result * result * valid_col), jnp.sum(is_valid)])
    return (result, stat_sums)

def reference(tokens, segments, routes, slot_table, ln_gain, ln_shift, qkv_proj, qv_bias, out_proj, out_bias, centroids, ffn_gain, ffn_shift, up_proj, up_bias, down_proj, down_bias, cotangent):
    params = tuple((weight_arg.astype(jnp.float32) for weight_arg in (ln_gain, ln_shift, qkv_proj, qv_bias, out_proj, out_bias, centroids, ffn_gain, ffn_shift, up_proj, up_bias, down_proj, down_bias)))

    def one_pack(running, pack_inputs):
        grad_sums, stat_total = running
        pack_tokens, pack_segments, pack_routes, pack_slots, pack_cot = pack_inputs

        def closed(pack_rows, weight_set):
            return pack_forward(weight_set, pack_rows, pack_segments, pack_routes, pack_slots)
        result, pullback, stat_sums = jax.vjp(closed, pack_tokens, params, has_aux=True)
        token_grad, weight_grads = pullback(pack_cot)
        grad_sums = jax.tree.map(jnp.add, grad_sums, weight_grads)
        return ((grad_sums, stat_total + stat_sums), (result, token_grad))
    start = (jax.tree.map(jnp.zeros_like, params), jnp.zeros((5,), jnp.float32))
    packs_in = (tokens.astype(jnp.float32).reshape(PACKS, TOK_DEV, D), segments.reshape(PACKS, TOK_DEV), routes.reshape(PACKS, TOK_DEV), slot_table, cotangent.astype(jnp.float32).reshape(PACKS, TOK_DEV, D))
    (grad_sums, stat_total), (results, token_grads) = lax.scan(one_pack, start, packs_in)
    rms_values = jnp.sqrt(stat_total[:4] / (stat_total[4] * D))
    return (results.reshape(TOKENS, D).astype(jnp.bfloat16), token_grads.reshape(TOKENS, D).astype(jnp.bfloat16), grad_sums[0], grad_sums[1], grad_sums[2], grad_sums[3], grad_sums[4], grad_sums[5], grad_sums[6], grad_sums[7], grad_sums[8], grad_sums[9], grad_sums[10], grad_sums[11], grad_sums[12], rms_values)
```

```python
import jax
import jax.numpy as jnp
from jax import lax
from jax.experimental import pallas as pl
from jax.experimental.pallas import tpu as pltpu
from jax.sharding import PartitionSpec as P

HD = 64
MESH = pl.DeviceIdType.MESH
VM = pltpu.VMEM
F32 = jnp.float32
BF = jnp.bfloat16


norm_eps = 1e-05
highest = lax.Precision.HIGHEST


class Here:
    def __init__(self):
        d = lax.axis_index("dp")
        t = lax.axis_index("tensor")
        self.x, self.y, self.z = d // 16, (d // 4) % 4, d % 4
        self.h, self.c = t // 2, t % 2

    def dev(self, x=None, y=None, z=None, h=None, c=None):
        x = self.x if x is None else x
        y = self.y if y is None else y
        z = self.z if z is None else z
        h = self.h if h is None else h
        c = self.c if c is None else c
        return (x * 16 + y * 4 + z, h * 2 + c)

    def ring(self, axis, step, c=None):
        p = (getattr(self, axis) + step) % 4
        return self.dev(c=c, **{axis: p})


def greet(devices):
    bar = pltpu.get_barrier_semaphore()
    for dev in devices:
        pl.semaphore_signal(bar, inc=1, device_id=dev, device_id_type=MESH)
    pl.semaphore_wait(bar, len(devices))


class Sems:
    def __init__(self, send, recv):
        self.send, self.recv, self.n = send, recv, 0

    def copy(self, src, dst, dev):
        k = self.n
        self.n += 1
        cp = pltpu.make_async_remote_copy(
            src_ref=src,
            dst_ref=dst,
            send_sem=self.send.at[k],
            recv_sem=self.recv.at[k],
            device_id=dev,
            device_id_type=MESH,
        )
        cp.start()
        return cp


class RingSum:
    def __init__(self, here, axis, part, l1, l2, sems):
        self.p = getattr(here, axis)
        self.part, self.l1, self.l2, self.sems = part, l1, l2, sems
        self.plus, self.minus = here.ring(axis, 1), here.ring(axis, 3)
        self.n = part.shape[1] // 2
        self.cps = []

    def start(self):
        p, n, part, sems = self.p, self.n, self.part, self.sems
        far, up, dn = (p + 2) % 4, (p + 1) % 4, (p + 3) % 4
        lo, hi = pl.ds(0, n), pl.ds(n, n)
        self.a = sems.copy(part.at[far, lo], self.l1.at[0], self.plus)
        self.b = sems.copy(part.at[far, hi], self.l1.at[1], self.minus)
        self.cps.append(sems.copy(part.at[up, hi], self.l2.at[0, hi], self.plus))
        self.cps.append(sems.copy(part.at[dn, lo], self.l2.at[1, lo], self.minus))

    def middle(self):
        p, n, part, sems = self.p, self.n, self.part, self.sems
        up, dn = (p + 1) % 4, (p + 3) % 4
        lo, hi = pl.ds(0, n), pl.ds(n, n)
        self.a.wait_recv()
        part[up, lo] = part[up, lo] + self.l1[0]
        self.cps.append(sems.copy(part.at[up, lo], self.l2.at[0, lo], self.plus))
        self.b.wait_recv()
        part[dn, hi] = part[dn, hi] + self.l1[1]
        self.cps.append(sems.copy(part.at[dn, hi], self.l2.at[1, hi], self.minus))

    def arrive(self):
        for cp in self.cps:
            cp.wait_recv()

    def total(self):
        return self.part[self.p] + self.l2[0] + self.l2[1]

    def done(self):
        for cp in [self.a, self.b] + self.cps:
            cp.wait_send()


def tensor_sum_kernel(p_ref, out_ref, lc, sm, lx, rb, fin, ss, rs):
    here = Here()
    core = here.dev(c=1 - here.c)
    across = here.dev(h=1 - here.h)
    greet([core, across])
    sems = Sems(ss, rs)
    mine = pl.ds(pl.multiple_of(here.c * 128, 128), 128)
    other = pl.ds(pl.multiple_of((1 - here.c) * 128, 128), 128)
    cols = [pl.ds(n * 256, 256) for n in range(4)]
    first = [sems.copy(p_ref.at[other, cols[n]], lc.at[n], core) for n in range(4)]
    second, third = [], []
    for n in range(4):
        first[n].wait_recv()
        sm[n] = p_ref[mine, cols[n]] + lc[n]
        second.append(sems.copy(sm.at[n], lx.at[n], across))
    for n in range(4):
        second[n].wait_recv()
        both = sm[n] + lx[n]
        rb[n] = both
        out_ref[mine, cols[n]] = both
        third.append(sems.copy(rb.at[n], fin.at[n], core))
    for n in range(4):
        third[n].wait_recv()
        out_ref[other, cols[n]] = fin[n]
    for cp in first + second + third:
        cp.wait_send()


def tensor_sum(part, cid):
    buf = VM((4, 128, 256), F32)
    return pl.pallas_call(
        tensor_sum_kernel,
        out_shape=jax.ShapeDtypeStruct((256, 1024), F32),
        in_specs=[pl.BlockSpec(memory_space=VM)],
        out_specs=pl.BlockSpec(memory_space=VM),
        scratch_shapes=[buf] * 5
        + [pltpu.SemaphoreType.DMA((12,)), pltpu.SemaphoreType.DMA((12,))],
        compiler_params=pltpu.CompilerParams(
            collective_id=cid, has_side_effects=True, vmem_limit_bytes=16 * 2**20
        ),
    )(part)


def first_dims(a, b):
    return lax.dot_general(a, b, (((0,), (0,)), ((), ())), preferred_element_type=F32)


def expert_grads_kernel(
    su, yu, sw, yw, out_u, out_w, gs, ys, gy, part, l1, l2, half, lx, fin, land, ss, rs
):
    here = Here()
    x, c = here.x, here.c
    axes = ("y", "z")
    peers = []
    for axis in axes:
        for step in range(4):
            for dc in range(2):
                if step:
                    peers.append(here.ring(axis, step, c=(c + dc) % 2))
    peers.append(here.dev(c=1 - c))
    xpeer = here.dev(x=1 - x)
    peers.append(xpeer)
    greet(peers)
    sems = Sems(ss, rs)
    waits = []
    shared = []
    for m, (axis, s_ref) in enumerate(zip(axes, (su, sw))):
        p = getattr(here, axis)
        gs[m, p] = s_ref[c].astype(F32)
        near = [
            sems.copy(gs.at[m, p], gs.at[m, p], here.ring(axis, 1)),
            sems.copy(gs.at[m, p], gs.at[m, p], here.ring(axis, 3)),
        ]
        shared.append(near)
    moved = []
    for m, (axis, y_ref) in enumerate(zip(axes, (yu, yw))):
        p = getattr(here, axis)
        for e in range(2):
            for q in range(4):
                ys[m, q, e] = y_ref[e, :, q * 256 : (q + 1) * 256].astype(F32)
        for step in (1, 3, 2, 0):
            for dc in range(2):
                q, e = (p + step) % 4, (c + dc) % 2
                if step == 0 and dc == 0:
                    gy[m, p, c] = ys[m, p, c]
                    continue
                moved.append(
                    sems.copy(ys.at[m, q, e], gy.at[m, p, c], here.ring(axis, step, c=e))
                )
    relayed = []
    for m, axis in enumerate(axes):
        p = getattr(here, axis)
        dn, up = (p + 3) % 4, (p + 1) % 4
        lo, hi = pl.ds(0, 64), pl.ds(64, 64)
        shared[m][0].wait_recv()
        relayed.append(sems.copy(gs.at[m, dn, lo], gs.at[m, dn, lo], here.ring(axis, 1)))
        shared[m][1].wait_recv()
        relayed.append(sems.copy(gs.at[m, up, hi], gs.at[m, up, hi], here.ring(axis, 3)))
    for cp in relayed + moved:
        cp.wait_recv()
    sums = []
    for m in range(2):
        right = jnp.concatenate(
            [
                jnp.concatenate([gy[m, q, k] for q in range(4)], axis=0).astype(BF)
                for k in range(2)
            ],
            axis=1,
        )

        def block(k, carry, m=m, right=right):
            lanes = pl.ds(pl.multiple_of(k * 128, 128), 128)
            left = gs[m, :, :, lanes].reshape(512, 128).astype(BF)
            res = first_dims(left, right).reshape(4, 32, 512)
            if m == 0:
                for z in range(4):
                    part[m, z, k // 4, k % 4] = res[z]
            else:
                part[m, k % 4, k // 4] = res
            return carry

        lax.fori_loop(0, 8, block, 0)
        ring = RingSum(here, axes[1 - m], part.at[m], l1.at[m], l2.at[m], sems)
        ring.start()
        sums.append(ring)
    for m in range(2):
        sums[m].middle()
    swaps = []
    for m in range(2):
        sums[m].arrive()
        half[m] = sums[m].total()
        swaps.append(sems.copy(half.at[m, 1 - x], lx.at[m], xpeer))
    last = []
    for m, axis in enumerate(axes):
        p = getattr(here, axis)
        swaps[m].wait_recv()
        mine = half[m, x] + lx[m]
        for k in range(2):
            fin[m, :, k] = mine[:, :, k * 256 : (k + 1) * 256]
        for step in (1, 3, 2, 0):
            for dc in range(2):
                q, k = (p + step) % 4, (c + dc) % 2
                if step == 0 and dc == 0:
                    land[m, p, c] = fin[m, p, c]
                    continue
                last.append(
                    sems.copy(fin.at[m, q, k], land.at[m, p, c], here.ring(axis, step, c=k))
                )
    for cp in last:
        cp.wait_recv()
    for m, out in enumerate((out_u, out_w)):
        for e in range(2):
            for q in range(4):
                out[e, :, q * 256 : (q + 1) * 256] = land[m, q, e]
    for cp in [cp for near in shared for cp in near] + moved + relayed + swaps + last:
        cp.wait_send()
    for ring in sums:
        ring.done()


def expert_grads(su, yu, sw, yw, cid):
    out = jax.ShapeDtypeStruct((2, 32, 1024), F32)
    return pl.pallas_call(
        expert_grads_kernel,
        out_shape=(out, out),
        in_specs=[pl.BlockSpec(memory_space=VM)] * 4,
        out_specs=[pl.BlockSpec(memory_space=VM)] * 2,
        scratch_shapes=[
            VM((2, 4, 128, 1024), F32),
            VM((2, 4, 2, 128, 256), F32),
            VM((2, 4, 2, 128, 256), F32),
            VM((2, 4, 2, 4, 32, 512), F32),
            VM((2, 2, 1, 4, 32, 512), F32),
            VM((2, 2, 2, 4, 32, 512), F32),
            VM((2, 2, 4, 32, 512), F32),
            VM((2, 4, 32, 512), F32),
            VM((2, 4, 2, 32, 256), F32),
            VM((2, 4, 2, 32, 256), F32),
            pltpu.SemaphoreType.DMA((60,)),
            pltpu.SemaphoreType.DMA((60,)),
        ],
        compiler_params=pltpu.CompilerParams(
            collective_id=cid, has_side_effects=True, vmem_limit_bytes=48 * 2**20
        ),
    )(su, yu, sw, yw)


def attention_grads_kernel(
    normed, gqkv, gbranch, mixed, vec, out_g, out_v,
    part, l1, l2, mid, m1, m2, half, lx, vb, lv, ss, rs,
):
    here = Here()
    x = here.x
    hops = [
        here.dev(y=here.y + 1 - 2 * (here.y % 2)),
        here.dev(y=3 - here.y),
        here.dev(z=here.z + 1 - 2 * (here.z % 2)),
        here.dev(z=3 - here.z),
        here.dev(x=1 - x),
    ]
    greet(hops)
    sems = Sems(ss, rs)
    lefts = (normed, normed, normed, gbranch)
    rights = (gqkv.at[0], gqkv.at[1], gqkv.at[2], mixed)
    axes = ("y", "z")
    sums = []
    for m in range(2):
        for j in range(2):
            left_ref = lefts[2 * m + j]
            right = rights[2 * m + j][...]

            def block(k, carry, m=m, j=j, left_ref=left_ref, right=right):
                lanes = pl.ds(pl.multiple_of(k * 128, 128), 128)
                res = first_dims(left_ref[:, lanes], right).reshape(4, 32, 256)
                for z in range(4):
                    if m == 0:
                        part[m, k % 4, z, k // 4, :, j * 256 : (j + 1) * 256] = res[z]
                    else:
                        part[m, z, k % 4, k // 4, :, j * 256 : (j + 1) * 256] = res[z]
                return carry

            lax.fori_loop(0, 8, block, 0)
        ring = RingSum(here, axes[m], part.at[m], l1.at[m], l2.at[m], sems)
        ring.start()
        sums.append(ring)
    vb[0] = vec[...]
    hop_cps = []

    def hop(k):
        hop_cps.append(sems.copy(vb.at[k], lv.at[k], hops[k]))

    def hopped(k):
        hop_cps[k].wait_recv()
        vb[k + 1] = vb[k] + lv[k]

    hop(0)
    for m in range(2):
        sums[m].middle()
    hopped(0)
    hop(1)
    second = []
    for m in range(2):
        sums[m].arrive()
        mid[m] = sums[m].total()
        ring = RingSum(here, axes[1 - m], mid.at[m], m1.at[m], m2.at[m], sems)
        ring.start()
        second.append(ring)
    hopped(1)
    hop(2)
    for m in range(2):
        second[m].middle()
    hopped(2)
    hop(3)
    swaps = []
    for m in range(2):
        second[m].arrive()
        half[m] = second[m].total()
        swaps.append(sems.copy(half.at[m, 1 - x], lx.at[m], hops[4]))
    hopped(3)
    hop(4)
    for m in range(2):
        swaps[m].wait_recv()
        out_g[m] = half[m, x] + lx[m]
    hopped(4)
    out_v[...] = vb[5]
    for cp in hop_cps + swaps:
        cp.wait_send()
    for ring in sums + second:
        ring.done()


def attention_grads(normed, gqkv, gbranch, mixed, vec, cid):
    n = vec.shape[0]
    return pl.pallas_call(
        attention_grads_kernel,
        out_shape=(jax.ShapeDtypeStruct((2, 32, 512), F32), jax.ShapeDtypeStruct(vec.shape, F32)),
        in_specs=[pl.BlockSpec(memory_space=VM)] * 5,
        out_specs=[pl.BlockSpec(memory_space=VM)] * 2,
        scratch_shapes=[
            VM((2, 4, 4, 2, 32, 512), F32),
            VM((2, 2, 2, 2, 32, 512), F32),
            VM((2, 2, 4, 2, 32, 512), F32),
            VM((2, 4, 2, 32, 512), F32),
            VM((2, 2, 1, 32, 512), F32),
            VM((2, 2, 2, 32, 512), F32),
            VM((2, 2, 32, 512), F32),
            VM((2, 32, 512), F32),
            VM((6, n, 1024), F32),
            VM((5, n, 1024), F32),
            pltpu.SemaphoreType.DMA((40,)),
            pltpu.SemaphoreType.DMA((40,)),
        ],
        compiler_params=pltpu.CompilerParams(
            collective_id=cid, has_side_effects=True, vmem_limit_bytes=48 * 2**20
        ),
    )(normed, gqkv, gbranch, mixed, vec)


def layer_norm(inputs, norm_gain, norm_shift):
    center = inputs - jnp.mean(inputs, axis=-1, keepdims=True)
    spread = jnp.mean(center * center, axis=-1, keepdims=True)
    return center * lax.rsqrt(spread + norm_eps) * norm_gain + norm_shift


def gelu_tanh(inputs):
    return jax.nn.gelu(inputs, approximate=True)


def product(left, right):
    return jnp.dot(left, right, preferred_element_type=jnp.float32)


def local(
    tokens,
    segments,
    routes,
    slot_table,
    ln_gain,
    ln_shift,
    qkv_proj,
    qv_bias,
    out_proj,
    out_bias,
    centroids,
    ffn_gain,
    ffn_shift,
    up_proj,
    up_bias,
    down_proj,
    down_bias,
    cotangent,
):
    length, model_width = tokens.shape
    experts, capacity = (slot_table.shape[1], slot_table.shape[2])
    local_heads = qkv_proj.shape[2] // HD
    score_scale = HD ** (-0.5)
    residual = tokens.astype(jnp.float32)
    is_valid = (segments != 0).astype(jnp.float32)
    position = jnp.arange(length, dtype=jnp.int32)
    normed, norm_pull = jax.vjp(
        layer_norm, residual, ln_gain.astype(jnp.float32), ln_shift.astype(jnp.float32)
    )
    normed_low = normed.astype(jnp.bfloat16)
    query_heads = (
        (product(normed_low, qkv_proj[0]) + qv_bias[0].astype(jnp.float32))
        .astype(jnp.bfloat16)
        .reshape(length, local_heads, HD)
    )
    keyed_heads = (
        product(normed_low, qkv_proj[1]).astype(jnp.bfloat16).reshape(length, local_heads, HD)
    )
    value_heads = (
        (product(normed_low, qkv_proj[2]) + qv_bias[1].astype(jnp.float32))
        .astype(jnp.bfloat16)
        .reshape(length, local_heads, HD)
    )
    allowed = (
        (segments[:, None] == segments[None, :])
        & (position[None, :] <= position[:, None])
        & (segments[:, None] != 0)
    )
    raw_scores = (
        jnp.einsum("qhd,khd->hqk", query_heads, keyed_heads, preferred_element_type=jnp.float32)
        * score_scale
    )
    masked = jnp.where(allowed[None], raw_scores, -1e30)
    row_top = jnp.max(masked, axis=-1, keepdims=True)
    exponent = jnp.where(allowed[None], jnp.exp(masked - row_top), 0.0)
    row_total = jnp.sum(exponent, axis=-1, keepdims=True) + (1.0 - is_valid)[None, :, None]
    attn_probs = exponent / row_total
    probs_low = attn_probs.astype(jnp.bfloat16)
    attn_mixed = jnp.einsum(
        "hqk,khd->qhd", probs_low, value_heads, preferred_element_type=jnp.float32
    )
    mixed_low = attn_mixed.reshape(length, local_heads * HD).astype(jnp.bfloat16)
    branch = tensor_sum(product(mixed_low, out_proj), 0) + out_bias.astype(jnp.float32)
    hidden = residual + branch
    cent_rows = centroids.astype(jnp.float32)
    route_hot = (routes[:, None] == jnp.arange(experts, dtype=jnp.int32)[None, :]).astype(
        jnp.float32
    )
    router_scores = jnp.dot(hidden, cent_rows.T, precision=highest)
    logits = jnp.sum(router_scores * route_hot, axis=1)
    gate_sigmoid = jax.nn.sigmoid(logits)
    gating = gate_sigmoid * is_valid
    flat_slots = slot_table.reshape(-1)
    filled = (flat_slots < length).astype(jnp.float32)
    safe_slots = jnp.minimum(flat_slots, length - 1)
    expert_rows = [hidden[safe_slots] * filled[:, None]]
    saved_parts = []
    for sublayer in range(2):
        current = expert_rows[sublayer].reshape(experts, capacity, model_width)
        normed_e, ffn_pull = jax.vjp(
            layer_norm,
            current,
            ffn_gain[:, sublayer].astype(jnp.float32)[:, None, :],
            ffn_shift[:, sublayer].astype(jnp.float32)[:, None, :],
        )
        normed_e_low = normed_e.astype(jnp.bfloat16)
        pre_act = (
            jnp.einsum(
                "ecd,edf->ecf",
                normed_e_low,
                up_proj[:, sublayer],
                preferred_element_type=jnp.float32,
            )
            + up_bias[:, sublayer].astype(jnp.float32)[:, None, :]
        )
        act_value, gelu_pull = jax.vjp(gelu_tanh, pre_act)
        act_low = act_value.astype(jnp.bfloat16)
        partial_out = jnp.einsum(
            "ecf,efd->ecd", act_low, down_proj[:, sublayer], preferred_element_type=jnp.float32
        )
        branch_out = (
            tensor_sum(partial_out.reshape(256, 1024), 1 + sublayer).reshape(experts, capacity, model_width)
            + down_bias[:, sublayer].astype(jnp.float32)[:, None, :]
        )
        expert_rows.append((current + branch_out).reshape(experts * capacity, model_width))
        saved_parts.append((ffn_pull, normed_e_low, gelu_pull, act_low))
    combined = (
        jnp.zeros((length, model_width), jnp.float32)
        .at[flat_slots]
        .add(expert_rows[2], mode="drop")
    )
    result_value = hidden + gating[:, None] * combined
    result = result_value.astype(jnp.bfloat16)
    valid_col = is_valid[:, None]
    hidden_sq = jnp.sum(hidden * hidden * valid_col)
    first_sq = jnp.sum(expert_rows[1] * expert_rows[1] * filled[:, None])
    second_sq = jnp.sum(expert_rows[2] * expert_rows[2] * filled[:, None])
    result_sq = jnp.sum(result_value * result_value * valid_col)
    valid_count = jnp.sum(is_valid)
    grad_result = cotangent.astype(jnp.float32)
    grad_comb = gating[:, None] * grad_result
    grad_gate = jnp.sum(grad_result * combined, axis=1)
    grad_logit = grad_gate * gate_sigmoid * (1.0 - gate_sigmoid) * is_valid
    grad_hidden = grad_result + grad_logit[:, None] * jnp.dot(
        route_hot, cent_rows, precision=highest
    )
    centroid_local = jnp.dot(route_hot.T, grad_logit[:, None] * hidden, precision=highest)
    grad_rows = grad_comb[safe_slots] * filled[:, None]
    gain_parts = [None, None]
    shift_parts = [None, None]
    up_parts = [None, None]
    upbias_parts = [None, None]
    down_parts = [None, None]
    downbias_parts = [None, None]
    for sublayer in (1, 0):
        ffn_pull, normed_e_low, gelu_pull, act_low = saved_parts[sublayer]
        grad_out_low = grad_rows.reshape(experts, capacity, model_width).astype(jnp.bfloat16)
        downbias_parts[sublayer] = jnp.sum(grad_out_low, axis=1, dtype=jnp.float32)
        grad_act = jnp.einsum(
            "ecd,efd->ecf", grad_out_low, down_proj[:, sublayer], preferred_element_type=jnp.float32
        )
        grad_pre_low = gelu_pull(grad_act)[0].astype(jnp.bfloat16)
        upbias_parts[sublayer] = jnp.sum(grad_pre_low, axis=1, dtype=jnp.float32)
        up_parts[sublayer], down_parts[sublayer] = expert_grads(
            normed_e_low, grad_pre_low, grad_out_low, act_low, 6 + sublayer
        )
        grad_normed_part = jnp.einsum(
            "ecf,edf->ecd", grad_pre_low, up_proj[:, sublayer], preferred_element_type=jnp.float32
        )
        grad_normed_e = tensor_sum(grad_normed_part.reshape(256, 1024), 3 + sublayer).reshape(experts, capacity, model_width)
        grad_current, grad_gain_e, grad_shift_e = ffn_pull(grad_normed_e)
        gain_parts[sublayer] = grad_gain_e[:, 0]
        shift_parts[sublayer] = grad_shift_e[:, 0]
        grad_rows = grad_rows + grad_current.reshape(experts * capacity, model_width)
    gain_e_local = jnp.stack(gain_parts, axis=1)
    shift_e_local = jnp.stack(shift_parts, axis=1)
    upbias_local = jnp.stack(upbias_parts, axis=1)
    downbias_local = jnp.stack(downbias_parts, axis=1)
    grad_hidden = grad_hidden + jnp.zeros((length, model_width), jnp.float32).at[flat_slots].add(
        grad_rows, mode="drop"
    )
    grad_branch_low = grad_hidden.astype(jnp.bfloat16)
    outbias_local = jnp.sum(grad_branch_low, axis=0, dtype=jnp.float32)
    grad_mixed = (
        jnp.einsum("td,hd->th", grad_branch_low, out_proj, preferred_element_type=jnp.float32)
        .astype(jnp.bfloat16)
        .reshape(length, local_heads, HD)
    )
    grad_probs = jnp.einsum(
        "qhd,khd->hqk", grad_mixed, value_heads, preferred_element_type=jnp.float32
    )
    grad_value = jnp.einsum(
        "hqk,qhd->khd", probs_low, grad_mixed, preferred_element_type=jnp.float32
    ).astype(jnp.bfloat16)
    row_dot = jnp.sum(attn_probs * grad_probs, axis=-1, keepdims=True)
    grad_scores = (attn_probs * (grad_probs - row_dot)).astype(jnp.bfloat16)
    grad_query = (
        jnp.einsum("hqk,khd->qhd", grad_scores, keyed_heads, preferred_element_type=jnp.float32)
        * score_scale
    ).astype(jnp.bfloat16)
    grad_keyed = (
        jnp.einsum("hqk,qhd->khd", grad_scores, query_heads, preferred_element_type=jnp.float32)
        * score_scale
    ).astype(jnp.bfloat16)
    grad_qkv = jnp.stack([grad_query, grad_keyed, grad_value]).reshape(3, length, local_heads * HD)
    qvbias_local = jnp.stack(
        [
            jnp.sum(grad_qkv[0], axis=0, dtype=jnp.float32),
            jnp.sum(grad_qkv[2], axis=0, dtype=jnp.float32),
        ]
    )
    grad_normed = tensor_sum(
        jnp.einsum("sth,sdh->td", grad_qkv, qkv_proj, preferred_element_type=jnp.float32), 5
    )
    grad_residual, gain_local, shift_local = norm_pull(grad_normed)
    tokens_grad = (grad_hidden + grad_residual).astype(jnp.bfloat16)
    up_proj_grad = jnp.stack(up_parts, axis=1)
    down_proj_grad = jnp.swapaxes(jnp.stack(down_parts, axis=1), 2, 3)
    stats = jnp.stack([hidden_sq, first_sq, second_sq, result_sq, valid_count])
    vec = jnp.concatenate(
        [
            gain_local.reshape(1, 1024),
            shift_local.reshape(1, 1024),
            outbias_local.reshape(1, 1024),
            centroid_local,
            gain_e_local.reshape(4, 1024),
            shift_e_local.reshape(4, 1024),
            downbias_local.reshape(4, 1024),
            upbias_local.reshape(4, 1024),
            jnp.pad(qvbias_local.reshape(1, 512), ((0, 0), (0, 512))),
            jnp.pad(stats.reshape(1, 5), ((0, 0), (0, 1019))),
            jnp.zeros((1, 1024), F32),
        ],
        axis=0,
    )
    proj_grads, vec = attention_grads(normed_low, grad_qkv, grad_branch_low, mixed_low, vec, 8)
    qkv_proj_grad = jnp.stack(
        [proj_grads[0, :, :256], proj_grads[0, :, 256:], proj_grads[1, :, :256]]
    )
    out_proj_grad = proj_grads[1, :, 256:].T
    share = lax.dynamic_slice(vec[:17], (0, lax.axis_index("dp") * 32), (17, 32))
    ln_gain_grad, ln_shift_grad, out_bias_grad = share[0], share[1], share[2]
    centroids_grad = share[3:5]
    ffn_gain_grad = share[5:9].reshape(2, 2, 32)
    ffn_shift_grad = share[9:13].reshape(2, 2, 32)
    down_bias_grad = share[13:17].reshape(2, 2, 32)
    up_bias_grad = vec[17:21].reshape(2, 2, 1024)
    qv_bias_grad = vec[21, :512].reshape(2, 256)
    totals = vec[22, :5]
    rms_values = jnp.sqrt(
        jnp.stack([totals[0], totals[1], totals[2], totals[3]]) / (totals[4] * model_width)
    )
    return (
        result,
        tokens_grad,
        ln_gain_grad,
        ln_shift_grad,
        qkv_proj_grad,
        qv_bias_grad,
        out_proj_grad,
        out_bias_grad,
        centroids_grad,
        ffn_gain_grad,
        ffn_shift_grad,
        up_proj_grad,
        up_bias_grad,
        down_proj_grad,
        down_bias_grad,
        rms_values,
    )


def solution(mesh):
    return jax.shard_map(
        local,
        mesh=mesh,
        in_specs=(
            P("dp", None),
            P("dp"),
            P("dp"),
            P("dp", None, None),
            P(),
            P(),
            P(None, None, "tensor"),
            P(None, "tensor"),
            P("tensor", None),
            P(),
            P(),
            P(),
            P(),
            P(None, None, None, "tensor"),
            P(None, None, "tensor"),
            P(None, None, "tensor", None),
            P(),
            P("dp", None),
        ),
        out_specs=(
            P("dp", None),
            P("dp", None),
            P("dp"),
            P("dp"),
            P(None, "dp", "tensor"),
            P(None, "tensor"),
            P("tensor", "dp"),
            P("dp"),
            P(None, "dp"),
            P(None, None, "dp"),
            P(None, None, "dp"),
            P(None, None, "dp", "tensor"),
            P(None, None, "tensor"),
            P(None, None, "tensor", "dp"),
            P(None, None, "dp"),
            P(),
        ),
        check_vma=False,
    )
```

```python
import math

import jax
import jax.numpy as jnp
from jax import lax
from jax.experimental import pallas as pl
from jax.experimental.pallas import tpu as pltpu
from jax.sharding import PartitionSpec as P

HD = 64
MESH = pl.DeviceIdType.MESH
VM = pltpu.VMEM
F32 = jnp.float32
BF = jnp.bfloat16
EPS = 1e-05
SCALE = HD ** (-0.5)
ROOT = math.sqrt(2.0 / math.pi)
COLS = [pl.ds(n * 256, 256) for n in range(4)]
LN_GAIN, LN_SHIFT, OUT_BIAS, CENT, GAIN, SHIFT, DOWN_B, UP_B, QV_B, STATS = (
    0, 1, 2, 3, 5, 9, 13, 17, 21, 22,
)


class Here:
    def __init__(self):
        d = lax.axis_index("dp")
        t = lax.axis_index("tensor")
        self.x, self.y, self.z = d // 16, (d // 4) % 4, d % 4
        self.h, self.c = t // 2, t % 2

    def dev(self, x=None, y=None, z=None, h=None, c=None):
        x = self.x if x is None else x
        y = self.y if y is None else y
        z = self.z if z is None else z
        h = self.h if h is None else h
        c = self.c if c is None else c
        return (x * 16 + y * 4 + z, h * 2 + c)

    def ring(self, axis, step, c=None):
        p = (getattr(self, axis) + step) % 4
        return self.dev(c=c, **{axis: p})


class Sems:
    def __init__(self, send, recv):
        self.send, self.recv, self.n = send, recv, 0

    def copy(self, src, dst, dev):
        k = self.n
        self.n += 1
        cp = pltpu.make_async_remote_copy(
            src_ref=src,
            dst_ref=dst,
            send_sem=self.send.at[k],
            recv_sem=self.recv.at[k],
            device_id=dev,
            device_id_type=MESH,
        )
        cp.start()
        return cp


def nn(a, b):
    return jnp.dot(a, b, preferred_element_type=F32)


def nt(a, b):
    return lax.dot_general(a, b, (((1,), (1,)), ((), ())), preferred_element_type=F32)


def tn(a, b):
    return lax.dot_general(a, b, (((0,), (0,)), ((), ())), preferred_element_type=F32)


def pick(hot, v):
    a = v.astype(BF)
    rest = v - a.astype(F32)
    b = rest.astype(BF)
    c = (rest - b.astype(F32)).astype(BF)
    return nn(hot, a) + nn(hot, b) + nn(hot, c)


def unit(v):
    center = v - jnp.mean(v, axis=-1, keepdims=True)
    r = lax.rsqrt(jnp.mean(center * center, axis=-1, keepdims=True) + EPS)
    return center * r, r


def unit_back(grad, gain, n, r):
    u = grad * gain
    return r * (u - jnp.mean(u, axis=-1, keepdims=True) - n * jnp.mean(u * n, axis=-1, keepdims=True))


def fold(v):
    return jnp.sum(v.reshape(v.shape[0] // 8, 8, v.shape[1]), axis=0)


def down_rows(v):
    return jnp.sum(v, axis=0, keepdims=True)


def rows32(i):
    return pl.ds(pl.multiple_of(i * 32, 32), 32)


class TensorSum:
    def __init__(self, here, sems, p, lc, lx, out):
        self.sems, self.p, self.lc, self.lx, self.out = sems, p, lc, lx, out
        self.core = here.dev(c=1 - here.c)
        self.across = here.dev(h=1 - here.h)
        self.mine = pl.ds(pl.multiple_of(here.c * 128, 128), 128)
        self.other = pl.ds(pl.multiple_of((1 - here.c) * 128, 128), 128)
        self.a, self.b, self.d = [], [], []

    def first(self, n):
        self.a.append(self.sems.copy(self.p.at[n, self.other], self.lc.at[n], self.core))

    def second(self, n):
        self.a[n].wait_recv()
        self.p[n, self.mine] = self.p[n, self.mine] + self.lc[n]
        self.b.append(self.sems.copy(self.p.at[n, self.mine], self.lx.at[n], self.across))

    def third(self, n):
        self.b[n].wait_recv()
        self.out[self.mine, COLS[n]] = self.p[n, self.mine] + self.lx[n]
        spot = self.out.at[self.mine, COLS[n]]
        self.d.append(self.sems.copy(spot, spot, self.core))

    def send(self, make):
        for n in range(4):
            self.p[n] = make(n)
            self.first(n)
            if n:
                self.second(n - 1)
        self.second(3)

    def end(self):
        for n in range(4):
            self.third(n)
        for cp in self.d:
            cp.wait_recv()
        for cp in self.a + self.b + self.d:
            cp.wait_send()


class RingSum:
    def __init__(self, here, axis, buf, base, rows, l1, l2, sems):
        self.p = getattr(here, axis)
        self.buf, self.base, self.rows = buf, base, rows
        self.l1, self.l2, self.sems = l1, l2, sems
        self.plus, self.minus = here.ring(axis, 1), here.ring(axis, 3)
        self.cps = []

    def part(self, step, half):
        n = self.rows // 2
        at = self.base + ((self.p + step) % 4) * self.rows + half * n
        return pl.ds(pl.multiple_of(at, n), n)

    def own(self):
        at = self.base + self.p * self.rows
        return pl.ds(pl.multiple_of(at, self.rows), self.rows)

    def start(self):
        n, buf, sems = self.rows // 2, self.buf, self.sems
        lo, hi = pl.ds(0, n), pl.ds(n, n)
        self.a = sems.copy(buf.at[self.part(2, 0)], self.l1.at[0], self.plus)
        self.b = sems.copy(buf.at[self.part(2, 1)], self.l1.at[1], self.minus)
        self.cps.append(sems.copy(buf.at[self.part(1, 1)], self.l2.at[0, hi], self.plus))
        self.cps.append(sems.copy(buf.at[self.part(3, 0)], self.l2.at[1, lo], self.minus))
        return self

    def middle(self):
        n, buf, sems = self.rows // 2, self.buf, self.sems
        lo, hi = pl.ds(0, n), pl.ds(n, n)
        up, dn = self.part(1, 0), self.part(3, 1)
        self.a.wait_recv()
        buf[up] = buf[up] + self.l1[0]
        self.cps.append(sems.copy(buf.at[up], self.l2.at[0, lo], self.plus))
        self.b.wait_recv()
        buf[dn] = buf[dn] + self.l1[1]
        self.cps.append(sems.copy(buf.at[dn], self.l2.at[1, hi], self.minus))

    def arrive(self):
        for cp in self.cps:
            cp.wait_recv()
        own = self.own()
        self.buf[own] = self.buf[own] + self.l2[0] + self.l2[1]

    def done(self):
        for cp in [self.a, self.b] + self.cps:
            cp.wait_send()


class Shared:
    def __init__(self, here, axis, buf, sems):
        self.here, self.axis, self.buf, self.sems = here, axis, buf, sems
        self.p = getattr(here, axis)

    def spot(self, step, half=None):
        at = ((self.p + step) % 4) * 256
        if half is None:
            return pl.ds(pl.multiple_of(at, 256), 256)
        return pl.ds(pl.multiple_of(at + half * 128, 128), 128)

    def start(self, src):
        rows = pl.ds(pl.multiple_of(self.here.c * 128, 128), 128)
        for half in range(2):
            self.buf[self.spot(0, half)] = src[rows, half * 512 : half * 512 + 512].astype(F32)
        mine = self.buf.at[self.spot(0)]
        self.near = [self.sems.copy(mine, mine, self.here.ring(self.axis, s)) for s in (1, 3)]
        return self

    def relay(self):
        self.far = []
        for cp, frm, to, half in ((self.near[0], 3, 1, 0), (self.near[1], 1, 3, 1)):
            cp.wait_recv()
            part = self.buf.at[self.spot(frm, half)]
            self.far.append(self.sems.copy(part, part, self.here.ring(self.axis, to)))

    def arrive(self):
        for cp in self.far:
            cp.wait_recv()

    def done(self):
        for cp in self.near + self.far:
            cp.wait_send()


class Moved:
    def __init__(self, here, axis, ys, gy, sems):
        self.here, self.axis, self.ys, self.gy, self.sems = here, axis, ys, gy, sems

    def start(self, src):
        here, axis, ys, gy = self.here, self.axis, self.ys, self.gy
        p, c = getattr(here, axis), here.c
        for q in range(4):
            ys[q] = src[:, q * 256 : q * 256 + 256].astype(F32)
        self.cps = []
        for step in (1, 3, 2, 0):
            for dc in range(2):
                q, e = (p + step) % 4, (c + dc) % 2
                rows = pl.ds(pl.multiple_of(e * 128, 128), 128)
                if step == 0 and dc == 0:
                    gy[p, c] = ys[q, rows]
                    continue
                to = here.ring(axis, step, c=e)
                self.cps.append(self.sems.copy(ys.at[q, rows], gy.at[p, c], to))
        return self

    def sent(self):
        for cp in self.cps:
            cp.wait_send()

    def arrive(self):
        for cp in self.cps:
            cp.wait_recv()


class ExpertGrads:
    def __init__(self, here, m, gs, gy, right, part, l1, l2, lx, land, sems):
        self.here, self.m, self.gs, self.gy, self.right = here, m, gs, gy, right
        self.part, self.lx, self.land, self.sems = part, lx, land, sems
        self.axis = ("y", "z")[m]
        self.ring = RingSum(here, ("z", "y")[m], part, 0, 256, l1, l2, sems)

    def multiply(self):
        for p in range(4):
            for k in range(2):
                self.right[p * 128 : p * 128 + 128, k * 256 : k * 256 + 256] = self.gy[p, k].astype(BF)

        def block(k, carry):
            lanes = pl.ds(pl.multiple_of((k % 4) * 128, 128), 128)
            left = [
                self.gs[pl.ds(pl.multiple_of(p * 256 + (k // 4) * 128, 128), 128), lanes].astype(BF)
                for p in range(4)
            ]
            res = tn(jnp.concatenate(left, axis=0), self.right[...])
            x, y = k // 4, k % 4
            if self.m == 0:
                for z in range(4):
                    at = pl.multiple_of(z * 256 + (x * 4 + y) * 32, 32)
                    self.part[pl.ds(at, 32)] = res[z * 32 : z * 32 + 32]
            else:
                self.part[pl.ds(pl.multiple_of(y * 256 + x * 128, 128), 128)] = res
            return carry

        lax.fori_loop(0, 8, block, 0)
        self.ring.start()

    def across(self):
        here, base = self.here, self.ring.p * 256
        self.ring.arrive()
        away = pl.ds(pl.multiple_of(base + (1 - here.x) * 128, 128), 128)
        self.swap = self.sems.copy(self.part.at[away], self.lx, here.dev(x=1 - here.x))

    def spread(self):
        here, base = self.here, self.ring.p * 256 + self.here.x * 128
        self.swap.wait_recv()
        mine = pl.ds(pl.multiple_of(base, 128), 128)
        self.part[mine] = self.part[mine] + self.lx[...]
        p, c = getattr(here, self.axis), here.c
        self.last = []
        for step in (1, 3, 2, 0):
            for dc in range(2):
                q, k = (p + step) % 4, (c + dc) % 2
                rows = pl.ds(pl.multiple_of(base + q * 32, 32), 32)
                lanes = pl.ds(pl.multiple_of(k * 256, 256), 256)
                if step == 0 and dc == 0:
                    self.land[p, c] = self.part[rows, lanes]
                    continue
                self.last.append(
                    self.sems.copy(
                        self.part.at[rows, lanes],
                        self.land.at[p, c],
                        here.ring(self.axis, step, c=k),
                    )
                )

    def finish(self, out, j):
        for cp in self.last:
            cp.wait_recv()
        for e in range(2):
            for q in range(4):
                out[e, j, :, q * 256 : q * 256 + 256] = self.land[q, e]
        for cp in [self.swap] + self.last:
            cp.wait_send()
        self.ring.done()


INPUTS = (
    "tok", "seg", "routes", "slots", "ln_gain", "ln_shift", "qkv_w", "qv_bias", "out_w", "out_bias",
    "cent", "ffn_gain", "ffn_shift", "up_w", "up_bias", "down_w", "down_bias", "cot",
)
IN_HBM = ("up_w", "down_w", "qkv_w", "out_w")
OUTPUTS = {
    "result": ((256, 1024), BF),
    "tokens_grad": ((256, 1024), BF),
    "qkv_grad": ((3, 32, 256), F32),
    "out_grad": ((32, 256), F32),
    "up_grad": ((2, 2, 32, 1024), F32),
    "down_grad": ((2, 2, 32, 1024), F32),
    "sums": ((24, 1024), F32),
}
PART = ((1024, 512), F32)
SQUARE = ((256, 1024), F32)
LOW = ((256, 1024), BF)
SCRATCH = {
    "wqkv": ((3, 1024, 256), BF), "wout": ((256, 1024), BF),
    "wup": ((2, 1024, 1024), BF), "wdn": ((2, 1024, 1024), BF),
    "normed": LOW, "q": ((256, 256), BF), "k": ((256, 256), BF), "v": ((256, 256), BF),
    "mixed": ((256, 256), BF), "probs": ((4, 256, 256), F32),
    "gq": ((256, 256), BF), "gk": ((256, 256), BF), "gv": ((256, 256), BF),
    "hot_s": ((256, 256), BF), "hot_t": ((256, 256), BF),
    "valid": ((256, 1), F32), "filled": ((256, 1), F32), "route": ((256, 1), F32),
    "sig": ((256, 1), F32), "gating": ((256, 1), F32), "segc": ((256, 1), F32),
    "hidden": SQUARE, "rows0": SQUARE, "rows1": SQUARE, "rows2": SQUARE,
    "slope0": SQUARE, "gwork": SQUARE, "grows": SQUARE, "ghidden": SQUARE,
    "n": LOW, "act": LOW, "go": LOW, "gp": LOW,
    "pa": ((4, 256, 256), F32), "lca": ((4, 128, 256), F32), "lxa": ((2, 4, 128, 256), F32),
    "pb": ((4, 256, 256), F32), "lcb": ((4, 128, 256), F32), "lxb": ((4, 128, 256), F32),
    "gs0u": PART, "gs0w": PART, "gs1u": PART, "gs1w": PART,
    "ysu": ((4, 256, 256), F32), "ysw": ((4, 256, 256), F32),
    "gy0u": ((4, 2, 128, 256), F32), "gy0w": ((4, 2, 128, 256), F32),
    "gy1u": ((4, 2, 128, 256), F32), "gy1w": ((4, 2, 128, 256), F32),
    "right": ((512, 512), BF),
    "partu": PART, "partw": PART,
    "l1": ((2, 2, 128, 512), F32), "l2": ((2, 2, 256, 512), F32),
    "lx": ((2, 2, 128, 512), F32), "land": ((2, 2, 4, 2, 32, 256), F32),
    "a1": ((2, 2, 128, 512), F32), "a2": ((2, 2, 256, 512), F32),
    "b1": ((2, 2, 32, 512), F32), "b2": ((2, 2, 64, 512), F32), "ax": ((2, 32, 512), F32),
    "vb": ((6, 24, 1024), F32), "lv": ((5, 24, 1024), F32),
}
N_SEMS = 240


class Bag:
    pass


def layer_kernel(*refs):
    B = Bag()
    for name, ref in zip([*INPUTS, *OUTPUTS, *SCRATCH, "ss", "rs", "ws"], refs):
        setattr(B, name, ref)
    B.n0 = B.n1 = B.gbranch = B.n
    B.act0 = B.act1 = B.act
    B.go0 = B.go1 = B.go
    B.gp0 = B.gp1 = B.gp
    here = Here()
    sems = Sems(B.ss, B.rs)
    x, c = here.x, here.c
    vec = B.vb.at[0]

    hops = [
        here.dev(y=here.y + 1 - 2 * (here.y % 2)),
        here.dev(y=3 - here.y),
        here.dev(z=here.z + 1 - 2 * (here.z % 2)),
        here.dev(z=3 - here.z),
        here.dev(x=1 - x),
    ]
    peers = [here.dev(c=1 - c), here.dev(h=1 - here.h), here.dev(x=1 - x)]
    for axis in ("y", "z"):
        for step in (1, 2, 3):
            for dc in range(2):
                peers.append(here.ring(axis, step, c=(c + dc) % 2))
    bar = pltpu.get_barrier_semaphore()
    for dev in peers:
        pl.semaphore_signal(bar, inc=1, device_id=dev, device_id_type=MESH)

    def fetch(pairs, at):
        cps = [pltpu.make_async_copy(s, t, B.ws.at[at + k]) for k, (s, t) in enumerate(pairs)]
        for cp in cps:
            cp.start()
        return cps

    def fetch_experts(j):
        return fetch(
            [(B.up_w.at[e, j], B.wup.at[e]) for e in range(2)]
            + [(B.down_w.at[e, j], B.wdn.at[e]) for e in range(2)],
            2,
        )

    heads = fetch([(B.qkv_w, B.wqkv), (B.out_w, B.wout)], 0)
    experts = fetch_experts(0)

    B.vb[0] = jnp.zeros((24, 1024), F32)
    lane1024 = lax.broadcasted_iota(jnp.int32, (1, 1024), 1)

    def stat(k, total):
        row = jnp.where(lane1024 == k, total, 0.0)
        vec[STATS : STATS + 1] = vec[STATS : STATS + 1] + row

    def total(v):
        return jnp.sum(jnp.sum(v, axis=1, keepdims=True), axis=0, keepdims=True)

    down_i = lax.broadcasted_iota(jnp.int32, (256, 256), 0)
    along_i = lax.broadcasted_iota(jnp.int32, (256, 256), 1)

    def column(row):
        return jnp.sum(jnp.where(down_i == along_i, row, 0.0), axis=1, keepdims=True)

    seg_row = B.seg[...].astype(F32)
    slot_row = jnp.concatenate([B.slots[0, 0:1], B.slots[0, 1:2]], axis=1)
    slot_col = column(slot_row.astype(F32))
    B.segc[...] = column(seg_row)
    B.route[...] = column(B.routes[...].astype(F32))
    B.valid[...] = (B.segc[...] != 0.0).astype(F32)
    B.filled[...] = (slot_col < 256.0).astype(F32)
    B.hot_s[...] = jnp.where(slot_col == along_i.astype(F32), 1.0, 0.0).astype(BF)
    B.hot_t[...] = jnp.where(slot_row == down_i, 1.0, 0.0).astype(BF)
    stat(4, total(B.valid[...]))

    def allowed():
        return (B.segc[...] == seg_row) & (along_i <= down_i) & (B.segc[...] != 0.0)

    head_of = along_i // HD

    gain = B.ln_gain[...].astype(F32)
    shift = B.ln_shift[...].astype(F32)

    def norm_block(i, carry):
        n, _ = unit(B.tok[rows32(i)].astype(F32))
        B.normed[rows32(i)] = (n * gain + shift).astype(BF)
        return carry

    lax.fori_loop(0, 8, norm_block, 0)
    for cp in heads:
        cp.wait()
    qv_bias = B.qv_bias[...].astype(F32)
    B.q[...] = (nn(B.normed[...], B.wqkv[0]) + qv_bias[0:1]).astype(BF)
    B.k[...] = nn(B.normed[...], B.wqkv[1]).astype(BF)
    B.v[...] = (nn(B.normed[...], B.wqkv[2]) + qv_bias[1:2]).astype(BF)

    def one_head(value, hh):
        return jnp.where(head_of == hh, value.astype(F32), 0.0)

    mixed = jnp.zeros((256, 256), F32)
    for hh in range(4):
        s = nt(one_head(B.q[...], hh).astype(BF), B.k[...]) * SCALE
        ok = allowed()
        s = jnp.where(ok, s, -1e30)
        e = jnp.where(ok, jnp.exp(s - jnp.max(s, axis=-1, keepdims=True)), 0.0)
        probs = e / (jnp.sum(e, axis=-1, keepdims=True) + (1.0 - B.valid[...]))
        B.probs[hh] = probs
        mixed = mixed + one_head(nn(probs.astype(BF), B.v[...]), hh)
    B.mixed[...] = mixed.astype(BF)

    pl.semaphore_wait(bar, len(peers))
    branch = TensorSum(here, sems, B.pa, B.lca, B.lxa.at[0], B.hidden)
    branch.send(lambda n: nn(B.mixed[...], B.wout[:, COLS[n]]))
    branch.end()

    out_bias = B.out_bias[...].astype(F32)
    cent = B.cent[...].astype(F32)

    def hidden_block(i, carry):
        rows = rows32(i)
        h = B.tok[rows].astype(F32) + (B.hidden[rows] + out_bias)
        B.hidden[rows] = h
        scores = [jnp.sum(h * cent[e : e + 1], axis=-1, keepdims=True) for e in range(2)]
        logits = jnp.where(B.route[rows] == 1.0, scores[1], scores[0])
        sig = 1.0 / (1.0 + jnp.exp(-logits))
        B.sig[rows] = sig
        B.gating[rows] = sig * B.valid[rows]
        return carry + fold(h * h * B.valid[rows])

    stat(0, total(lax.fori_loop(0, 8, hidden_block, jnp.zeros((8, 1024), F32))))
    for n in range(4):
        B.rows0[:, COLS[n]] = pick(B.hot_s[...], B.hidden[:, COLS[n]])
    ffn_gain = B.ffn_gain[...].astype(F32)
    ffn_shift = B.ffn_shift[...].astype(F32)
    up_bias = B.up_bias[...].astype(F32)
    down_bias = B.down_bias[...].astype(F32)

    def expert_norm(rows_ref, low_ref, j):
        for e in range(2):
            g, s = ffn_gain[e, j : j + 1], ffn_shift[e, j : j + 1]

            def block(i, carry, e=e, g=g, s=s):
                rows = rows32(e * 4 + i)
                n, _ = unit(rows_ref[rows])
                low_ref[rows] = (n * g + s).astype(BF)
                return carry

            lax.fori_loop(0, 4, block, 0)

    def gelu_parts(v):
        t = jnp.tanh(ROOT * (v + 0.044715 * (v * v * v)))
        cdf = 0.5 * (1.0 + t)
        slope = cdf + (0.5 * ROOT) * v * (1.0 - t * t) * (1.0 + (3.0 * 0.044715) * (v * v))
        return v * cdf, slope

    def half(e):
        return pl.ds(e * 128, 128)

    expert_norm(B.rows0, B.n0, 0)
    for cp in experts:
        cp.wait()
    for e in range(2):
        for n in range(4):
            pre = nn(B.n0[half(e)], B.wup[e, :, COLS[n]]) + up_bias[e, 0:1, n * 256 : n * 256 + 256]
            act, slope = gelu_parts(pre)
            B.act0[half(e), COLS[n]] = act.astype(BF)
            B.slope0[half(e), COLS[n]] = slope

    def down(act_ref):
        def make(n):
            return jnp.concatenate(
                [nn(act_ref[half(e)], B.wdn[e, :, COLS[n]]) for e in range(2)], axis=0
            )

        return make

    first = TensorSum(here, sems, B.pa, B.lca, B.lxa.at[1], B.rows1)
    first.send(down(B.act0))
    experts = fetch_experts(1)
    s0u = Shared(here, "y", B.gs0u, sems).start(B.n0)
    m0w = Moved(here, "z", B.ysw, B.gy0w, sems).start(B.act0)
    for n in range(4):
        g = pick(B.hot_s[...], B.gating[...] * B.cot[:, COLS[n]].astype(F32))
        B.grows[:, COLS[n]] = g
        B.go1[:, COLS[n]] = g.astype(BF)
    for e in range(2):
        vec[DOWN_B + e * 2 + 1 : DOWN_B + e * 2 + 2] = down_rows(B.go1[half(e)].astype(F32))
    s1w = Shared(here, "z", B.gs1w, sems).start(B.go1)
    for cp in experts:
        cp.wait()
    for e in range(2):
        for n in range(4):
            B.gwork[half(e), COLS[n]] = nt(B.go1[half(e)], B.wdn[e, COLS[n], :])
    first.end()

    sq = jnp.zeros((8, 1024), F32)
    for e in range(2):
        bias = down_bias[e, 0:1]

        def rows1_block(i, carry, e=e, bias=bias):
            rows = rows32(e * 4 + i)
            r1 = B.rows0[rows] + (B.rows1[rows] + bias)
            B.rows1[rows] = r1
            return carry + fold(r1 * r1 * B.filled[rows])

        sq = lax.fori_loop(0, 4, rows1_block, sq)
    stat(1, total(sq))
    expert_norm(B.rows1, B.n1, 1)
    for e in range(2):
        for n in range(4):
            pre = nn(B.n1[half(e)], B.wup[e, :, COLS[n]]) + up_bias[e, 1:2, n * 256 : n * 256 + 256]
            act, slope = gelu_parts(pre)
            B.act1[half(e), COLS[n]] = act.astype(BF)
            gp = (B.gwork[half(e), COLS[n]] * slope).astype(BF)
            B.gp1[half(e), COLS[n]] = gp
            vec[UP_B + e * 2 + 1 : UP_B + e * 2 + 2, COLS[n]] = down_rows(gp.astype(F32))

    def normed_grad(gp_ref):
        def make(n):
            return jnp.concatenate(
                [nt(gp_ref[half(e)], B.wup[e, COLS[n], :]) for e in range(2)], axis=0
            )

        return make

    back1 = TensorSum(here, sems, B.pa, B.lca, B.lxa.at[0], B.gwork)
    back1.send(normed_grad(B.gp1))
    m1u = Moved(here, "y", B.ysu, B.gy1u, sems).start(B.gp1)
    second = TensorSum(here, sems, B.pb, B.lcb, B.lxb, B.rows2)
    second.send(down(B.act1))
    experts = fetch_experts(0)
    s0u.relay()
    s1u = Shared(here, "y", B.gs1u, sems).start(B.n1)
    m0w.sent()
    m1w = Moved(here, "z", B.ysw, B.gy1w, sems).start(B.act1)
    s1w.relay()
    back1.end()

    def expert_norm_back(rows_ref, j, go_ref):
        for e in range(2):
            g = ffn_gain[e, j : j + 1]

            def block(i, carry, e=e, g=g):
                rows = rows32(e * 4 + i)
                n, r = unit(rows_ref[rows])
                gn = B.gwork[rows]
                new = B.grows[rows] + unit_back(gn, g, n, r)
                B.grows[rows] = new
                out = [carry[0] + fold(gn * n), carry[1] + fold(gn)]
                if go_ref is not None:
                    low = new.astype(BF)
                    go_ref[rows] = low
                    out.append(carry[2] + fold(low.astype(F32)))
                return tuple(out)

            zero = jnp.zeros((8, 1024), F32)
            sums = lax.fori_loop(0, 4, block, (zero,) * (2 if go_ref is None else 3))
            at = e * 2 + j
            vec[GAIN + at : GAIN + at + 1] = down_rows(sums[0])
            vec[SHIFT + at : SHIFT + at + 1] = down_rows(sums[1])
            if go_ref is not None:
                vec[DOWN_B + e * 2 : DOWN_B + e * 2 + 1] = down_rows(sums[2])

    expert_norm_back(B.rows1, 1, B.go0)
    for cp in experts:
        cp.wait()
    for e in range(2):
        for n in range(4):
            ga = nt(B.go0[half(e)], B.wdn[e, COLS[n], :])
            gp = (ga * B.slope0[half(e), COLS[n]]).astype(BF)
            B.gp0[half(e), COLS[n]] = gp
            vec[UP_B + e * 2 : UP_B + e * 2 + 1, COLS[n]] = down_rows(gp.astype(F32))
    back0 = TensorSum(here, sems, B.pa, B.lca, B.lxa.at[1], B.gwork)
    back0.send(normed_grad(B.gp0))
    s1u.relay()
    m1u.sent()
    m0u = Moved(here, "y", B.ysu, B.gy0u, sems).start(B.gp0)
    s0w = Shared(here, "z", B.gs0w, sems).start(B.go0)
    second.end()
    sq = jnp.zeros((8, 1024), F32)
    for e in range(2):
        bias = down_bias[e, 1:2]

        def rows2_block(i, carry, e=e, bias=bias):
            rows = rows32(e * 4 + i)
            r2 = B.rows1[rows] + (B.rows2[rows] + bias)
            B.rows2[rows] = r2
            return carry + fold(r2 * r2 * B.filled[rows])

        sq = lax.fori_loop(0, 4, rows2_block, sq)
    stat(2, total(sq))
    gate_grad = jnp.zeros((256, 1), F32)
    result_sq = jnp.zeros((256, 1), F32)
    for n in range(4):
        comb = pick(B.hot_t[...], B.rows2[:, COLS[n]])
        res = B.hidden[:, COLS[n]] + B.gating[...] * comb
        B.result[:, COLS[n]] = res.astype(BF)
        result_sq = result_sq + jnp.sum(res * res, axis=-1, keepdims=True)
        gate_grad = gate_grad + jnp.sum(B.cot[:, COLS[n]].astype(F32) * comb, axis=-1, keepdims=True)
    stat(3, total(result_sq * B.valid[...]))
    B.gating[...] = gate_grad * B.sig[...] * (1.0 - B.sig[...]) * B.valid[...]

    def gate_block(i, carry):
        rows = rows32(i)
        gl, second_route = B.gating[rows], B.route[rows] == 1.0
        B.ghidden[rows] = B.cot[rows].astype(F32) + gl * jnp.where(second_route, cent[1:2], cent[0:1])
        v = gl * B.hidden[rows]
        return (
            carry[0] + fold(jnp.where(second_route, 0.0, v)),
            carry[1] + fold(jnp.where(second_route, v, 0.0)),
        )

    zero = jnp.zeros((8, 1024), F32)
    sums = lax.fori_loop(0, 8, gate_block, (zero, zero))
    for e in range(2):
        vec[CENT + e : CENT + e + 1] = down_rows(sums[e])
    back0.end()

    expert_norm_back(B.rows0, 0, None)
    for n in range(4):
        g = B.ghidden[:, COLS[n]] + pick(B.hot_t[...], B.grows[:, COLS[n]])
        B.ghidden[:, COLS[n]] = g
        low = g.astype(BF)
        B.gbranch[:, COLS[n]] = low
        vec[OUT_BIAS : OUT_BIAS + 1, COLS[n]] = down_rows(low.astype(F32))
    gm = nt(B.gbranch[...], B.wout[...]).astype(BF)
    gq = jnp.zeros((256, 256), F32)
    gk = jnp.zeros((256, 256), F32)
    gv = jnp.zeros((256, 256), F32)
    for hh in range(4):
        probs = B.probs[hh]
        gp = nt(one_head(gm, hh).astype(BF), B.v[...])
        gv = gv + one_head(tn(probs.astype(BF), gm), hh)
        gs = (probs * (gp - jnp.sum(probs * gp, axis=-1, keepdims=True))).astype(BF)
        gq = gq + one_head(nn(gs, B.k[...]), hh)
        gk = gk + one_head(tn(gs, B.q[...]), hh)
    B.gq[...] = (gq * SCALE).astype(BF)
    B.gk[...] = (gk * SCALE).astype(BF)
    B.gv[...] = gv.astype(BF)
    vec[QV_B : QV_B + 1, 0:256] = down_rows(B.gq[...].astype(F32))
    vec[QV_B : QV_B + 1, 256:512] = down_rows(B.gv[...].astype(F32))
    back = TensorSum(here, sems, B.pa, B.lca, B.lxa.at[0], B.gwork)
    grads = (B.gq, B.gk, B.gv)
    back.send(lambda n: sum(nt(grads[s][...], B.wqkv[s, COLS[n], :]) for s in range(3)))

    s1u.arrive()
    s1w.arrive()
    m1u.arrive()
    m1w.arrive()
    eg1 = [
        ExpertGrads(here, m, (B.gs1u, B.gs1w)[m], (B.gy1u, B.gy1w)[m], B.right,
                    (B.partu, B.partw)[m], B.l1.at[m], B.l2.at[m], B.lx.at[0, m], B.land.at[0, m], sems)
        for m in range(2)
    ]
    for g in eg1:
        g.multiply()
    s0w.relay()
    s1u.done()
    s1w.done()
    lefts = (B.normed, B.normed, B.normed, B.gbranch)
    rights = (B.gq, B.gk, B.gv, B.mixed)
    apart = (B.gs1u, B.gs1w)
    rings = []
    for m in range(2):
        for j in range(2):

            def block(k, carry, m=m, left=lefts[2 * m + j], right=rights[2 * m + j], j=j):
                lanes = pl.ds(pl.multiple_of(k * 128, 128), 128)
                res = tn(left[:, lanes], right[...])
                for z in range(4):
                    if m == 0:
                        at = (k % 4) * 256 + (z * 2 + k // 4) * 32
                    else:
                        at = z * 256 + ((k % 4) * 2 + k // 4) * 32
                    apart[m][pl.ds(pl.multiple_of(at, 32), 32), j * 256 : j * 256 + 256] = res[
                        z * 32 : z * 32 + 32
                    ]
                return carry

            lax.fori_loop(0, 8, block, 0)
        rings.append(RingSum(here, ("y", "z")[m], apart[m], 0, 256, B.a1.at[m], B.a2.at[m], sems).start())
    back.end()

    zero = jnp.zeros((8, 1024), F32)

    def last_block(i, carry):
        rows = rows32(i)
        n, r = unit(B.tok[rows].astype(F32))
        gn = B.gwork[rows]
        B.tokens_grad[rows] = (B.ghidden[rows] + unit_back(gn, gain, n, r)).astype(BF)
        return carry[0] + fold(gn * n), carry[1] + fold(gn)

    sums = lax.fori_loop(0, 8, last_block, (zero, zero))
    vec[LN_GAIN : LN_GAIN + 1] = down_rows(sums[0])
    vec[LN_SHIFT : LN_SHIFT + 1] = down_rows(sums[1])
    hop_cps = []

    def hop(k):
        hop_cps.append(sems.copy(B.vb.at[k], B.lv.at[k], hops[k]))

    def hopped(k):
        hop_cps[k].wait_recv()
        B.vb[k + 1] = B.vb[k] + B.lv[k]

    hop(0)
    for g in eg1:
        g.ring.middle()
    for ring in rings:
        ring.middle()
    hopped(0)
    hop(1)
    for g in eg1:
        g.across()
    hopped(1)
    hop(2)
    for g in eg1:
        g.spread()
    s0u.arrive()
    s0w.arrive()
    m0u.arrive()
    m0w.arrive()
    for m, g in enumerate(eg1):
        g.finish((B.up_grad, B.down_grad)[m], 1)
    eg0 = [
        ExpertGrads(here, m, (B.gs0u, B.gs0w)[m], (B.gy0u, B.gy0w)[m], B.right,
                    (B.partu, B.partw)[m], B.l1.at[m], B.l2.at[m], B.lx.at[1, m], B.land.at[1, m], sems)
        for m in range(2)
    ]
    for g in eg0:
        g.multiply()
    hopped(2)
    hop(3)
    rings2 = []
    for m in range(2):
        rings[m].arrive()
        rings2.append(
            RingSum(here, ("z", "y")[m], apart[m], rings[m].p * 256, 64, B.b1.at[m], B.b2.at[m], sems).start()
        )
    for g in eg0:
        g.ring.middle()
    for ring in rings2:
        ring.middle()
    hopped(3)
    hop(4)
    swaps = []
    for m in range(2):
        rings2[m].arrive()
        base = rings2[m].base + rings2[m].p * 64
        away = pl.ds(pl.multiple_of(base + (1 - x) * 32, 32), 32)
        swaps.append(sems.copy(apart[m].at[away], B.ax.at[m], hops[4]))
    for g in eg0:
        g.across()
    for m in range(2):
        swaps[m].wait_recv()
        base = rings2[m].base + rings2[m].p * 64
        mine = apart[m][pl.ds(pl.multiple_of(base + x * 32, 32), 32)] + B.ax[m]
        if m == 0:
            B.qkv_grad[0] = mine[:, :256]
            B.qkv_grad[1] = mine[:, 256:]
        else:
            B.qkv_grad[2] = mine[:, :256]
            B.out_grad[...] = mine[:, 256:]
    for g in eg0:
        g.spread()
    hopped(4)
    B.sums[...] = B.vb[5]
    for m, g in enumerate(eg0):
        g.finish((B.up_grad, B.down_grad)[m], 0)
    for job in (m1u, m1w, m0u, m0w):
        if job in (m1w, m0u):
            job.sent()
    for job in (s0u, s0w, *rings, *rings2):
        job.done()
    for cp in hop_cps + swaps:
        cp.wait_send()


def local(
    tokens, segments, routes, slot_table, ln_gain, ln_shift, qkv_proj, qv_bias, out_proj, out_bias,
    centroids, ffn_gain, ffn_shift, up_proj, up_bias, down_proj, down_bias, cotangent,
):
    in_specs = [
        pl.BlockSpec(memory_space=pl.ANY if name in IN_HBM else VM) for name in INPUTS
    ]
    outs = pl.pallas_call(
        layer_kernel,
        out_shape=tuple(jax.ShapeDtypeStruct(*spec) for spec in OUTPUTS.values()),
        in_specs=in_specs,
        out_specs=[pl.BlockSpec(memory_space=VM)] * len(OUTPUTS),
        scratch_shapes=[VM(*spec) for spec in SCRATCH.values()]
        + [pltpu.SemaphoreType.DMA((N_SEMS,)), pltpu.SemaphoreType.DMA((N_SEMS,)), pltpu.SemaphoreType.DMA((6,))],
        compiler_params=pltpu.CompilerParams(
            collective_id=0, has_side_effects=True, vmem_limit_bytes=VMEM_LIMIT
        ),
    )(
        tokens, segments.reshape(1, 256), routes.reshape(1, 256), slot_table,
        ln_gain.reshape(1, 1024), ln_shift.reshape(1, 1024), qkv_proj, qv_bias, out_proj,
        out_bias.reshape(1, 1024), centroids, ffn_gain, ffn_shift, up_proj, up_bias, down_proj,
        down_bias, cotangent,
    )
    result, tokens_grad, qkv_grad, out_grad, up_grad, down_grad, sums = outs
    share = lax.dynamic_slice(sums[:17], (0, lax.axis_index("dp") * 32), (17, 32))
    totals = sums[STATS, :5]
    return (
        result,
        tokens_grad,
        share[LN_GAIN],
        share[LN_SHIFT],
        qkv_grad,
        sums[QV_B, :512].reshape(2, 256),
        out_grad.T,
        share[OUT_BIAS],
        share[CENT : CENT + 2],
        share[GAIN : GAIN + 4].reshape(2, 2, 32),
        share[SHIFT : SHIFT + 4].reshape(2, 2, 32),
        up_grad,
        sums[UP_B : UP_B + 4].reshape(2, 2, 1024),
        jnp.swapaxes(down_grad, 2, 3),
        share[DOWN_B : DOWN_B + 4].reshape(2, 2, 32),
        jnp.sqrt(totals[:4] / (totals[4] * 1024)),
    )


VMEM_LIMIT = 63 * 2**20


def solution(mesh):
    return jax.shard_map(
        local,
        mesh=mesh,
        in_specs=(
            P("dp", None),
            P("dp"),
            P("dp"),
            P("dp", None, None),
            P(),
            P(),
            P(None, None, "tensor"),
            P(None, "tensor"),
            P("tensor", None),
            P(),
            P(),
            P(),
            P(),
            P(None, None, None, "tensor"),
            P(None, None, "tensor"),
            P(None, None, "tensor", None),
            P(),
            P("dp", None),
        ),
        out_specs=(
            P("dp", None),
            P("dp", None),
            P("dp"),
            P("dp"),
            P(None, "dp", "tensor"),
            P(None, "tensor"),
            P("tensor", "dp"),
            P("dp"),
            P(None, "dp"),
            P(None, None, "dp"),
            P(None, None, "dp"),
            P(None, None, "dp", "tensor"),
            P(None, None, "tensor"),
            P(None, None, "tensor", "dp"),
            P(None, None, "dp"),
            P(),
        ),
        check_vma=False,
    )
```

```python
import math

import jax
import jax.numpy as jnp
from jax import lax
from jax.experimental import pallas as pl
from jax.experimental.pallas import tpu as pltpu
from jax.sharding import PartitionSpec as P

HD = 64
MESH = pl.DeviceIdType.MESH
VM = pltpu.VMEM
F32 = jnp.float32
BF = jnp.bfloat16
EPS = 1e-05
SCALE = HD ** (-0.5)
ROOT = math.sqrt(2.0 / math.pi)
COLS = [pl.ds(n * 256, 256) for n in range(4)]
LN_GAIN, LN_SHIFT, OUT_BIAS, CENT, GAIN, SHIFT, DOWN_B, UP_B, QV_B, STATS = (
    0, 1, 2, 3, 5, 9, 13, 17, 21, 22,
)


class Here:
    def __init__(self):
        d = lax.axis_index("dp")
        t = lax.axis_index("tensor")
        self.x, self.y, self.z = d // 16, (d // 4) % 4, d % 4
        self.h, self.c = t // 2, t % 2

    def dev(self, x=None, y=None, z=None, h=None, c=None):
        x = self.x if x is None else x
        y = self.y if y is None else y
        z = self.z if z is None else z
        h = self.h if h is None else h
        c = self.c if c is None else c
        return (x * 16 + y * 4 + z, h * 2 + c)

    def ring(self, axis, step, c=None):
        p = (getattr(self, axis) + step) % 4
        return self.dev(c=c, **{axis: p})


class Sems:
    def __init__(self, send, recv):
        self.send, self.recv, self.n = send, recv, 0

    def copy(self, src, dst, dev):
        k = self.n
        self.n += 1
        cp = pltpu.make_async_remote_copy(
            src_ref=src,
            dst_ref=dst,
            send_sem=self.send.at[k],
            recv_sem=self.recv.at[k],
            device_id=dev,
            device_id_type=MESH,
        )
        cp.start()
        return cp


def nn(a, b):
    return jnp.dot(a, b, preferred_element_type=F32)


def nt(a, b):
    return lax.dot_general(a, b, (((1,), (1,)), ((), ())), preferred_element_type=F32)


def tn(a, b):
    return lax.dot_general(a, b, (((0,), (0,)), ((), ())), preferred_element_type=F32)


def pick(hot, v):
    a = v.astype(BF)
    rest = v - a.astype(F32)
    b = rest.astype(BF)
    c = (rest - b.astype(F32)).astype(BF)
    return nn(hot, a) + nn(hot, b) + nn(hot, c)


def unit(v):
    center = v - jnp.mean(v, axis=-1, keepdims=True)
    r = lax.rsqrt(jnp.mean(center * center, axis=-1, keepdims=True) + EPS)
    return center * r, r


def unit_back(grad, gain, n, r):
    u = grad * gain
    return r * (u - jnp.mean(u, axis=-1, keepdims=True) - n * jnp.mean(u * n, axis=-1, keepdims=True))


def fold(v):
    return jnp.sum(v.reshape(v.shape[0] // 8, 8, v.shape[1]), axis=0)


def down_rows(v):
    return jnp.sum(v, axis=0, keepdims=True)


def rows32(i):
    return pl.ds(pl.multiple_of(i * 32, 32), 32)


class TensorSum:
    def __init__(self, here, sems, p, lc, lx, out):
        self.sems, self.p, self.lc, self.lx, self.out = sems, p, lc, lx, out
        self.core = here.dev(c=1 - here.c)
        self.across = here.dev(h=1 - here.h)
        self.mine = pl.ds(pl.multiple_of(here.c * 128, 128), 128)
        self.other = pl.ds(pl.multiple_of((1 - here.c) * 128, 128), 128)
        self.a, self.b, self.d = [], [], []

    def first(self, n):
        self.a.append(self.sems.copy(self.p.at[n, self.other], self.lc.at[n], self.core))

    def second(self, n):
        self.a[n].wait_recv()
        self.p[n, self.mine] = self.p[n, self.mine] + self.lc[n]
        self.b.append(self.sems.copy(self.p.at[n, self.mine], self.lx.at[n], self.across))

    def third(self, n):
        self.b[n].wait_recv()
        self.out[self.mine, COLS[n]] = self.p[n, self.mine] + self.lx[n]
        spot = self.out.at[self.mine, COLS[n]]
        self.d.append(self.sems.copy(spot, spot, self.core))

    def send(self, make):
        for n in range(4):
            self.p[n] = make(n)
            self.first(n)
            if n:
                self.second(n - 1)
        self.second(3)

    def end(self):
        for n in range(len(self.d), 4):
            self.third(n)
        for cp in self.d:
            cp.wait_recv()
        for cp in self.a + self.b + self.d:
            cp.wait_send()


class RingSum:
    def __init__(self, here, axis, buf, base, rows, l1, l2, sems):
        self.p = getattr(here, axis)
        self.buf, self.base, self.rows = buf, base, rows
        self.l1, self.l2, self.sems = l1, l2, sems
        self.plus, self.minus = here.ring(axis, 1), here.ring(axis, 3)
        self.cps = []

    def part(self, step, half):
        n = self.rows // 2
        at = self.base + ((self.p + step) % 4) * self.rows + half * n
        return pl.ds(pl.multiple_of(at, n), n)

    def own(self):
        at = self.base + self.p * self.rows
        return pl.ds(pl.multiple_of(at, self.rows), self.rows)

    def start(self):
        n, buf, sems = self.rows // 2, self.buf, self.sems
        lo, hi = pl.ds(0, n), pl.ds(n, n)
        self.a = sems.copy(buf.at[self.part(2, 0)], self.l1[0], self.plus)
        self.b = sems.copy(buf.at[self.part(2, 1)], self.l1[1], self.minus)
        self.cps.append(sems.copy(buf.at[self.part(1, 1)], self.l2[0].at[hi], self.plus))
        self.cps.append(sems.copy(buf.at[self.part(3, 0)], self.l2[1].at[lo], self.minus))
        return self

    def middle(self):
        n, buf, sems = self.rows // 2, self.buf, self.sems
        lo, hi = pl.ds(0, n), pl.ds(n, n)
        up, dn = self.part(1, 0), self.part(3, 1)
        self.a.wait_recv()
        buf[up] = buf[up] + self.l1[0][...]
        self.cps.append(sems.copy(buf.at[up], self.l2[0].at[lo], self.plus))
        self.b.wait_recv()
        buf[dn] = buf[dn] + self.l1[1][...]
        self.cps.append(sems.copy(buf.at[dn], self.l2[1].at[hi], self.minus))

    def arrive(self):
        for cp in self.cps:
            cp.wait_recv()
        own = self.own()
        self.buf[own] = self.buf[own] + self.l2[0][...] + self.l2[1][...]

    def done(self):
        for cp in [self.a, self.b] + self.cps:
            cp.wait_send()


class Shared:
    def __init__(self, here, axis, buf, sems):
        self.here, self.axis, self.buf, self.sems = here, axis, buf, sems
        self.p = getattr(here, axis)

    def spot(self, step, half=None):
        at = ((self.p + step) % 4) * 256
        if half is None:
            return pl.ds(pl.multiple_of(at, 256), 256)
        return pl.ds(pl.multiple_of(at + half * 128, 128), 128)

    def start(self, src):
        rows = pl.ds(pl.multiple_of(self.here.c * 128, 128), 128)
        for half in range(2):
            self.buf[self.spot(0, half)] = src[rows, half * 512 : half * 512 + 512].astype(F32)
        mine = self.buf.at[self.spot(0)]
        self.near = [self.sems.copy(mine, mine, self.here.ring(self.axis, s)) for s in (1, 3)]
        return self

    def relay(self):
        self.far = []
        for cp, frm, to, half in ((self.near[0], 3, 1, 0), (self.near[1], 1, 3, 1)):
            cp.wait_recv()
            part = self.buf.at[self.spot(frm, half)]
            self.far.append(self.sems.copy(part, part, self.here.ring(self.axis, to)))

    def arrive(self):
        for cp in self.far:
            cp.wait_recv()

    def done(self):
        for cp in self.near + self.far:
            cp.wait_send()


class Moved:
    def __init__(self, here, axis, lane, ys, gy, sems):
        self.here, self.axis, self.ys, self.gy, self.sems = here, axis, ys, gy, sems
        self.lanes = pl.ds(lane, 256)

    def start(self, src):
        here, axis, ys, gy, lanes = self.here, self.axis, self.ys, self.gy, self.lanes
        p, c = getattr(here, axis), here.c
        for q in range(4):
            ys[q * 256 : q * 256 + 256, lanes] = src[:, q * 256 : q * 256 + 256].astype(F32)
        spot = pl.ds(pl.multiple_of(p * 256 + c * 128, 128), 128)
        self.cps = []
        for step in (1, 3, 2, 0):
            for dc in range(2):
                q, e = (p + step) % 4, (c + dc) % 2
                rows = pl.ds(pl.multiple_of(q * 256 + e * 128, 128), 128)
                if step == 0 and dc == 0:
                    gy[spot, lanes] = ys[rows, lanes]
                    continue
                to = here.ring(axis, step, c=e)
                self.cps.append(self.sems.copy(ys.at[rows, lanes], gy.at[spot, lanes], to))
        return self

    def sent(self):
        for cp in self.cps:
            cp.wait_send()

    def arrive(self):
        for cp in self.cps:
            cp.wait_recv()


class ExpertGrads:
    def __init__(self, here, m, shared, moved, right, part, l1, l2, lx, land, sems):
        self.here, self.m, self.shared, self.moved, self.right = here, m, shared, moved, right
        self.part, self.lx, self.land, self.sems = part, lx, land, sems
        self.axis = ("y", "z")[m]
        self.ring = RingSum(here, ("z", "y")[m], part, 0, 256, l1, l2, sems)

    def multiply(self):
        self.shared.arrive()
        self.moved.arrive()
        gs, gy, lanes = self.shared.buf, self.moved.gy, self.moved.lanes
        for p in range(4):
            for k in range(2):
                rows = pl.ds(p * 256 + k * 128, 128)
                self.right[p * 128 : p * 128 + 128, k * 256 : k * 256 + 256] = gy[rows, lanes].astype(BF)

        def block(k, carry):
            lanes = pl.ds(pl.multiple_of((k % 4) * 128, 128), 128)
            left = [
                gs[pl.ds(pl.multiple_of(p * 256 + (k // 4) * 128, 128), 128), lanes].astype(BF)
                for p in range(4)
            ]
            res = tn(jnp.concatenate(left, axis=0), self.right[...])
            x, y = k // 4, k % 4
            if self.m == 0:
                for z in range(4):
                    at = pl.multiple_of(z * 256 + (x * 4 + y) * 32, 32)
                    self.part[pl.ds(at, 32)] = res[z * 32 : z * 32 + 32]
            else:
                self.part[pl.ds(pl.multiple_of(y * 256 + x * 128, 128), 128)] = res
            return carry

        lax.fori_loop(0, 8, block, 0)
        self.ring.start()

    def across(self):
        here, base = self.here, self.ring.p * 256
        self.ring.arrive()
        away = pl.ds(pl.multiple_of(base + (1 - here.x) * 128, 128), 128)
        self.swap = self.sems.copy(self.part.at[away], self.lx, here.dev(x=1 - here.x))

    def spread(self):
        here, base = self.here, self.ring.p * 256 + self.here.x * 128
        self.swap.wait_recv()
        mine = pl.ds(pl.multiple_of(base, 128), 128)
        self.part[mine] = self.part[mine] + self.lx[...]
        p, c = getattr(here, self.axis), here.c
        self.last = []
        for step in (1, 3, 2, 0):
            for dc in range(2):
                q, k = (p + step) % 4, (c + dc) % 2
                rows = pl.ds(pl.multiple_of(base + q * 32, 32), 32)
                lanes = pl.ds(pl.multiple_of(k * 256, 256), 256)
                if step == 0 and dc == 0:
                    self.land[p, c] = self.part[rows, lanes]
                    continue
                self.last.append(
                    self.sems.copy(
                        self.part.at[rows, lanes],
                        self.land.at[p, c],
                        here.ring(self.axis, step, c=k),
                    )
                )

    def finish(self, out, j):
        for cp in self.last:
            cp.wait_recv()
        for e in range(2):
            for q in range(4):
                out[e, j, :, q * 256 : q * 256 + 256] = self.land[q, e]
        for cp in [self.swap] + self.last:
            cp.wait_send()
        self.ring.done()


INPUTS = (
    "tok", "seg", "routes", "slots", "ln_gain", "ln_shift", "qkv_w", "qv_bias", "out_w", "out_bias",
    "cent", "ffn_gain", "ffn_shift", "up_w", "up_bias", "down_w", "down_bias", "cot",
)
IN_HBM = ("up_w", "down_w", "qkv_w", "out_w")
OUTPUTS = {
    "result": ((256, 1024), BF),
    "tokens_grad": ((256, 1024), BF),
    "qkv_grad": ((3, 32, 256), F32),
    "out_grad": ((32, 256), F32),
    "up_grad": ((2, 2, 32, 1024), F32),
    "down_grad": ((2, 2, 32, 1024), F32),
    "sums": ((24, 1024), F32),
}
PART = ((1024, 512), F32)
SQUARE = ((256, 1024), F32)
LOW = ((256, 1024), BF)
SCRATCH = {
    "wqkv": ((3, 1024, 256), BF), "wout": ((256, 1024), BF),
    "wup": ((2, 1024, 1024), BF), "wdn": ((2, 1024, 1024), BF),
    "normed": LOW, "q": ((256, 256), BF), "k": ((256, 256), BF), "v": ((256, 256), BF),
    "mixed": ((256, 256), BF), "probs": ((4, 256, 256), F32),
    "gq": ((256, 256), BF), "gk": ((256, 256), BF), "gv": ((256, 256), BF),
    "hot_s": ((256, 256), BF), "hot_t": ((256, 256), BF),
    "valid": ((256, 1), F32), "filled": ((256, 1), F32), "route": ((256, 1), F32),
    "sig": ((256, 1), F32), "gating": ((256, 1), F32), "segc": ((256, 1), F32),
    "hidden": SQUARE, "rows0": SQUARE, "rows1": SQUARE, "rows2": SQUARE,
    "slope0": SQUARE, "gwork": SQUARE, "grows": SQUARE, "ghidden": SQUARE,
    "n": LOW, "act": LOW, "go": LOW, "gp": LOW,
    "pa": ((4, 256, 256), F32), "lca": ((4, 128, 256), F32), "lxa": ((2, 4, 128, 256), F32),
    "pb": ((4, 256, 256), F32), "lcb": ((4, 128, 256), F32), "lxb": ((4, 128, 256), F32),
    "gs0u": PART, "gs0w": PART, "gs1u": PART, "gs1w": PART,
    "ys": PART, "gy0": PART, "gy1": PART,
    "right": ((512, 512), BF),
    "partu": PART, "partw": PART,
    "l1": ((2, 2, 128, 512), F32), "l2": ((2, 2, 256, 512), F32),
    "lx": ((2, 2, 128, 512), F32), "land": ((2, 2, 4, 2, 32, 256), F32),
    "a1": ((2, 2, 128, 512), F32), "a2": ((2, 2, 256, 512), F32),
    "b1": ((2, 2, 32, 512), F32), "b2": ((2, 2, 64, 512), F32), "ax": ((2, 32, 512), F32),
    "vb": ((10, 24, 1024), F32),
}
N_SEMS = 240


class Totals:
    def __init__(self, here, buf, sems):
        self.here, self.buf, self.sems, self.cps = here, buf, sems, []
        self.wait = []

    def swap(self):
        self.wait = [self.sems.copy(self.buf.at[0], self.buf.at[1], self.here.dev(x=1 - self.here.x))]
        self.cps += self.wait

    def collect(self):
        for cp in self.wait:
            cp.wait_recv()

    def ring(self, axis):
        buf, p = self.buf, getattr(self.here, axis)
        at = (2 if axis == "y" else 6) + p
        self.collect()
        if axis == "y":
            buf[at] = buf[0] + buf[1]
        else:
            buf[at] = (buf[2] + buf[3]) + (buf[4] + buf[5])
        self.wait = [
            self.sems.copy(buf.at[at], buf.at[at], self.here.ring(axis, step)) for step in (1, 3, 2)
        ]
        self.cps += self.wait

    def finish(self, out):
        self.collect()
        buf = self.buf
        out[...] = (buf[6] + buf[7]) + (buf[8] + buf[9])

    def done(self):
        for cp in self.cps:
            cp.wait_send()


class Bag:
    pass


def two(ref):
    return [ref.at[0], ref.at[1]]


def layer_kernel(*refs):
    B = Bag()
    for name, ref in zip([*INPUTS, *OUTPUTS, *SCRATCH, "ss", "rs", "ws", "free"], refs):
        setattr(B, name, ref)
    B.n0 = B.n1 = B.gbranch = B.n
    B.act0 = B.act1 = B.act
    B.go0 = B.go1 = B.go
    B.gp0 = B.gp1 = B.gp
    here = Here()
    sems = Sems(B.ss, B.rs)
    x, c = here.x, here.c
    vec = B.vb.at[0]

    peers = [here.dev(c=1 - c), here.dev(h=1 - here.h), here.dev(x=1 - x)]
    for axis in ("y", "z"):
        for step in (1, 2, 3):
            for dc in range(2):
                peers.append(here.ring(axis, step, c=(c + dc) % 2))
    bar = pltpu.get_barrier_semaphore()
    for dev in peers:
        pl.semaphore_signal(bar, inc=1, device_id=dev, device_id_type=MESH)

    def fetch(pairs, at):
        cps = [pltpu.make_async_copy(s, t, B.ws.at[at + k]) for k, (s, t) in enumerate(pairs)]
        for cp in cps:
            cp.start()
        return cps

    def fetch_experts(j):
        return fetch(
            [(B.up_w.at[e, j], B.wup.at[e]) for e in range(2)]
            + [(B.down_w.at[e, j], B.wdn.at[e]) for e in range(2)],
            2,
        )

    heads = fetch([(B.qkv_w, B.wqkv), (B.out_w, B.wout)], 0)
    experts = fetch_experts(0)

    B.vb[0] = jnp.zeros((24, 1024), F32)
    lane1024 = lax.broadcasted_iota(jnp.int32, (1, 1024), 1)

    def stat(k, total):
        row = jnp.where(lane1024 == k, total, 0.0)
        vec[STATS : STATS + 1] = vec[STATS : STATS + 1] + row

    def total(v):
        return jnp.sum(jnp.sum(v, axis=1, keepdims=True), axis=0, keepdims=True)

    down_i = lax.broadcasted_iota(jnp.int32, (256, 256), 0)
    along_i = lax.broadcasted_iota(jnp.int32, (256, 256), 1)

    def column(row):
        return jnp.sum(jnp.where(down_i == along_i, row, 0.0), axis=1, keepdims=True)

    seg_row = B.seg[...].astype(F32)
    slot_row = jnp.concatenate([B.slots[0, 0:1], B.slots[0, 1:2]], axis=1)
    slot_col = column(slot_row.astype(F32))
    B.segc[...] = column(seg_row)
    B.route[...] = column(B.routes[...].astype(F32))
    B.valid[...] = (B.segc[...] != 0.0).astype(F32)
    B.filled[...] = (slot_col < 256.0).astype(F32)
    B.hot_s[...] = jnp.where(slot_col == along_i.astype(F32), 1.0, 0.0).astype(BF)
    B.hot_t[...] = jnp.where(slot_row == down_i, 1.0, 0.0).astype(BF)
    stat(4, total(B.valid[...]))

    def allowed():
        return (B.segc[...] == seg_row) & (along_i <= down_i) & (B.segc[...] != 0.0)

    head_of = along_i // HD

    gain = B.ln_gain[...].astype(F32).reshape(1, 1024)
    shift = B.ln_shift[...].astype(F32).reshape(1, 1024)

    def norm_block(i, carry):
        n, _ = unit(B.tok[rows32(i)].astype(F32))
        B.normed[rows32(i)] = (n * gain + shift).astype(BF)
        return carry

    lax.fori_loop(0, 8, norm_block, 0)
    for cp in heads:
        cp.wait()
    qv_bias = B.qv_bias[...].astype(F32)
    B.q[...] = (nn(B.normed[...], B.wqkv[0]) + qv_bias[0:1]).astype(BF)
    B.k[...] = nn(B.normed[...], B.wqkv[1]).astype(BF)
    B.v[...] = (nn(B.normed[...], B.wqkv[2]) + qv_bias[1:2]).astype(BF)

    def one_head(value, hh):
        return jnp.where(head_of == hh, value.astype(F32), 0.0)

    mixed = jnp.zeros((256, 256), F32)
    for hh in range(4):
        s = nt(one_head(B.q[...], hh).astype(BF), B.k[...]) * SCALE
        ok = allowed()
        s = jnp.where(ok, s, -1e30)
        e = jnp.where(ok, jnp.exp(s - jnp.max(s, axis=-1, keepdims=True)), 0.0)
        probs = e / (jnp.sum(e, axis=-1, keepdims=True) + (1.0 - B.valid[...]))
        B.probs[hh] = probs
        mixed = mixed + one_head(nn(probs.astype(BF), B.v[...]), hh)
    B.mixed[...] = mixed.astype(BF)

    pl.semaphore_wait(bar, len(peers))
    branch = TensorSum(here, sems, B.pa, B.lca, B.lxa.at[0], B.hidden)
    branch.send(lambda n: nn(B.mixed[...], B.wout[:, COLS[n]]))
    branch.end()

    out_bias = B.out_bias[...].astype(F32).reshape(1, 1024)
    cent = B.cent[...].astype(F32)

    def hidden_block(i, carry):
        rows = rows32(i)
        h = B.tok[rows].astype(F32) + (B.hidden[rows] + out_bias)
        B.hidden[rows] = h
        scores = [jnp.sum(h * cent[e : e + 1], axis=-1, keepdims=True) for e in range(2)]
        logits = jnp.where(B.route[rows] == 1.0, scores[1], scores[0])
        sig = 1.0 / (1.0 + jnp.exp(-logits))
        B.sig[rows] = sig
        B.gating[rows] = sig * B.valid[rows]
        return carry + fold(h * h * B.valid[rows])

    stat(0, total(lax.fori_loop(0, 8, hidden_block, jnp.zeros((8, 1024), F32))))
    for n in range(4):
        B.rows0[:, COLS[n]] = pick(B.hot_s[...], B.hidden[:, COLS[n]])
    ffn_gain = B.ffn_gain[...].astype(F32)
    ffn_shift = B.ffn_shift[...].astype(F32)
    up_bias = B.up_bias[...].astype(F32)
    down_bias = B.down_bias[...].astype(F32)

    def expert_norm(rows_ref, low_ref, j):
        for e in range(2):
            g, s = ffn_gain[e, j : j + 1], ffn_shift[e, j : j + 1]

            def block(i, carry, e=e, g=g, s=s):
                rows = rows32(e * 4 + i)
                n, _ = unit(rows_ref[rows])
                low_ref[rows] = (n * g + s).astype(BF)
                return carry

            lax.fori_loop(0, 4, block, 0)

    def gelu_parts(v):
        t = jnp.tanh(ROOT * (v + 0.044715 * (v * v * v)))
        cdf = 0.5 * (1.0 + t)
        slope = cdf + (0.5 * ROOT) * v * (1.0 - t * t) * (1.0 + (3.0 * 0.044715) * (v * v))
        return v * cdf, slope

    def half(e):
        return pl.ds(e * 128, 128)

    expert_norm(B.rows0, B.n0, 0)
    for cp in experts:
        cp.wait()
    for e in range(2):
        for n in range(4):
            pre = nn(B.n0[half(e)], B.wup[e, :, COLS[n]]) + up_bias[e, 0:1, n * 256 : n * 256 + 256]
            act, slope = gelu_parts(pre)
            B.act0[half(e), COLS[n]] = act.astype(BF)
            B.slope0[half(e), COLS[n]] = slope

    def down(act_ref):
        def make(n):
            return jnp.concatenate(
                [nn(act_ref[half(e)], B.wdn[e, :, COLS[n]]) for e in range(2)], axis=0
            )

        return make

    first = TensorSum(here, sems, B.pa, B.lca, B.lxa.at[1], B.rows1)
    first.send(down(B.act0))
    experts = fetch_experts(1)
    s0u = Shared(here, "y", B.gs0u, sems).start(B.n0)
    m0w = Moved(here, "z", 256, B.ys, B.gy0, sems).start(B.act0)
    for n in range(4):
        g = pick(B.hot_s[...], B.gating[...] * B.cot[:, COLS[n]].astype(F32))
        B.grows[:, COLS[n]] = g
        B.go1[:, COLS[n]] = g.astype(BF)
    for e in range(2):
        vec[DOWN_B + e * 2 + 1 : DOWN_B + e * 2 + 2] = down_rows(B.go1[half(e)].astype(F32))
    s1w = Shared(here, "z", B.gs1w, sems).start(B.go1)
    for cp in experts:
        cp.wait()
    for e in range(2):
        for n in range(4):
            B.gwork[half(e), COLS[n]] = nt(B.go1[half(e)], B.wdn[e, COLS[n], :])
    for n in range(3):
        first.third(n)
    s0u.relay()
    first.end()

    sq = jnp.zeros((8, 1024), F32)
    for e in range(2):
        bias = down_bias[e, 0:1]

        def rows1_block(i, carry, e=e, bias=bias):
            rows = rows32(e * 4 + i)
            r1 = B.rows0[rows] + (B.rows1[rows] + bias)
            B.rows1[rows] = r1
            return carry + fold(r1 * r1 * B.filled[rows])

        sq = lax.fori_loop(0, 4, rows1_block, sq)
    stat(1, total(sq))
    expert_norm(B.rows1, B.n1, 1)
    s1u = Shared(here, "y", B.gs1u, sems).start(B.n1)
    for e in range(2):
        for n in range(4):
            pre = nn(B.n1[half(e)], B.wup[e, :, COLS[n]]) + up_bias[e, 1:2, n * 256 : n * 256 + 256]
            act, slope = gelu_parts(pre)
            B.act1[half(e), COLS[n]] = act.astype(BF)
            gp = (B.gwork[half(e), COLS[n]] * slope).astype(BF)
            B.gp1[half(e), COLS[n]] = gp
            vec[UP_B + e * 2 + 1 : UP_B + e * 2 + 2, COLS[n]] = down_rows(gp.astype(F32))

    def normed_grad(gp_ref):
        def make(n):
            return jnp.concatenate(
                [nt(gp_ref[half(e)], B.wup[e, COLS[n], :]) for e in range(2)], axis=0
            )

        return make

    back1 = TensorSum(here, sems, B.pa, B.lca, B.lxa.at[0], B.gwork)
    back1.send(normed_grad(B.gp1))
    m1u = Moved(here, "y", 0, B.ys, B.gy1, sems).start(B.gp1)
    second = TensorSum(here, sems, B.pb, B.lcb, B.lxb, B.rows2)
    second.send(down(B.act1))
    experts = fetch_experts(0)
    m0w.sent()
    m1w = Moved(here, "z", 256, B.ys, B.gy1, sems).start(B.act1)
    s1w.relay()
    back1.end()

    def expert_norm_back(rows_ref, j, go_ref):
        for e in range(2):
            g = ffn_gain[e, j : j + 1]

            def block(i, carry, e=e, g=g):
                rows = rows32(e * 4 + i)
                n, r = unit(rows_ref[rows])
                gn = B.gwork[rows]
                new = B.grows[rows] + unit_back(gn, g, n, r)
                B.grows[rows] = new
                out = [carry[0] + fold(gn * n), carry[1] + fold(gn)]
                if go_ref is not None:
                    low = new.astype(BF)
                    go_ref[rows] = low
                    out.append(carry[2] + fold(low.astype(F32)))
                return tuple(out)

            zero = jnp.zeros((8, 1024), F32)
            sums = lax.fori_loop(0, 4, block, (zero,) * (2 if go_ref is None else 3))
            at = e * 2 + j
            vec[GAIN + at : GAIN + at + 1] = down_rows(sums[0])
            vec[SHIFT + at : SHIFT + at + 1] = down_rows(sums[1])
            if go_ref is not None:
                vec[DOWN_B + e * 2 : DOWN_B + e * 2 + 1] = down_rows(sums[2])

    expert_norm_back(B.rows1, 1, B.go0)
    s0w = Shared(here, "z", B.gs0w, sems).start(B.go0)
    for cp in experts:
        cp.wait()
    for e in range(2):
        for n in range(4):
            ga = nt(B.go0[half(e)], B.wdn[e, COLS[n], :])
            gp = (ga * B.slope0[half(e), COLS[n]]).astype(BF)
            B.gp0[half(e), COLS[n]] = gp
            vec[UP_B + e * 2 : UP_B + e * 2 + 1, COLS[n]] = down_rows(gp.astype(F32))
    back0 = TensorSum(here, sems, B.pa, B.lca, B.lxa.at[1], B.gwork)
    back0.send(normed_grad(B.gp0))
    s1u.relay()
    m1u.sent()
    m0u = Moved(here, "y", 0, B.ys, B.gy0, sems).start(B.gp0)
    eg1 = [
        ExpertGrads(here, m, (s1u, s1w)[m], (m1u, m1w)[m], B.right, (B.partu, B.partw)[m],
                    two(B.l1.at[m]), two(B.l2.at[m]), B.lx.at[0, m], B.land.at[0, m], sems)
        for m in range(2)
    ]
    eg1[1].multiply()
    second.end()
    sq = jnp.zeros((8, 1024), F32)
    for e in range(2):
        bias = down_bias[e, 1:2]

        def rows2_block(i, carry, e=e, bias=bias):
            rows = rows32(e * 4 + i)
            r2 = B.rows1[rows] + (B.rows2[rows] + bias)
            B.rows2[rows] = r2
            return carry + fold(r2 * r2 * B.filled[rows])

        sq = lax.fori_loop(0, 4, rows2_block, sq)
    stat(2, total(sq))
    gate_grad = jnp.zeros((256, 1), F32)
    result_sq = jnp.zeros((256, 1), F32)
    for n in range(4):
        comb = pick(B.hot_t[...], B.rows2[:, COLS[n]])
        res = B.hidden[:, COLS[n]] + B.gating[...] * comb
        B.result[:, COLS[n]] = res.astype(BF)
        result_sq = result_sq + jnp.sum(res * res, axis=-1, keepdims=True)
        gate_grad = gate_grad + jnp.sum(B.cot[:, COLS[n]].astype(F32) * comb, axis=-1, keepdims=True)
    stat(3, total(result_sq * B.valid[...]))
    B.gating[...] = gate_grad * B.sig[...] * (1.0 - B.sig[...]) * B.valid[...]

    def gate_block(i, carry):
        rows = rows32(i)
        gl, second_route = B.gating[rows], B.route[rows] == 1.0
        B.ghidden[rows] = B.cot[rows].astype(F32) + gl * jnp.where(second_route, cent[1:2], cent[0:1])
        v = gl * B.hidden[rows]
        return (
            carry[0] + fold(jnp.where(second_route, 0.0, v)),
            carry[1] + fold(jnp.where(second_route, v, 0.0)),
        )

    zero = jnp.zeros((8, 1024), F32)
    sums = lax.fori_loop(0, 8, gate_block, (zero, zero))
    for e in range(2):
        vec[CENT + e : CENT + e + 1] = down_rows(sums[e])
    for k, axis in enumerate(("z", "y")):
        for step in (1, 3):
            pl.semaphore_signal(
                B.free.at[k], inc=1, device_id=here.ring(axis, step), device_id_type=MESH
            )
    for n in range(3):
        back0.third(n)
    s0w.relay()
    back0.end()

    expert_norm_back(B.rows0, 0, None)
    for n in range(4):
        g = B.ghidden[:, COLS[n]] + pick(B.hot_t[...], B.grows[:, COLS[n]])
        B.ghidden[:, COLS[n]] = g
        low = g.astype(BF)
        B.gbranch[:, COLS[n]] = low
        vec[OUT_BIAS : OUT_BIAS + 1, COLS[n]] = down_rows(low.astype(F32))
    gm = nt(B.gbranch[...], B.wout[...]).astype(BF)
    gq = jnp.zeros((256, 256), F32)
    gk = jnp.zeros((256, 256), F32)
    gv = jnp.zeros((256, 256), F32)
    for hh in range(4):
        probs = B.probs[hh]
        gp = nt(one_head(gm, hh).astype(BF), B.v[...])
        gv = gv + one_head(tn(probs.astype(BF), gm), hh)
        gs = (probs * (gp - jnp.sum(probs * gp, axis=-1, keepdims=True))).astype(BF)
        gq = gq + one_head(nn(gs, B.k[...]), hh)
        gk = gk + one_head(tn(gs, B.q[...]), hh)
    B.gq[...] = (gq * SCALE).astype(BF)
    B.gk[...] = (gk * SCALE).astype(BF)
    B.gv[...] = gv.astype(BF)
    vec[QV_B : QV_B + 1, 0:256] = down_rows(B.gq[...].astype(F32))
    vec[QV_B : QV_B + 1, 256:512] = down_rows(B.gv[...].astype(F32))
    back = TensorSum(here, sems, B.pa, B.lca, B.lxa.at[0], B.gwork)
    grads = (B.gq, B.gk, B.gv)
    back.send(lambda n: sum(nt(grads[s][...], B.wqkv[s, COLS[n], :]) for s in range(3)))

    eg1[0].multiply()
    m1w.sent()
    m0u.sent()
    wide = [pl.ds(0, 512), pl.ds(512, 512)]
    eg0 = [
        ExpertGrads(here, m, (s0u, s0w)[m], (m0u, m0w)[m], B.right, (B.ys, B.gy1)[m],
                    [B.slope0.at[pl.ds(128 * k, 128), wide[m]] for k in range(2)],
                    [(B.hidden, B.rows2)[m].at[:, wide[k]] for k in range(2)],
                    B.lx.at[1, m], B.land.at[1, m], sems)
        for m in range(2)
    ]
    for m in range(2):
        pl.semaphore_wait(B.free.at[m], 2)
        eg0[m].multiply()
    eg1[1].ring.middle()
    eg1[0].ring.middle()
    s1u.done()
    s1w.done()
    lefts = (B.normed, B.normed, B.normed, B.gbranch)
    rights = (B.gq, B.gk, B.gv, B.mixed)
    apart = (B.gs1u, B.gs1w)
    rings = []
    for m in range(2):
        for j in range(2):

            def block(k, carry, m=m, left=lefts[2 * m + j], right=rights[2 * m + j], j=j):
                lanes = pl.ds(pl.multiple_of(k * 128, 128), 128)
                res = tn(left[:, lanes], right[...])
                for z in range(4):
                    if m == 0:
                        at = (k % 4) * 256 + (z * 2 + k // 4) * 32
                    else:
                        at = z * 256 + ((k % 4) * 2 + k // 4) * 32
                    apart[m][pl.ds(pl.multiple_of(at, 32), 32), j * 256 : j * 256 + 256] = res[
                        z * 32 : z * 32 + 32
                    ]
                return carry

            lax.fori_loop(0, 8, block, 0)
        rings.append(RingSum(here, ("y", "z")[m], apart[m], 0, 256, two(B.a1.at[m]), two(B.a2.at[m]), sems).start())
    back.end()

    zero = jnp.zeros((8, 1024), F32)

    def last_block(i, carry):
        rows = rows32(i)
        n, r = unit(B.tok[rows].astype(F32))
        gn = B.gwork[rows]
        B.tokens_grad[rows] = (B.ghidden[rows] + unit_back(gn, gain, n, r)).astype(BF)
        return carry[0] + fold(gn * n), carry[1] + fold(gn)

    sums = lax.fori_loop(0, 8, last_block, (zero, zero))
    vec[LN_GAIN : LN_GAIN + 1] = down_rows(sums[0])
    vec[LN_SHIFT : LN_SHIFT + 1] = down_rows(sums[1])
    gather = Totals(here, B.vb, sems)
    gather.swap()
    eg1[1].across()
    eg1[0].across()
    for g in (eg0[1], eg0[0]):
        g.ring.middle()
    for ring in rings:
        ring.middle()
    gather.ring("y")
    for g in eg1:
        g.spread()
    for g in (eg0[1], eg0[0]):
        g.across()
    gather.ring("z")
    rings2 = []
    for m in range(2):
        rings[m].arrive()
        rings2.append(
            RingSum(here, ("z", "y")[m], apart[m], rings[m].p * 256, 64,
                    two(B.b1.at[m]), two(B.b2.at[m]), sems).start()
        )
    for g in (eg0[1], eg0[0]):
        g.spread()
    for ring in rings2:
        ring.middle()
    for m, g in enumerate(eg1):
        g.finish((B.up_grad, B.down_grad)[m], 1)
    swaps = []
    for m in range(2):
        rings2[m].arrive()
        base = rings2[m].base + rings2[m].p * 64
        away = pl.ds(pl.multiple_of(base + (1 - x) * 32, 32), 32)
        swaps.append(sems.copy(apart[m].at[away], B.ax.at[m], here.dev(x=1 - x)))
    gather.finish(B.sums)
    for m, g in enumerate(eg0):
        g.finish((B.up_grad, B.down_grad)[m], 0)
    for m in range(2):
        swaps[m].wait_recv()
        base = rings2[m].base + rings2[m].p * 64
        mine = apart[m][pl.ds(pl.multiple_of(base + x * 32, 32), 32)] + B.ax[m]
        if m == 0:
            B.qkv_grad[0] = mine[:, :256]
            B.qkv_grad[1] = mine[:, 256:]
        else:
            B.qkv_grad[2] = mine[:, :256]
            B.out_grad[...] = mine[:, 256:]
    for job in (s0u, s0w, gather, *rings, *rings2):
        job.done()
    for cp in swaps:
        cp.wait_send()


def finish_kernel(*refs):
    big_in, sums, big_out = refs[:6], refs[6], refs[7:13]
    gain, shift, out_b, cent, ffn_g, ffn_s, down_b, up_b, qv_b, rms, sem = refs[13:]
    cps = [pltpu.make_async_copy(a, b, sem.at[k]) for k, (a, b) in enumerate(zip(big_in, big_out))]
    for cp in cps:
        cp.start()
    d = lax.axis_index("dp")
    near = sums[:, pl.ds(pl.multiple_of((d // 4) * 128, 128), 128)]
    share = near[:, :32]
    for k in range(1, 4):
        share = jnp.where(d % 4 == k, near[:, k * 32 : k * 32 + 32], share)
    for ref, at in ((gain, LN_GAIN), (shift, LN_SHIFT), (out_b, OUT_BIAS)):
        ref[...] = share[at : at + 1]
    cent[...] = share[CENT : CENT + 2]
    for ref, at in ((ffn_g, GAIN), (ffn_s, SHIFT), (down_b, DOWN_B)):
        for e in range(2):
            ref[e] = share[at + e * 2 : at + e * 2 + 2]
    for e in range(2):
        up_b[e] = sums[UP_B + e * 2 : UP_B + e * 2 + 2]
    qv_b[0:1] = sums[QV_B : QV_B + 1, 0:256]
    qv_b[1:2] = sums[QV_B : QV_B + 1, 256:512]
    totals = sums[STATS : STATS + 1, 0:128]
    rms[...] = jnp.sqrt(totals[:, :4] / (totals[:, 4:5] * 1024.0))
    for cp in cps:
        cp.wait()


SMALL = [(1, 32), (1, 32), (1, 32), (2, 32), (2, 2, 32), (2, 2, 32), (2, 2, 32), (2, 2, 1024), (2, 256), (1, 4)]


def local(
    tokens, segments, routes, slot_table, ln_gain, ln_shift, qkv_proj, qv_bias, out_proj, out_bias,
    centroids, ffn_gain, ffn_shift, up_proj, up_bias, down_proj, down_bias, cotangent,
):
    in_specs = [
        pl.BlockSpec(memory_space=pl.ANY if name in IN_HBM else VM) for name in INPUTS
    ]
    outs = pl.pallas_call(
        layer_kernel,
        out_shape=tuple(jax.ShapeDtypeStruct(*spec) for spec in OUTPUTS.values()),
        in_specs=in_specs,
        out_specs=[pl.BlockSpec(memory_space=VM)] * len(OUTPUTS),
        scratch_shapes=[VM(*spec) for spec in SCRATCH.values()]
        + [pltpu.SemaphoreType.DMA((N_SEMS,)), pltpu.SemaphoreType.DMA((N_SEMS,)), pltpu.SemaphoreType.DMA((6,)), pltpu.SemaphoreType.REGULAR((2,))],
        compiler_params=pltpu.CompilerParams(
            collective_id=0, has_side_effects=True, vmem_limit_bytes=VMEM_LIMIT
        ),
    )(
        tokens, segments.reshape(1, 256), routes.reshape(1, 256), slot_table,
        ln_gain, ln_shift, qkv_proj, qv_bias, out_proj,
        out_bias, centroids, ffn_gain, ffn_shift, up_proj, up_bias, down_proj,
        down_bias, cotangent,
    )
    anywhere = pl.BlockSpec(memory_space=pl.ANY)
    near = pl.BlockSpec(memory_space=VM)
    (
        result, tokens_grad, qkv_grad, out_grad, up_grad, down_grad,
        gain, shift, out_b, cent, ffn_g, ffn_s, down_b, up_b, qv_b, rms,
    ) = pl.pallas_call(
        finish_kernel,
        out_shape=tuple(jax.ShapeDtypeStruct(a.shape, a.dtype) for a in outs[:6])
        + tuple(jax.ShapeDtypeStruct(shape, F32) for shape in SMALL),
        in_specs=[near] * 7,
        out_specs=[anywhere] * 6 + [near] * len(SMALL),
        scratch_shapes=[pltpu.SemaphoreType.DMA((6,))],
    )(*outs)
    return (
        result,
        tokens_grad,
        gain.reshape(32),
        shift.reshape(32),
        qkv_grad,
        qv_b,
        out_grad.T,
        out_b.reshape(32),
        cent,
        ffn_g,
        ffn_s,
        up_grad,
        up_b,
        jnp.swapaxes(down_grad, 2, 3),
        down_b,
        rms.reshape(4),
    )


VMEM_LIMIT = 63 * 2**20


def solution(mesh):
    return jax.shard_map(
        local,
        mesh=mesh,
        in_specs=(
            P("dp", None),
            P("dp"),
            P("dp"),
            P("dp", None, None),
            P(),
            P(),
            P(None, None, "tensor"),
            P(None, "tensor"),
            P("tensor", None),
            P(),
            P(),
            P(),
            P(),
            P(None, None, None, "tensor"),
            P(None, None, "tensor"),
            P(None, None, "tensor", None),
            P(),
            P("dp", None),
        ),
        out_specs=(
            P("dp", None),
            P("dp", None),
            P("dp"),
            P("dp"),
            P(None, "dp", "tensor"),
            P(None, "tensor"),
            P("tensor", "dp"),
            P("dp"),
            P(None, "dp"),
            P(None, None, "dp"),
            P(None, None, "dp"),
            P(None, None, "dp", "tensor"),
            P(None, None, "tensor"),
            P(None, None, "tensor", "dp"),
            P(None, None, "dp"),
            P(),
        ),
        check_vma=False,
    )
```

```python
import math

import jax
import jax.numpy as jnp
from jax import lax
from jax.experimental import pallas as pl
from jax.experimental.pallas import tpu as pltpu
from jax.sharding import PartitionSpec as P

HD = 64
MESH = pl.DeviceIdType.MESH
OTHER = {"a": "b", "b": "a"}
VM = pltpu.VMEM
F32 = jnp.float32
BF = jnp.bfloat16
EPS = 1e-05
SCALE = HD ** (-0.5)
ROOT = math.sqrt(2.0 / math.pi)
COLS = [pl.ds(n * 256, 256) for n in range(4)]
LN_GAIN, LN_SHIFT, OUT_BIAS, CENT, GAIN, SHIFT, DOWN_B, UP_B, QV_B, STATS = (
    0, 1, 2, 3, 5, 9, 13, 17, 21, 22,
)


class Here:
    def __init__(self):
        d = lax.axis_index("dp")
        t = lax.axis_index("tensor")
        self.x, self.y, self.z = d // 16, (d // 4) % 4, d % 4
        self.h, self.c = t // 2, t % 2
        self.a = self.y * (1 - self.c) + self.z * self.c
        self.b = self.z * (1 - self.c) + self.y * self.c

    def dev(self, x=None, y=None, z=None, h=None, c=None):
        x = self.x if x is None else x
        y = self.y if y is None else y
        z = self.z if z is None else z
        h = self.h if h is None else h
        c = self.c if c is None else c
        return (x * 16 + y * 4 + z, h * 2 + c)

    def ring(self, axis, step, c=None):
        on_y = {"y": 1, "z": 0, "a": 1 - self.c, "b": self.c}[axis]
        y, z = (self.y + step * on_y) % 4, (self.z + step * (1 - on_y)) % 4
        return self.dev(y=y, z=z, c=c)


class Sems:
    def __init__(self, send, recv):
        self.send, self.recv, self.n = send, recv, 0

    def copy(self, src, dst, dev):
        k = self.n
        self.n += 1
        cp = pltpu.make_async_remote_copy(
            src_ref=src,
            dst_ref=dst,
            send_sem=self.send.at[k],
            recv_sem=self.recv.at[k],
            device_id=dev,
            device_id_type=MESH,
        )
        cp.start()
        return cp


def nn(a, b):
    return jnp.dot(a, b, preferred_element_type=F32)


def nt(a, b):
    return lax.dot_general(a, b, (((1,), (1,)), ((), ())), preferred_element_type=F32)


def tn(a, b):
    return lax.dot_general(a, b, (((0,), (0,)), ((), ())), preferred_element_type=F32)


def pick(hot, v):
    a = v.astype(BF)
    rest = v - a.astype(F32)
    b = rest.astype(BF)
    c = (rest - b.astype(F32)).astype(BF)
    return nn(hot, a) + nn(hot, b) + nn(hot, c)


def unit(v):
    center = v - jnp.mean(v, axis=-1, keepdims=True)
    r = lax.rsqrt(jnp.mean(center * center, axis=-1, keepdims=True) + EPS)
    return center * r, r


def unit_back(grad, gain, n, r):
    u = grad * gain
    return r * (u - jnp.mean(u, axis=-1, keepdims=True) - n * jnp.mean(u * n, axis=-1, keepdims=True))


def fold(v):
    return jnp.sum(v.reshape(v.shape[0] // 8, 8, v.shape[1]), axis=0)


def down_rows(v):
    return jnp.sum(v, axis=0, keepdims=True)


def rows32(i):
    return pl.ds(pl.multiple_of(i * 32, 32), 32)


class TensorSum:
    def __init__(self, here, sems, p, lc, lx, out):
        self.sems, self.p, self.lc, self.lx, self.out = sems, p, lc, lx, out
        self.core = here.dev(c=1 - here.c)
        self.across = here.dev(h=1 - here.h)
        self.mine = pl.ds(pl.multiple_of(here.c * 128, 128), 128)
        self.other = pl.ds(pl.multiple_of((1 - here.c) * 128, 128), 128)
        self.a, self.b, self.d = [], [], []

    def first(self, n):
        self.a.append(self.sems.copy(self.p.at[n, self.other], self.lc.at[n], self.core))

    def second(self, n):
        self.a[n].wait_recv()
        self.p[n, self.mine] = self.p[n, self.mine] + self.lc[n]
        self.b.append(self.sems.copy(self.p.at[n, self.mine], self.lx.at[n], self.across))

    def third(self, n):
        self.b[n].wait_recv()
        self.out[self.mine, COLS[n]] = self.p[n, self.mine] + self.lx[n]
        spot = self.out.at[self.mine, COLS[n]]
        self.d.append(self.sems.copy(spot, spot, self.core))

    def send(self, make):
        for n in range(4):
            self.p[n] = make(n)
            self.first(n)
            if n:
                self.second(n - 1)
        self.second(3)

    def end(self):
        for n in range(len(self.d), 4):
            self.third(n)
        for cp in self.d:
            cp.wait_recv()
        for cp in self.a + self.b + self.d:
            cp.wait_send()


class RingSum:
    def __init__(self, here, axis, buf, base, rows, l1, l2, sems):
        self.p = getattr(here, axis)
        self.buf, self.base, self.rows = buf, base, rows
        self.l1, self.l2, self.sems = l1, l2, sems
        self.plus, self.minus = here.ring(axis, 1), here.ring(axis, 3)
        self.cps = []

    def part(self, step, half):
        n = self.rows // 2
        at = self.base + ((self.p + step) % 4) * self.rows + half * n
        return pl.ds(pl.multiple_of(at, n), n)

    def own(self):
        at = self.base + self.p * self.rows
        return pl.ds(pl.multiple_of(at, self.rows), self.rows)

    def start(self):
        n, buf, sems = self.rows // 2, self.buf, self.sems
        lo, hi = pl.ds(0, n), pl.ds(n, n)
        self.a = sems.copy(buf.at[self.part(2, 0)], self.l1[0], self.plus)
        self.b = sems.copy(buf.at[self.part(2, 1)], self.l1[1], self.minus)
        self.cps.append(sems.copy(buf.at[self.part(1, 1)], self.l2[0].at[hi], self.plus))
        self.cps.append(sems.copy(buf.at[self.part(3, 0)], self.l2[1].at[lo], self.minus))
        return self

    def middle(self):
        n, buf, sems = self.rows // 2, self.buf, self.sems
        lo, hi = pl.ds(0, n), pl.ds(n, n)
        up, dn = self.part(1, 0), self.part(3, 1)
        self.a.wait_recv()
        buf[up] = buf[up] + self.l1[0][...]
        self.cps.append(sems.copy(buf.at[up], self.l2[0].at[lo], self.plus))
        self.b.wait_recv()
        buf[dn] = buf[dn] + self.l1[1][...]
        self.cps.append(sems.copy(buf.at[dn], self.l2[1].at[hi], self.minus))

    def arrive(self):
        for cp in self.cps:
            cp.wait_recv()
        own = self.own()
        self.buf[own] = self.buf[own] + self.l2[0][...] + self.l2[1][...]

    def done(self):
        for cp in [self.a, self.b] + self.cps:
            cp.wait_send()


class Shared:
    def __init__(self, here, axis, buf, sems):
        self.here, self.axis, self.buf, self.sems = here, axis, buf, sems
        self.p = getattr(here, axis)

    def spot(self, step, half=None):
        at = ((self.p + step) % 4) * 256
        if half is None:
            return pl.ds(pl.multiple_of(at, 256), 256)
        return pl.ds(pl.multiple_of(at + half * 128, 128), 128)

    def start(self, src):
        rows = pl.ds(pl.multiple_of(self.here.c * 128, 128), 128)
        for half in range(2):
            part = src[rows, half * 512 : half * 512 + 512]
            self.buf[self.spot(0, half)] = part.astype(F32)
        mine = self.buf.at[self.spot(0)]
        self.near = [self.sems.copy(mine, mine, self.here.ring(self.axis, s)) for s in (1, 3)]
        return self

    def relay(self):
        self.far = []
        for cp, frm, to, half in ((self.near[0], 3, 1, 0), (self.near[1], 1, 3, 1)):
            cp.wait_recv()
            part = self.buf.at[self.spot(frm, half)]
            self.far.append(self.sems.copy(part, part, self.here.ring(self.axis, to)))

    def arrive(self):
        for cp in self.far:
            cp.wait_recv()

    def done(self):
        for cp in self.near + self.far:
            cp.wait_send()


class Moved:
    def __init__(self, here, axis, lane, ys, gy, sems):
        self.here, self.axis, self.ys, self.gy, self.sems = here, axis, ys, gy, sems
        self.lanes = pl.ds(lane, 256)

    def start(self, src):
        here, ys, gy, lanes = self.here, self.ys, self.gy, self.lanes
        c = here.c
        for q in range(4):
            ys[q * 256 : q * 256 + 256, lanes] = src[:, q * 256 : q * 256 + 256].astype(F32)
        self.cps = []
        for step in (1, 3, 2, 0):
            for dc in range(2):
                axis = self.axis if dc == 0 else OTHER[self.axis]
                p, e = getattr(here, axis), (c + dc) % 2
                q = (p + step) % 4
                spot = pl.ds(pl.multiple_of(p * 256 + c * 128, 128), 128)
                rows = pl.ds(pl.multiple_of(q * 256 + e * 128, 128), 128)
                if step == 0 and dc == 0:
                    gy[spot, lanes] = ys[rows, lanes]
                    continue
                to = here.ring(axis, step, c=e)
                self.cps.append(self.sems.copy(ys.at[rows, lanes], gy.at[spot, lanes], to))
        return self

    def sent(self):
        for cp in self.cps:
            cp.wait_send()

    def arrive(self):
        for cp in self.cps:
            cp.wait_recv()


class ExpertGrads:
    def __init__(self, here, m, shared, moved, right, part, l1, l2, lx, land, sems, gates=None):
        self.here, self.m, self.shared, self.moved, self.right = here, m, shared, moved, right
        self.part, self.lx, self.land, self.sems, self.gates = part, lx, land, sems, gates
        self.axis = "ab"[m]
        self.ring = RingSum(here, OTHER[self.axis], part, 0, 256, l1, l2, sems)

    def multiply(self):
        self.shared.arrive()
        self.moved.arrive()
        gs, gy, lanes = self.shared.buf, self.moved.gy, self.moved.lanes
        for p in range(4):
            for k in range(2):
                rows = pl.ds(p * 256 + k * 128, 128)
                self.right[p * 128 : p * 128 + 128, k * 256 : k * 256 + 256] = gy[rows, lanes].astype(BF)
        gates = self.gates() if self.gates else None
        ring_on_y = (self.m + self.here.c) % 2
        per_y, per_z = 32 + 224 * ring_on_y, 256 - 224 * ring_on_y

        def block(k, carry):
            lanes = pl.ds(pl.multiple_of((k % 4) * 128, 128), 128)
            left = []
            for p in range(4):
                v = gs[pl.ds(pl.multiple_of(p * 256 + (k // 4) * 128, 128), 128), lanes]
                left.append((v if gates is None else gates[p] * v).astype(BF))
            res = tn(jnp.concatenate(left, axis=0), self.right[...])
            for z in range(4):
                at = (k // 4) * 128 + (k % 4) * per_y + z * per_z
                self.part[pl.ds(pl.multiple_of(at, 32), 32)] = res[z * 32 : z * 32 + 32]
            return carry

        lax.fori_loop(0, 8, block, 0)
        self.ring.start()

    def send_x(self, base, rows):
        here = self.here
        away = pl.ds(pl.multiple_of(base + (1 - here.x) * rows, rows), rows)
        self.swap = self.sems.copy(self.part.at[away], self.lx, here.dev(x=1 - here.x))

    def add_x(self, base, rows):
        self.swap.wait_recv()
        mine = pl.ds(pl.multiple_of(base + self.here.x * rows, rows), rows)
        self.part[mine] = self.part[mine] + self.lx[...]

    def across(self):
        self.ring.arrive()
        self.send_x(self.ring.p * 256, 128)

    def spread(self):
        here = self.here
        self.add_x(self.ring.p * 256, 128)
        base = self.ring.p * 256 + here.x * 128
        p, c = getattr(here, self.axis), here.c
        self.last = []
        for step in (1, 3, 2, 0):
            for dc in range(2):
                q, k = (p + step) % 4, (c + dc) % 2
                rows = pl.ds(pl.multiple_of(base + q * 32, 32), 32)
                lanes = pl.ds(pl.multiple_of(k * 256, 256), 256)
                if step == 0 and dc == 0:
                    self.land[p, c] = self.part[rows, lanes]
                    continue
                self.last.append(
                    self.sems.copy(
                        self.part.at[rows, lanes],
                        self.land.at[p, c],
                        here.ring(self.axis, step, c=k),
                    )
                )

    def finish(self, out, j):
        for cp in self.last:
            cp.wait_recv()
        for e in range(2):
            for q in range(4):
                out[e, j, :, q * 256 : q * 256 + 256] = self.land[q, e]
        for cp in [self.swap] + self.last:
            cp.wait_send()
        self.ring.done()


INPUTS = (
    "tok", "seg", "routes", "slots", "ln_gain", "ln_shift", "qkv_w", "qv_bias", "out_w", "out_bias",
    "cent", "ffn_gain", "ffn_shift", "up_w", "up_bias", "down_w", "down_bias", "cot",
)
IN_HBM = ("up_w", "down_w", "qkv_w", "out_w")
OUTPUTS = {
    "result": ((256, 1024), BF),
    "tokens_grad": ((256, 1024), BF),
    "qkv_grad": ((3, 32, 256), F32),
    "out_grad": ((32, 256), F32),
    "up_grad": ((2, 2, 32, 1024), F32),
    "down_grad": ((2, 2, 32, 1024), F32),
    "sums": ((24, 1024), F32),
}
PART = ((1024, 512), F32)
SQUARE = ((256, 1024), F32)
LOW = ((256, 1024), BF)
SCRATCH = {
    "wqkv": ((3, 1024, 256), BF), "wout": ((256, 1024), BF),
    "wup": ((2, 1024, 1024), BF), "wdn": ((2, 1024, 1024), BF),
    "normed": LOW, "q": ((256, 256), BF), "k": ((256, 256), BF), "v": ((256, 256), BF),
    "mixed": ((256, 256), BF), "probs": ((4, 256, 256), F32),
    "gq": ((256, 256), BF), "gk": ((256, 256), BF), "gv": ((256, 256), BF),
    "hot_s": ((256, 256), BF), "hot_t": ((256, 256), BF),
    "valid": ((256, 1), F32), "filled": ((256, 1), F32), "route": ((256, 1), F32),
    "sig": ((256, 1), F32), "gating": ((256, 1), F32), "segc": ((256, 1), F32),
    "hidden": SQUARE, "rows0": SQUARE, "rows1": SQUARE, "rows2": SQUARE,
    "slope0": SQUARE, "gwork": SQUARE, "grows": SQUARE, "ghidden": SQUARE,
    "n": LOW, "act": LOW, "go": LOW, "gp": LOW,
    "pa": ((4, 256, 256), F32), "lca": ((4, 128, 256), F32), "lxa": ((2, 4, 128, 256), F32),
    "pb": ((4, 256, 256), F32), "lcb": ((4, 128, 256), F32), "lxb": ((4, 128, 256), F32),
    "gs0u": PART, "gs0w": PART, "gs1u": PART, "gs1w": PART,
    "ys": PART, "gy0": PART, "gy1": PART,
    "right": ((512, 512), BF),
    "partu": PART, "partw": PART,
    "l1": ((2, 2, 128, 512), F32), "l2": ((2, 2, 256, 512), F32),
    "lx": ((2, 2, 128, 512), F32), "gates": ((4, 8, 128), F32), "land": ((2, 2, 4, 2, 32, 256), F32),
    "a1": ((2, 2, 128, 512), F32), "a2": ((2, 2, 256, 512), F32),
    "b1": ((2, 2, 32, 512), F32), "b2": ((2, 2, 64, 512), F32), "ax": ((2, 32, 512), F32),
    "vb": ((11, 24, 1024), F32),
}
N_SEMS = 240


class Totals:
    def __init__(self, here, buf, sems):
        self.here, self.buf, self.sems, self.cps, self.wait = here, buf, sems, [], []

    def send(self, at, to, devices):
        spots = self.buf.at[at], self.buf.at[to]
        self.wait = [self.sems.copy(*spots, dev) for dev in devices]
        self.cps += self.wait

    def four(self, at):
        for cp in self.wait:
            cp.wait_recv()
        buf = self.buf
        return (buf[at] + buf[at + 1]) + (buf[at + 2] + buf[at + 3])

    def ring_y(self):
        at = 1 + self.here.y
        self.buf[at] = self.buf[0]
        self.send(at, at, [self.here.ring("y", step) for step in (1, 3, 2)])

    def ring_z(self):
        at = 5 + self.here.z
        self.buf[at] = self.four(1)
        self.send(at, at, [self.here.ring("z", step) for step in (1, 3, 2)])

    def pair(self):
        self.buf[9] = self.four(5)
        self.send(9, 10, [self.here.dev(x=1 - self.here.x)])

    def finish(self, out):
        self.wait[0].wait_recv()
        out[...] = self.buf[9] + self.buf[10]

    def done(self):
        for cp in self.cps:
            cp.wait_send()


ORDER = (
    "n1_relay", "gp0", "mul10", "back0_0", "go0_relay", "mul11", "rows2", "result", "mul00",
    "back0_1", "mul01", "back0_2", "back0_end", "attention", "mid10", "mid00", "mid11", "x10",
    "back_0", "mid01", "back_1", "attn1", "x01", "back_2", "tokens", "attn_mid1", "x11", "attn0",
    "x00", "sums_z", "attn_mid0", "attn_next1", "spread01", "attn_next0", "attn_mid_next1",
    "sums_x", "spread11", "attn_mid_next0", "spread00", "spread10", "sums_out", "attn_x1",
    "attn_x0", "out00", "out01", "attn_out1", "out10", "out11", "attn_out0",
)


class Bag:
    pass


def two(ref):
    return [ref.at[0], ref.at[1]]


def layer_kernel(*refs):
    B = Bag()
    for name, ref in zip([*INPUTS, *OUTPUTS, *SCRATCH, "ss", "rs", "ws", "free"], refs):
        setattr(B, name, ref)
    B.n0 = B.n1 = B.gbranch = B.n
    B.act0 = B.act1 = B.act
    B.go0 = B.go1 = B.go
    B.gp0 = B.gp1 = B.gp
    here = Here()
    sems = Sems(B.ss, B.rs)
    x, c = here.x, here.c
    vec = B.vb.at[0]

    peers = [here.dev(c=1 - c), here.dev(h=1 - here.h), here.dev(x=1 - x)]
    for axis in ("y", "z"):
        for step in (1, 2, 3):
            for dc in range(2):
                peers.append(here.ring(axis, step, c=(c + dc) % 2))
    bar = pltpu.get_barrier_semaphore()
    for dev in peers:
        pl.semaphore_signal(bar, inc=1, device_id=dev, device_id_type=MESH)

    def fetch(pairs, at):
        cps = [pltpu.make_async_copy(s, t, B.ws.at[at + k]) for k, (s, t) in enumerate(pairs)]
        for cp in cps:
            cp.start()
        return cps

    def fetch_experts(j):
        return fetch(
            [(B.up_w.at[e, j], B.wup.at[e]) for e in range(2)]
            + [(B.down_w.at[e, j], B.wdn.at[e]) for e in range(2)],
            2,
        )

    heads = fetch([(B.qkv_w, B.wqkv), (B.out_w, B.wout)], 0)
    experts = fetch_experts(0)

    B.vb[0] = jnp.zeros((24, 1024), F32)
    lane1024 = lax.broadcasted_iota(jnp.int32, (1, 1024), 1)

    def stat(k, total):
        row = jnp.where(lane1024 == k, total, 0.0)
        vec[STATS : STATS + 1] = vec[STATS : STATS + 1] + row

    def total(v):
        return jnp.sum(jnp.sum(v, axis=1, keepdims=True), axis=0, keepdims=True)

    down_i = lax.broadcasted_iota(jnp.int32, (256, 256), 0)
    along_i = lax.broadcasted_iota(jnp.int32, (256, 256), 1)

    def column(row):
        return jnp.sum(jnp.where(down_i == along_i, row, 0.0), axis=1, keepdims=True)

    seg_row = B.seg[...].astype(F32)
    B.segc[...] = column(seg_row)
    B.valid[...] = (B.segc[...] != 0.0).astype(F32)

    def allowed():
        return (B.segc[...] == seg_row) & (along_i <= down_i) & (B.segc[...] != 0.0)

    head_of = along_i // HD

    gain = B.ln_gain[...].astype(F32).reshape(1, 1024)
    shift = B.ln_shift[...].astype(F32).reshape(1, 1024)

    def norm_block(i, carry):
        n, _ = unit(B.tok[rows32(i)].astype(F32))
        B.normed[rows32(i)] = (n * gain + shift).astype(BF)
        return carry

    lax.fori_loop(0, 8, norm_block, 0)
    for cp in heads:
        cp.wait()
    qv_bias = B.qv_bias[...].astype(F32)
    B.q[...] = (nn(B.normed[...], B.wqkv[0]) + qv_bias[0:1]).astype(BF)
    B.k[...] = nn(B.normed[...], B.wqkv[1]).astype(BF)
    B.v[...] = (nn(B.normed[...], B.wqkv[2]) + qv_bias[1:2]).astype(BF)

    def one_head(value, hh):
        return jnp.where(head_of == hh, value.astype(F32), 0.0)

    mixed = jnp.zeros((256, 256), F32)
    for hh in range(4):
        s = nt(one_head(B.q[...], hh).astype(BF), B.k[...]) * SCALE
        ok = allowed()
        s = jnp.where(ok, s, -1e30)
        e = jnp.where(ok, jnp.exp(s - jnp.max(s, axis=-1, keepdims=True)), 0.0)
        probs = e / (jnp.sum(e, axis=-1, keepdims=True) + (1.0 - B.valid[...]))
        B.probs[hh] = probs
        mixed = mixed + one_head(nn(probs.astype(BF), B.v[...]), hh)
    B.mixed[...] = mixed.astype(BF)

    pl.semaphore_wait(bar, len(peers))
    branch = TensorSum(here, sems, B.pa, B.lca, B.lxa.at[0], B.hidden)
    branch.send(lambda n: nn(B.mixed[...], B.wout[:, COLS[n]]))
    slot_row = jnp.concatenate([B.slots[0, 0:1], B.slots[0, 1:2]], axis=1)
    slot_col = column(slot_row.astype(F32))
    B.hot_s[...] = jnp.where(slot_col == along_i.astype(F32), 1.0, 0.0).astype(BF)
    for n in range(4):
        B.grows[:, COLS[n]] = nn(B.hot_s[...], B.cot[:, COLS[n]])
    s1w = Shared(here, "b", B.gs1w, sems).start(B.grows)
    B.route[...] = column(B.routes[...].astype(F32))
    B.filled[...] = (slot_col < 256.0).astype(F32)
    B.hot_t[...] = jnp.where(slot_row == down_i, 1.0, 0.0).astype(BF)
    stat(4, total(B.valid[...]))
    for n in range(2):
        branch.third(n)
    s1w.relay()
    branch.end()

    out_bias = B.out_bias[...].astype(F32).reshape(1, 1024)
    cent = B.cent[...].astype(F32)

    def hidden_block(i, carry):
        rows = rows32(i)
        h = B.tok[rows].astype(F32) + (B.hidden[rows] + out_bias)
        B.hidden[rows] = h
        scores = [jnp.sum(h * cent[e : e + 1], axis=-1, keepdims=True) for e in range(2)]
        logits = jnp.where(B.route[rows] == 1.0, scores[1], scores[0])
        sig = 1.0 / (1.0 + jnp.exp(-logits))
        B.sig[rows] = sig
        B.gating[rows] = sig * B.valid[rows]
        return carry + fold(h * h * B.valid[rows])

    stat(0, total(lax.fori_loop(0, 8, hidden_block, jnp.zeros((8, 1024), F32))))
    for n in range(4):
        B.rows0[:, COLS[n]] = pick(B.hot_s[...], B.hidden[:, COLS[n]])
    ffn_gain = B.ffn_gain[...].astype(F32)
    ffn_shift = B.ffn_shift[...].astype(F32)
    up_bias = B.up_bias[...].astype(F32)
    down_bias = B.down_bias[...].astype(F32)

    def expert_norm(rows_ref, low_ref, j):
        for e in range(2):
            g, s = ffn_gain[e, j : j + 1], ffn_shift[e, j : j + 1]

            def block(i, carry, e=e, g=g, s=s):
                rows = rows32(e * 4 + i)
                n, _ = unit(rows_ref[rows])
                low_ref[rows] = (n * g + s).astype(BF)
                return carry

            lax.fori_loop(0, 4, block, 0)

    def gelu_parts(v):
        t = jnp.tanh(ROOT * (v + 0.044715 * (v * v * v)))
        cdf = 0.5 * (1.0 + t)
        slope = cdf + (0.5 * ROOT) * v * (1.0 - t * t) * (1.0 + (3.0 * 0.044715) * (v * v))
        return v * cdf, slope

    def half(e):
        return pl.ds(e * 128, 128)

    expert_norm(B.rows0, B.n0, 0)
    s0u = Shared(here, "a", B.gs0u, sems).start(B.n0)
    for cp in experts:
        cp.wait()
    for e in range(2):
        for n in range(4):
            pre = nn(B.n0[half(e)], B.wup[e, :, COLS[n]]) + up_bias[e, 0:1, n * 256 : n * 256 + 256]
            act, slope = gelu_parts(pre)
            B.act0[half(e), COLS[n]] = act.astype(BF)
            B.slope0[half(e), COLS[n]] = slope

    def down(act_ref):
        def make(n):
            return jnp.concatenate(
                [nn(act_ref[half(e)], B.wdn[e, :, COLS[n]]) for e in range(2)], axis=0
            )

        return make

    first = TensorSum(here, sems, B.pa, B.lca, B.lxa.at[1], B.rows1)
    first.send(down(B.act0))
    experts = fetch_experts(1)
    m0w = Moved(here, "b", 256, B.ys, B.gy0, sems).start(B.act0)
    gate_row = down_rows(B.hot_t[...].astype(F32) * B.gating[...])
    gate_col = column(gate_row)
    B.gates[here.b] = jnp.broadcast_to(jnp.where(c == 0, gate_row[:, :128], gate_row[:, 128:]), (8, 128))
    mine = B.gates.at[here.b]
    gate_cps = [sems.copy(mine, mine, here.ring("b", step)) for step in (1, 3, 2)]
    for n in range(4):
        g = gate_col * B.grows[:, COLS[n]]
        B.grows[:, COLS[n]] = g
        B.go1[:, COLS[n]] = g.astype(BF)
    for e in range(2):
        vec[DOWN_B + e * 2 + 1 : DOWN_B + e * 2 + 2] = down_rows(B.go1[half(e)].astype(F32))
    for cp in experts:
        cp.wait()
    for e in range(2):
        for n in range(4):
            B.gwork[half(e), COLS[n]] = nt(B.go1[half(e)], B.wdn[e, COLS[n], :])
    for n in range(3):
        first.third(n)
    s0u.relay()
    first.end()

    sq = jnp.zeros((8, 1024), F32)
    for e in range(2):
        bias = down_bias[e, 0:1]

        def rows1_block(i, carry, e=e, bias=bias):
            rows = rows32(e * 4 + i)
            r1 = B.rows0[rows] + (B.rows1[rows] + bias)
            B.rows1[rows] = r1
            return carry + fold(r1 * r1 * B.filled[rows])

        sq = lax.fori_loop(0, 4, rows1_block, sq)
    stat(1, total(sq))
    expert_norm(B.rows1, B.n1, 1)
    s1u = Shared(here, "a", B.gs1u, sems).start(B.n1)
    for e in range(2):
        for n in range(4):
            pre = nn(B.n1[half(e)], B.wup[e, :, COLS[n]]) + up_bias[e, 1:2, n * 256 : n * 256 + 256]
            act, slope = gelu_parts(pre)
            B.act1[half(e), COLS[n]] = act.astype(BF)
            gp = (B.gwork[half(e), COLS[n]] * slope).astype(BF)
            B.gp1[half(e), COLS[n]] = gp
            vec[UP_B + e * 2 + 1 : UP_B + e * 2 + 2, COLS[n]] = down_rows(gp.astype(F32))

    def normed_grad(gp_ref):
        def make(n):
            return jnp.concatenate(
                [nt(gp_ref[half(e)], B.wup[e, COLS[n], :]) for e in range(2)], axis=0
            )

        return make

    back1 = TensorSum(here, sems, B.pa, B.lca, B.lxa.at[0], B.gwork)
    back1.send(normed_grad(B.gp1))
    m1u = Moved(here, "a", 0, B.ys, B.gy1, sems).start(B.gp1)
    second = TensorSum(here, sems, B.pb, B.lcb, B.lxb, B.rows2)
    second.send(down(B.act1))
    experts = fetch_experts(0)
    m0w.sent()
    m1w = Moved(here, "b", 256, B.ys, B.gy1, sems).start(B.act1)
    back1.end()

    def expert_norm_back(rows_ref, j, go_ref):
        for e in range(2):
            g = ffn_gain[e, j : j + 1]

            def block(i, carry, e=e, g=g):
                rows = rows32(e * 4 + i)
                n, r = unit(rows_ref[rows])
                gn = B.gwork[rows]
                new = B.grows[rows] + unit_back(gn, g, n, r)
                B.grows[rows] = new
                out = [carry[0] + fold(gn * n), carry[1] + fold(gn)]
                if go_ref is not None:
                    low = new.astype(BF)
                    go_ref[rows] = low
                    out.append(carry[2] + fold(low.astype(F32)))
                return tuple(out)

            zero = jnp.zeros((8, 1024), F32)
            sums = lax.fori_loop(0, 4, block, (zero,) * (2 if go_ref is None else 3))
            at = e * 2 + j
            vec[GAIN + at : GAIN + at + 1] = down_rows(sums[0])
            vec[SHIFT + at : SHIFT + at + 1] = down_rows(sums[1])
            if go_ref is not None:
                vec[DOWN_B + e * 2 : DOWN_B + e * 2 + 1] = down_rows(sums[2])

    expert_norm_back(B.rows1, 1, B.go0)
    s0w = Shared(here, "b", B.gs0w, sems).start(B.go0)
    for cp in experts:
        cp.wait()
    for e in range(2):
        for n in range(4):
            ga = nt(B.go0[half(e)], B.wdn[e, COLS[n], :])
            gp = (ga * B.slope0[half(e), COLS[n]]).astype(BF)
            B.gp0[half(e), COLS[n]] = gp
            vec[UP_B + e * 2 : UP_B + e * 2 + 1, COLS[n]] = down_rows(gp.astype(F32))
    back0 = TensorSum(here, sems, B.pa, B.lca, B.lxa.at[1], B.gwork)
    back0.send(normed_grad(B.gp0))
    state = {}
    def slot_gates():
        for cp in gate_cps:
            cp.wait_recv()
        eye = down_i[:128, :128] == along_i[:128, :128]
        return [
            jnp.sum(jnp.where(eye, B.gates[p, 0:1], 0.0), axis=1, keepdims=True) for p in range(4)
        ]

    eg1 = [
        ExpertGrads(here, m, (s1u, s1w)[m], (m1u, m1w)[m], B.right, (B.partu, B.partw)[m],
                    two(B.l1.at[m]), two(B.l2.at[m]), B.lx.at[0, m], B.land.at[0, m], sems,
                    gates=(None, slot_gates)[m])
        for m in range(2)
    ]
    m0u = Moved(here, "a", 0, B.ys, B.gy0, sems)
    wide = [pl.ds(0, 512), pl.ds(512, 512)]
    eg0 = [
        ExpertGrads(here, m, (s0u, s0w)[m], (m0u, m0w)[m], B.right, (B.ys, B.gy1)[m],
                    [B.slope0.at[pl.ds(128 * k, 128), wide[m]] for k in range(2)],
                    [(B.hidden, B.rows2)[m].at[:, wide[k]] for k in range(2)],
                    B.lx.at[1, m], B.land.at[1, m], sems)
        for m in range(2)
    ]
    lefts = (B.normed, B.normed, B.normed, B.gbranch)
    rights = (B.gq, B.gk, B.gv, B.mixed)
    apart = (B.gs1u, B.gs1w)
    rings, rings2, swaps = {}, {}, {}
    gather = Totals(here, B.vb, sems)

    def move_gp0():
        m1u.sent()
        m0u.start(B.gp0)

    def result():
        sq = jnp.zeros((8, 1024), F32)
        for e in range(2):
            bias = down_bias[e, 1:2]

            def rows2_block(i, carry, e=e, bias=bias):
                rows = rows32(e * 4 + i)
                r2 = B.rows1[rows] + (B.rows2[rows] + bias)
                B.rows2[rows] = r2
                return carry + fold(r2 * r2 * B.filled[rows])

            sq = lax.fori_loop(0, 4, rows2_block, sq)
        stat(2, total(sq))
        gate_grad = jnp.zeros((256, 1), F32)
        result_sq = jnp.zeros((256, 1), F32)
        for n in range(4):
            comb = pick(B.hot_t[...], B.rows2[:, COLS[n]])
            res = B.hidden[:, COLS[n]] + B.gating[...] * comb
            B.result[:, COLS[n]] = res.astype(BF)
            result_sq = result_sq + jnp.sum(res * res, axis=-1, keepdims=True)
            gate_grad = gate_grad + jnp.sum(B.cot[:, COLS[n]].astype(F32) * comb, axis=-1, keepdims=True)
        stat(3, total(result_sq * B.valid[...]))
        B.gating[...] = gate_grad * B.sig[...] * (1.0 - B.sig[...]) * B.valid[...]

        def gate_block(i, carry):
            rows = rows32(i)
            gl, second_route = B.gating[rows], B.route[rows] == 1.0
            B.ghidden[rows] = B.cot[rows].astype(F32) + gl * jnp.where(second_route, cent[1:2], cent[0:1])
            v = gl * B.hidden[rows]
            return (
                carry[0] + fold(jnp.where(second_route, 0.0, v)),
                carry[1] + fold(jnp.where(second_route, v, 0.0)),
            )

        zero = jnp.zeros((8, 1024), F32)
        sums = lax.fori_loop(0, 8, gate_block, (zero, zero))
        for e in range(2):
            vec[CENT + e : CENT + e + 1] = down_rows(sums[e])
        for k, axis in enumerate(("b", "a")):
            for step in (1, 3):
                pl.semaphore_signal(
                    B.free.at[k], inc=1, device_id=here.ring(axis, step), device_id_type=MESH
                )

    def attention_back():
        expert_norm_back(B.rows0, 0, None)
        for n in range(4):
            g = B.ghidden[:, COLS[n]] + pick(B.hot_t[...], B.grows[:, COLS[n]])
            B.ghidden[:, COLS[n]] = g
            low = g.astype(BF)
            B.gbranch[:, COLS[n]] = low
            vec[OUT_BIAS : OUT_BIAS + 1, COLS[n]] = down_rows(low.astype(F32))
        gm = nt(B.gbranch[...], B.wout[...]).astype(BF)
        gq = jnp.zeros((256, 256), F32)
        gk = jnp.zeros((256, 256), F32)
        gv = jnp.zeros((256, 256), F32)
        for hh in range(4):
            probs = B.probs[hh]
            gp = nt(one_head(gm, hh).astype(BF), B.v[...])
            gv = gv + one_head(tn(probs.astype(BF), gm), hh)
            gs = (probs * (gp - jnp.sum(probs * gp, axis=-1, keepdims=True))).astype(BF)
            gq = gq + one_head(nn(gs, B.k[...]), hh)
            gk = gk + one_head(tn(gs, B.q[...]), hh)
        B.gq[...] = (gq * SCALE).astype(BF)
        B.gk[...] = (gk * SCALE).astype(BF)
        B.gv[...] = gv.astype(BF)
        vec[QV_B : QV_B + 1, 0:256] = down_rows(B.gq[...].astype(F32))
        vec[QV_B : QV_B + 1, 256:512] = down_rows(B.gv[...].astype(F32))
        state["back"] = back = TensorSum(here, sems, B.pa, B.lca, B.lxa.at[0], B.gwork)
        grads = (B.gq, B.gk, B.gv)
        back.send(lambda n: sum(nt(grads[s][...], B.wqkv[s, COLS[n], :]) for s in range(3)))


    def first_sublayer(m):
        if m == 0:
            m1w.sent()
            m0u.sent()
        pl.semaphore_wait(B.free.at[m], 2)
        eg0[m].multiply()

    def attention_grads(m):
        (s1u, s1w)[m].done()
        last_y = (m + c) % 2
        for j in range(2):

            def block(k, carry, m=m, last_y=last_y, left=lefts[2 * m + j], right=rights[2 * m + j], j=j):
                lanes = pl.ds(pl.multiple_of(k * 128, 128), 128)
                res = tn(left[:, lanes], right[...])
                for z in range(4):
                    at = (k // 4) * 32 + (k % 4) * (256 - 192 * last_y) + z * (64 + 192 * last_y)
                    apart[m][pl.ds(pl.multiple_of(at, 32), 32), j * 256 : j * 256 + 256] = res[
                        z * 32 : z * 32 + 32
                    ]
                return carry

            lax.fori_loop(0, 8, block, 0)
        rings[m] = RingSum(here, "ab"[m], apart[m], 0, 256, two(B.a1.at[m]), two(B.a2.at[m]), sems)
        rings[m].start()

    def tokens_back():
        state["back"].end()
        zero = jnp.zeros((8, 1024), F32)

        def last_block(i, carry):
            rows = rows32(i)
            n, r = unit(B.tok[rows].astype(F32))
            gn = B.gwork[rows]
            B.tokens_grad[rows] = (B.ghidden[rows] + unit_back(gn, gain, n, r)).astype(BF)
            return carry[0] + fold(gn * n), carry[1] + fold(gn)

        sums = lax.fori_loop(0, 8, last_block, (zero, zero))
        vec[LN_GAIN : LN_GAIN + 1] = down_rows(sums[0])
        vec[LN_SHIFT : LN_SHIFT + 1] = down_rows(sums[1])
        gather.ring_y()

    def second_ring(m):
        rings[m].arrive()
        base = rings[m].p * 256
        b1, b2 = two(B.b1.at[m]), two(B.b2.at[m])
        rings2[m] = RingSum(here, "ba"[m], apart[m], base, 64, b1, b2, sems)
        rings2[m].start()

    def attention_swap(m):
        rings2[m].arrive()
        base = rings2[m].base + rings2[m].p * 64
        away = pl.ds(pl.multiple_of(base + (1 - x) * 32, 32), 32)
        swaps[m] = sems.copy(apart[m].at[away], B.ax.at[m], here.dev(x=1 - x))

    def attention_out(m):
        swaps[m].wait_recv()
        base = rings2[m].base + rings2[m].p * 64
        mine = apart[m][pl.ds(pl.multiple_of(base + x * 32, 32), 32)] + B.ax[m]
        if m == 0:
            B.qkv_grad[0] = mine[:, :256]
            B.qkv_grad[1] = mine[:, 256:]
        else:
            B.qkv_grad[2] = mine[:, :256]
            B.out_grad[...] = mine[:, 256:]

    steps = {
        "n1_relay": s1u.relay,
        "gp0": move_gp0,
        "rows2": second.end,
        "result": result,
        "go0_relay": s0w.relay,
        "back0_end": back0.end,
        "attention": attention_back,
        "tokens": tokens_back,
        "sums_z": gather.ring_z,
        "sums_x": gather.pair,
        "sums_out": lambda: gather.finish(B.sums),
    }
    for n in range(3):
        steps[f"back0_{n}"] = lambda n=n: back0.third(n)
        steps[f"back_{n}"] = lambda n=n: state["back"].third(n)
    for m in range(2):
        for j, g in ((1, eg1[m]), (0, eg0[m])):
            at = f"{j}{m}"
            steps["mul" + at] = g.multiply if j else lambda m=m: first_sublayer(m)
            steps["mid" + at] = g.ring.middle
            steps["x" + at] = g.across
            steps["spread" + at] = g.spread
            steps["out" + at] = lambda g=g, m=m, j=j: g.finish((B.up_grad, B.down_grad)[m], j)
        steps[f"attn{m}"] = lambda m=m: attention_grads(m)
        steps[f"attn_mid{m}"] = lambda m=m: rings[m].middle()
        steps[f"attn_next{m}"] = lambda m=m: second_ring(m)
        steps[f"attn_mid_next{m}"] = lambda m=m: rings2[m].middle()
        steps[f"attn_x{m}"] = lambda m=m: attention_swap(m)
        steps[f"attn_out{m}"] = lambda m=m: attention_out(m)
    for name in ORDER:
        steps[name]()
    for job in (s0u, s0w, gather, *rings.values(), *rings2.values()):
        job.done()
    for cp in [*swaps.values(), *gate_cps]:
        cp.wait_send()


def finish_kernel(*refs):
    big_in, sums, big_out = refs[:6], refs[6], refs[7:13]
    gain, shift, out_b, cent, ffn_g, ffn_s, down_b, up_b, qv_b, rms, sem = refs[13:]
    cps = [pltpu.make_async_copy(a, b, sem.at[k]) for k, (a, b) in enumerate(zip(big_in, big_out))]
    for cp in cps:
        cp.start()
    d = lax.axis_index("dp")
    near = sums[:, pl.ds(pl.multiple_of((d // 4) * 128, 128), 128)]
    share = near[:, :32]
    for k in range(1, 4):
        share = jnp.where(d % 4 == k, near[:, k * 32 : k * 32 + 32], share)
    for ref, at in ((gain, LN_GAIN), (shift, LN_SHIFT), (out_b, OUT_BIAS)):
        ref[...] = share[at : at + 1]
    cent[...] = share[CENT : CENT + 2]
    for ref, at in ((ffn_g, GAIN), (ffn_s, SHIFT), (down_b, DOWN_B)):
        for e in range(2):
            ref[e] = share[at + e * 2 : at + e * 2 + 2]
    for e in range(2):
        up_b[e] = sums[UP_B + e * 2 : UP_B + e * 2 + 2]
    qv_b[0:1] = sums[QV_B : QV_B + 1, 0:256]
    qv_b[1:2] = sums[QV_B : QV_B + 1, 256:512]
    totals = sums[STATS : STATS + 1, 0:128]
    rms[...] = jnp.sqrt(totals[:, :4] / (totals[:, 4:5] * 1024.0))
    for cp in cps:
        cp.wait()


SMALL = [(1, 32), (1, 32), (1, 32), (2, 32), (2, 2, 32), (2, 2, 32), (2, 2, 32), (2, 2, 1024), (2, 256), (1, 4)]


def local(
    tokens, segments, routes, slot_table, ln_gain, ln_shift, qkv_proj, qv_bias, out_proj, out_bias,
    centroids, ffn_gain, ffn_shift, up_proj, up_bias, down_proj, down_bias, cotangent,
):
    in_specs = [
        pl.BlockSpec(memory_space=pl.ANY if name in IN_HBM else VM) for name in INPUTS
    ]
    outs = pl.pallas_call(
        layer_kernel,
        out_shape=tuple(jax.ShapeDtypeStruct(*spec) for spec in OUTPUTS.values()),
        in_specs=in_specs,
        out_specs=[pl.BlockSpec(memory_space=VM)] * len(OUTPUTS),
        scratch_shapes=[VM(*spec) for spec in SCRATCH.values()]
        + [pltpu.SemaphoreType.DMA((N_SEMS,)), pltpu.SemaphoreType.DMA((N_SEMS,)), pltpu.SemaphoreType.DMA((6,)), pltpu.SemaphoreType.REGULAR((2,))],
        compiler_params=pltpu.CompilerParams(
            collective_id=0, has_side_effects=True, vmem_limit_bytes=VMEM_LIMIT
        ),
    )(
        tokens, segments.reshape(1, 256), routes.reshape(1, 256), slot_table,
        ln_gain, ln_shift, qkv_proj, qv_bias, out_proj,
        out_bias, centroids, ffn_gain, ffn_shift, up_proj, up_bias, down_proj,
        down_bias, cotangent,
    )
    anywhere = pl.BlockSpec(memory_space=pl.ANY)
    near = pl.BlockSpec(memory_space=VM)
    (
        result, tokens_grad, qkv_grad, out_grad, up_grad, down_grad,
        gain, shift, out_b, cent, ffn_g, ffn_s, down_b, up_b, qv_b, rms,
    ) = pl.pallas_call(
        finish_kernel,
        out_shape=tuple(jax.ShapeDtypeStruct(a.shape, a.dtype) for a in outs[:6])
        + tuple(jax.ShapeDtypeStruct(shape, F32) for shape in SMALL),
        in_specs=[near] * 7,
        out_specs=[anywhere] * 6 + [near] * len(SMALL),
        scratch_shapes=[pltpu.SemaphoreType.DMA((6,))],
    )(*outs)
    return (
        result,
        tokens_grad,
        gain.reshape(32),
        shift.reshape(32),
        qkv_grad,
        qv_b,
        out_grad.T,
        out_b.reshape(32),
        cent,
        ffn_g,
        ffn_s,
        up_grad,
        up_b,
        jnp.swapaxes(down_grad, 2, 3),
        down_b,
        rms.reshape(4),
    )


VMEM_LIMIT = 63 * 2**20


def solution(mesh):
    return jax.shard_map(
        local,
        mesh=mesh,
        in_specs=(
            P("dp", None),
            P("dp"),
            P("dp"),
            P("dp", None, None),
            P(),
            P(),
            P(None, None, "tensor"),
            P(None, "tensor"),
            P("tensor", None),
            P(),
            P(),
            P(),
            P(),
            P(None, None, None, "tensor"),
            P(None, None, "tensor"),
            P(None, None, "tensor", None),
            P(),
            P("dp", None),
        ),
        out_specs=(
            P("dp", None),
            P("dp", None),
            P("dp"),
            P("dp"),
            P(None, "dp", "tensor"),
            P(None, "tensor"),
            P("tensor", "dp"),
            P("dp"),
            P(None, "dp"),
            P(None, None, "dp"),
            P(None, None, "dp"),
            P(None, None, "dp", "tensor"),
            P(None, None, "tensor"),
            P(None, None, "tensor", "dp"),
            P(None, None, "dp"),
            P(),
        ),
        check_vma=False,
    )
```

```python
import math

import jax
import jax.numpy as jnp
from jax import lax
from jax.experimental import pallas as pl
from jax.experimental.pallas import tpu as pltpu
from jax.sharding import PartitionSpec as P

HD = 64
MESH = pl.DeviceIdType.MESH
OTHER = {"a": "b", "b": "a"}
VM = pltpu.VMEM
F32 = jnp.float32
BF = jnp.bfloat16
EPS = 1e-05
SCALE = HD ** (-0.5)
ROOT = math.sqrt(2.0 / math.pi)
COLS = [pl.ds(n * 256, 256) for n in range(4)]
LN_GAIN, LN_SHIFT, OUT_BIAS, CENT, GAIN, SHIFT, DOWN_B, UP_B, QV_B, STATS = (
    0, 1, 2, 3, 5, 9, 13, 17, 21, 22,
)


class Here:
    def __init__(self):
        d = lax.axis_index("dp")
        t = lax.axis_index("tensor")
        self.x, self.y, self.z = d // 16, (d // 4) % 4, d % 4
        self.h, self.c = t // 2, t % 2
        self.a = self.y * (1 - self.c) + self.z * self.c
        self.b = self.z * (1 - self.c) + self.y * self.c

    def dev(self, x=None, y=None, z=None, h=None, c=None):
        x = self.x if x is None else x
        y = self.y if y is None else y
        z = self.z if z is None else z
        h = self.h if h is None else h
        c = self.c if c is None else c
        return (x * 16 + y * 4 + z, h * 2 + c)

    def ring(self, axis, step, c=None):
        on_y = {"y": 1, "z": 0, "a": 1 - self.c, "b": self.c}[axis]
        y, z = (self.y + step * on_y) % 4, (self.z + step * (1 - on_y)) % 4
        return self.dev(y=y, z=z, c=c)


class Sems:
    def __init__(self, send, recv):
        self.send, self.recv, self.n = send, recv, 0

    def block(self, n):
        self.n += n
        return self.n - n

    def all_recv(self, k, view):
        pltpu.make_async_copy(view, view, self.recv.at[k]).wait()

    def all_sent(self, k, view):
        pltpu.make_async_copy(view, view, self.send.at[k]).wait()

    def copy(self, src, dst, dev, k=None):
        if k is None:
            k = self.block(1)
        cp = pltpu.make_async_remote_copy(
            src_ref=src,
            dst_ref=dst,
            send_sem=self.send.at[k],
            recv_sem=self.recv.at[k],
            device_id=dev,
            device_id_type=MESH,
        )
        cp.start()
        return cp


def nn(a, b):
    return jnp.dot(a, b, preferred_element_type=F32)


def nt(a, b):
    return lax.dot_general(a, b, (((1,), (1,)), ((), ())), preferred_element_type=F32)


def tn(a, b):
    return lax.dot_general(a, b, (((0,), (0,)), ((), ())), preferred_element_type=F32)


def pick(hot, v):
    a = v.astype(BF)
    rest = v - a.astype(F32)
    b = rest.astype(BF)
    c = (rest - b.astype(F32)).astype(BF)
    return nn(hot, a) + nn(hot, b) + nn(hot, c)


def unit(v):
    center = v - jnp.mean(v, axis=-1, keepdims=True)
    r = lax.rsqrt(jnp.mean(center * center, axis=-1, keepdims=True) + EPS)
    return center * r, r


def unit_back(grad, gain, n, r):
    u = grad * gain
    return r * (u - jnp.mean(u, axis=-1, keepdims=True) - n * jnp.mean(u * n, axis=-1, keepdims=True))


def fold(v):
    return jnp.sum(v.reshape(v.shape[0] // 8, 8, v.shape[1]), axis=0)


def down_rows(v):
    return jnp.sum(v, axis=0, keepdims=True)


def rows32(i):
    return pl.ds(pl.multiple_of(i * 32, 32), 32)


class TensorSum:
    def __init__(self, here, sems, p, lc, lx, out, at):
        self.sems, self.p, self.lc, self.lx, self.out, self.at = sems, p, lc, lx, out, at
        self.core = here.dev(c=1 - here.c)
        self.across = here.dev(h=1 - here.h)
        self.mine = pl.ds(pl.multiple_of(here.c * 128, 128), 128)
        self.other = pl.ds(pl.multiple_of((1 - here.c) * 128, 128), 128)
        self.a, self.b, self.d = [], [], []

    def first(self, n):
        cp = self.sems.copy(self.p.at[n, self.other], self.lc.at[n], self.core, self.at[0] + n)
        self.a.append(cp)

    def second(self, n):
        self.a[n].wait_recv()
        self.p[n, self.mine] = self.p[n, self.mine] + self.lc[n]
        cp = self.sems.copy(self.p.at[n, self.mine], self.lx.at[n], self.across, self.at[1] + n)
        self.b.append(cp)

    def third(self, n):
        self.b[n].wait_recv()
        self.out[self.mine, COLS[n]] = self.p[n, self.mine] + self.lx[n]
        spot = self.out.at[self.mine, COLS[n]]
        self.d.append(self.sems.copy(spot, spot, self.core, self.at[2] + n))

    def send(self, make):
        for n in range(4):
            self.p[n] = make(n)
            self.first(n)
            if n:
                self.second(n - 1)
        self.second(3)

    def end(self):
        for n in range(len(self.d), 4):
            self.third(n)
        for cp in self.d:
            cp.wait_recv()
        for cp in self.a + self.b + self.d:
            cp.wait_send()


class RingSum:
    def __init__(self, here, axis, buf, base, rows, l1, l2, sems):
        self.p = getattr(here, axis)
        self.buf, self.base, self.rows = buf, base, rows
        self.l1, self.l2, self.sems = l1, l2, sems
        self.plus, self.minus = here.ring(axis, 1), here.ring(axis, 3)
        self.cps = []

    def part(self, step, half):
        n = self.rows // 2
        at = self.base + ((self.p + step) % 4) * self.rows + half * n
        return pl.ds(pl.multiple_of(at, n), n)

    def own(self):
        at = self.base + self.p * self.rows
        return pl.ds(pl.multiple_of(at, self.rows), self.rows)

    def start(self):
        n, buf, sems = self.rows // 2, self.buf, self.sems
        lo, hi = pl.ds(0, n), pl.ds(n, n)
        self.a = sems.copy(buf.at[self.part(2, 0)], self.l1[0], self.plus)
        self.b = sems.copy(buf.at[self.part(2, 1)], self.l1[1], self.minus)
        self.cps.append(sems.copy(buf.at[self.part(1, 1)], self.l2[0].at[hi], self.plus))
        self.cps.append(sems.copy(buf.at[self.part(3, 0)], self.l2[1].at[lo], self.minus))
        return self

    def middle(self):
        n, buf, sems = self.rows // 2, self.buf, self.sems
        lo, hi = pl.ds(0, n), pl.ds(n, n)
        up, dn = self.part(1, 0), self.part(3, 1)
        self.a.wait_recv()
        buf[up] = buf[up] + self.l1[0][...]
        self.cps.append(sems.copy(buf.at[up], self.l2[0].at[lo], self.plus))
        self.b.wait_recv()
        buf[dn] = buf[dn] + self.l1[1][...]
        self.cps.append(sems.copy(buf.at[dn], self.l2[1].at[hi], self.minus))

    def arrive(self):
        for cp in self.cps:
            cp.wait_recv()
        own = self.own()
        self.buf[own] = self.buf[own] + self.l2[0][...] + self.l2[1][...]

    def done(self):
        for cp in [self.a, self.b] + self.cps:
            cp.wait_send()


class Shared:
    def __init__(self, here, axis, buf, sems):
        self.here, self.axis, self.buf, self.sems = here, axis, buf, sems
        self.p = getattr(here, axis)

    def spot(self, step, half=None):
        at = ((self.p + step) % 4) * 256
        if half is None:
            return pl.ds(pl.multiple_of(at, 256), 256)
        return pl.ds(pl.multiple_of(at + half * 128, 128), 128)

    def start(self, src):
        rows = pl.ds(pl.multiple_of(self.here.c * 128, 128), 128)
        for half in range(2):
            part = src[rows, half * 512 : half * 512 + 512]
            self.buf[self.spot(0, half)] = part.astype(F32)
        mine = self.buf.at[self.spot(0)]
        self.near = [self.sems.copy(mine, mine, self.here.ring(self.axis, s)) for s in (1, 3)]
        return self

    def relay(self):
        self.far = []
        for cp, frm, to, half in ((self.near[0], 3, 1, 0), (self.near[1], 1, 3, 1)):
            cp.wait_recv()
            part = self.buf.at[self.spot(frm, half)]
            self.far.append(self.sems.copy(part, part, self.here.ring(self.axis, to)))

    def arrive(self):
        for cp in self.far:
            cp.wait_recv()

    def done(self):
        for cp in self.near + self.far:
            cp.wait_send()


class Moved:
    def __init__(self, here, axis, lane, ys, gy, sems):
        self.here, self.axis, self.ys, self.gy, self.sems = here, axis, ys, gy, sems
        self.lanes = pl.ds(lane, 256)

    def start(self, src):
        here, ys, gy, lanes = self.here, self.ys, self.gy, self.lanes
        c = here.c
        for q in range(4):
            ys[q * 256 : q * 256 + 256, lanes] = src[:, q * 256 : q * 256 + 256].astype(F32)
        self.k = self.sems.block(1)
        for step in (1, 3, 2, 0):
            for dc in range(2):
                axis = self.axis if dc == 0 else OTHER[self.axis]
                p, e = getattr(here, axis), (c + dc) % 2
                q = (p + step) % 4
                spot = pl.ds(pl.multiple_of(p * 256 + c * 128, 128), 128)
                rows = pl.ds(pl.multiple_of(q * 256 + e * 128, 128), 128)
                if step == 0 and dc == 0:
                    gy[spot, lanes] = ys[rows, lanes]
                    continue
                to = here.ring(axis, step, c=e)
                self.sems.copy(ys.at[rows, lanes], gy.at[spot, lanes], to, self.k)
        return self

    def sent(self):
        self.sems.all_sent(self.k, self.ys.at[pl.ds(0, 896), self.lanes])

    def arrive(self):
        self.sems.all_recv(self.k, self.gy.at[pl.ds(0, 896), self.lanes])


class ExpertGrads:
    def __init__(self, here, m, shared, moved, right, part, l1, l2, lx, land, sems, gates=None):
        self.here, self.m, self.shared, self.moved, self.right = here, m, shared, moved, right
        self.part, self.lx, self.land, self.sems, self.gates = part, lx, land, sems, gates
        self.axis = "ab"[m]
        self.ring = RingSum(here, OTHER[self.axis], part, 0, 256, l1, l2, sems)

    def multiply(self):
        self.shared.arrive()
        self.moved.arrive()
        gs, gy, lanes = self.shared.buf, self.moved.gy, self.moved.lanes
        for p in range(4):
            for k in range(2):
                rows = pl.ds(p * 256 + k * 128, 128)
                self.right[p * 128 : p * 128 + 128, k * 256 : k * 256 + 256] = gy[rows, lanes].astype(BF)
        gates = self.gates() if self.gates else None
        ring_on_y = (self.m + self.here.c) % 2
        per_y, per_z = 32 + 224 * ring_on_y, 256 - 224 * ring_on_y

        def block(k, carry):
            lanes = pl.ds(pl.multiple_of((k % 4) * 128, 128), 128)
            left = []
            for p in range(4):
                v = gs[pl.ds(pl.multiple_of(p * 256 + (k // 4) * 128, 128), 128), lanes]
                left.append((v if gates is None else gates[p] * v).astype(BF))
            res = tn(jnp.concatenate(left, axis=0), self.right[...])
            for z in range(4):
                at = (k // 4) * 128 + (k % 4) * per_y + z * per_z
                self.part[pl.ds(pl.multiple_of(at, 32), 32)] = res[z * 32 : z * 32 + 32]
            return carry

        lax.fori_loop(0, 8, block, 0)
        self.ring.start()

    def send_x(self, base, rows):
        here = self.here
        away = pl.ds(pl.multiple_of(base + (1 - here.x) * rows, rows), rows)
        self.swap = self.sems.copy(self.part.at[away], self.lx, here.dev(x=1 - here.x))

    def add_x(self, base, rows):
        self.swap.wait_recv()
        mine = pl.ds(pl.multiple_of(base + self.here.x * rows, rows), rows)
        self.part[mine] = self.part[mine] + self.lx[...]

    def across(self):
        self.ring.arrive()
        self.send_x(self.ring.p * 256, 128)

    def spread(self):
        here = self.here
        self.add_x(self.ring.p * 256, 128)
        base = self.ring.p * 256 + here.x * 128
        p, c = getattr(here, self.axis), here.c
        self.k = self.sems.block(1)
        for step in (1, 3, 2, 0):
            for dc in range(2):
                q, k = (p + step) % 4, (c + dc) % 2
                rows = pl.ds(pl.multiple_of(base + q * 32, 32), 32)
                lanes = pl.ds(pl.multiple_of(k * 256, 256), 256)
                if step == 0 and dc == 0:
                    self.land[p, c] = self.part[rows, lanes]
                    continue
                to = here.ring(self.axis, step, c=k)
                self.sems.copy(self.part.at[rows, lanes], self.land.at[p, c], to, self.k)

    def finish(self, out, j):
        seven = self.part.at[pl.ds(0, 224), pl.ds(0, 256)]
        self.sems.all_recv(self.k, seven)
        for e in range(2):
            for q in range(4):
                out[e, j, :, q * 256 : q * 256 + 256] = self.land[q, e]
        self.sems.all_sent(self.k, seven)
        self.swap.wait_send()
        self.ring.done()


INPUTS = (
    "tok", "seg", "routes", "slots", "ln_gain", "ln_shift", "qkv_w", "qv_bias", "out_w", "out_bias",
    "cent", "ffn_gain", "ffn_shift", "up_w", "up_bias", "down_w", "down_bias", "cot",
)
IN_HBM = ("up_w", "down_w", "qkv_w", "out_w")
OUTPUTS = {
    "result": ((256, 1024), BF),
    "tokens_grad": ((256, 1024), BF),
    "qkv_grad": ((3, 32, 256), F32),
    "out_grad": ((32, 256), F32),
    "up_grad": ((2, 2, 32, 1024), F32),
    "down_grad": ((2, 2, 32, 1024), F32),
    "sums": ((24, 1024), F32),
}
PART = ((1024, 512), F32)
SQUARE = ((256, 1024), F32)
LOW = ((256, 1024), BF)
SCRATCH = {
    "wqkv": ((3, 1024, 256), BF), "wout": ((256, 1024), BF),
    "wup": ((2, 1024, 1024), BF), "wdn": ((2, 1024, 1024), BF),
    "normed": LOW, "q": ((256, 256), BF), "k": ((256, 256), BF), "v": ((256, 256), BF),
    "mixed": ((256, 256), BF), "probs": ((4, 256, 256), F32),
    "gq": ((256, 256), BF), "gk": ((256, 256), BF), "gv": ((256, 256), BF),
    "hot_s": ((256, 256), BF), "hot_t": ((256, 256), BF),
    "valid": ((256, 1), F32), "filled": ((256, 1), F32), "route": ((256, 1), F32),
    "sig": ((256, 1), F32), "gating": ((256, 1), F32), "segc": ((256, 1), F32),
    "hidden": SQUARE, "rows0": SQUARE, "rows1": SQUARE, "rows2": SQUARE,
    "slope0": SQUARE, "gwork": SQUARE, "grows": SQUARE, "ghidden": SQUARE,
    "n": LOW, "act": LOW, "go": LOW, "gp": LOW,
    "pa": ((4, 256, 256), F32), "lca": ((4, 128, 256), F32), "lxa": ((2, 4, 128, 256), F32),
    "pb": ((4, 256, 256), F32), "lcb": ((4, 128, 256), F32), "lxb": ((4, 128, 256), F32),
    "gs0u": PART, "gs0w": PART, "gs1u": PART, "gs1w": PART,
    "ys": PART, "gy0": PART, "gy1": PART,
    "right": ((512, 512), BF),
    "partu": PART, "partw": PART,
    "l1": ((2, 2, 128, 512), F32), "l2": ((2, 2, 256, 512), F32),
    "lx": ((2, 2, 128, 512), F32), "gates": ((4, 8, 128), F32), "land": ((2, 2, 4, 2, 32, 256), F32),
    "a1": ((2, 2, 128, 512), F32), "a2": ((2, 2, 256, 512), F32),
    "b1": ((2, 2, 32, 512), F32), "b2": ((2, 2, 64, 512), F32), "ax": ((2, 32, 512), F32),
    "vb": ((11, 24, 1024), F32),
}
N_SEMS = 116


class Totals:
    def __init__(self, here, buf, sems):
        self.here, self.buf, self.sems, self.cps, self.wait = here, buf, sems, [], []

    def send(self, at, to, devices):
        spots = self.buf.at[at], self.buf.at[to]
        self.wait = [self.sems.copy(*spots, dev) for dev in devices]
        self.cps += self.wait

    def four(self, at):
        for cp in self.wait:
            cp.wait_recv()
        buf = self.buf
        return (buf[at] + buf[at + 1]) + (buf[at + 2] + buf[at + 3])

    def ring_y(self):
        at = 1 + self.here.y
        self.buf[at] = self.buf[0]
        self.send(at, at, [self.here.ring("y", step) for step in (1, 3, 2)])

    def ring_z(self):
        at = 5 + self.here.z
        self.buf[at] = self.four(1)
        self.send(at, at, [self.here.ring("z", step) for step in (1, 3, 2)])

    def pair(self):
        self.buf[9] = self.four(5)
        self.send(9, 10, [self.here.dev(x=1 - self.here.x)])

    def finish(self, out):
        self.wait[0].wait_recv()
        out[...] = self.buf[9] + self.buf[10]

    def done(self):
        for cp in self.cps:
            cp.wait_send()


class Bag:
    pass


def two(ref):
    return [ref.at[0], ref.at[1]]


def layer_kernel(*refs):
    B = Bag()
    for name, ref in zip([*INPUTS, *OUTPUTS, *SCRATCH, "ss", "rs", "ws", "free"], refs):
        setattr(B, name, ref)
    B.n0 = B.n1 = B.gbranch = B.n
    B.act0 = B.act1 = B.act
    B.go0 = B.go1 = B.go
    B.gp0 = B.gp1 = B.gp
    here = Here()
    sems = Sems(B.ss, B.rs)
    x, c = here.x, here.c
    vec = B.vb.at[0]
    even = [sems.block(4) for _ in range(3)]
    odd = [even[0], sems.block(4), even[2]]

    peers = [here.dev(c=1 - c), here.dev(h=1 - here.h), here.dev(x=1 - x)]
    for axis in ("y", "z"):
        for step in (1, 2, 3):
            for dc in range(2):
                peers.append(here.ring(axis, step, c=(c + dc) % 2))
    bar = pltpu.get_barrier_semaphore()
    for dev in peers:
        pl.semaphore_signal(bar, inc=1, device_id=dev, device_id_type=MESH)

    def fetch(pairs, at):
        cps = [pltpu.make_async_copy(s, t, B.ws.at[at + k]) for k, (s, t) in enumerate(pairs)]
        for cp in cps:
            cp.start()
        return cps

    def fetch_experts(j):
        return fetch(
            [(B.up_w.at[e, j], B.wup.at[e]) for e in range(2)]
            + [(B.down_w.at[e, j], B.wdn.at[e]) for e in range(2)],
            2,
        )

    heads = fetch([(B.qkv_w, B.wqkv), (B.out_w, B.wout)], 0)
    experts = fetch_experts(0)

    B.vb[0] = jnp.zeros((24, 1024), F32)
    lane1024 = lax.broadcasted_iota(jnp.int32, (1, 1024), 1)

    def stat(k, total):
        row = jnp.where(lane1024 == k, total, 0.0)
        vec[STATS : STATS + 1] = vec[STATS : STATS + 1] + row

    def total(v):
        return jnp.sum(jnp.sum(v, axis=1, keepdims=True), axis=0, keepdims=True)

    down_i = lax.broadcasted_iota(jnp.int32, (256, 256), 0)
    along_i = lax.broadcasted_iota(jnp.int32, (256, 256), 1)

    def column(row):
        return jnp.sum(jnp.where(down_i == along_i, row, 0.0), axis=1, keepdims=True)

    seg_row = B.seg[...].astype(F32)
    B.segc[...] = column(seg_row)
    B.valid[...] = (B.segc[...] != 0.0).astype(F32)

    def allowed():
        return (B.segc[...] == seg_row) & (along_i <= down_i) & (B.segc[...] != 0.0)

    head_of = along_i // HD

    gain = B.ln_gain[...].astype(F32).reshape(1, 1024)
    shift = B.ln_shift[...].astype(F32).reshape(1, 1024)

    def norm_block(i, carry):
        n, _ = unit(B.tok[rows32(i)].astype(F32))
        B.normed[rows32(i)] = (n * gain + shift).astype(BF)
        return carry

    lax.fori_loop(0, 8, norm_block, 0, unroll=2)
    for cp in heads:
        cp.wait()
    qv_bias = B.qv_bias[...].astype(F32)
    B.q[...] = (nn(B.normed[...], B.wqkv[0]) + qv_bias[0:1]).astype(BF)
    B.k[...] = nn(B.normed[...], B.wqkv[1]).astype(BF)
    B.v[...] = (nn(B.normed[...], B.wqkv[2]) + qv_bias[1:2]).astype(BF)

    def one_head(value, hh):
        return jnp.where(head_of == hh, value.astype(F32), 0.0)

    mixed = jnp.zeros((256, 256), F32)
    for hh in range(4):
        s = nt(one_head(B.q[...], hh).astype(BF), B.k[...]) * SCALE
        ok = allowed()
        s = jnp.where(ok, s, -1e30)
        e = jnp.where(ok, jnp.exp(s - jnp.max(s, axis=-1, keepdims=True)), 0.0)
        probs = e / (jnp.sum(e, axis=-1, keepdims=True) + (1.0 - B.valid[...]))
        B.probs[hh] = probs
        mixed = mixed + one_head(nn(probs.astype(BF), B.v[...]), hh)
    B.mixed[...] = mixed.astype(BF)

    pl.semaphore_wait(bar, len(peers))
    branch = TensorSum(here, sems, B.pa, B.lca, B.lxa.at[0], B.hidden, even)
    branch.send(lambda n: nn(B.mixed[...], B.wout[:, COLS[n]]))
    slot_row = jnp.concatenate([B.slots[0, 0:1], B.slots[0, 1:2]], axis=1)
    slot_col = column(slot_row.astype(F32))
    B.hot_s[...] = jnp.where(slot_col == along_i.astype(F32), 1.0, 0.0).astype(BF)
    for n in range(4):
        B.grows[:, COLS[n]] = nn(B.hot_s[...], B.cot[:, COLS[n]])
    s1w = Shared(here, "b", B.gs1w, sems).start(B.grows)
    B.route[...] = column(B.routes[...].astype(F32))
    B.filled[...] = (slot_col < 256.0).astype(F32)
    B.hot_t[...] = jnp.where(slot_row == down_i, 1.0, 0.0).astype(BF)
    stat(4, total(B.valid[...]))
    for n in range(2):
        branch.third(n)
    s1w.relay()
    branch.end()

    out_bias = B.out_bias[...].astype(F32).reshape(1, 1024)
    cent = B.cent[...].astype(F32)

    def hidden_block(i, carry):
        rows = rows32(i)
        h = B.tok[rows].astype(F32) + (B.hidden[rows] + out_bias)
        B.hidden[rows] = h
        scores = [jnp.sum(h * cent[e : e + 1], axis=-1, keepdims=True) for e in range(2)]
        logits = jnp.where(B.route[rows] == 1.0, scores[1], scores[0])
        sig = 1.0 / (1.0 + jnp.exp(-logits))
        B.sig[rows] = sig
        B.gating[rows] = sig * B.valid[rows]
        return carry + fold(h * h * B.valid[rows])

    stat(0, total(lax.fori_loop(0, 8, hidden_block, jnp.zeros((8, 1024), F32), unroll=2)))
    for n in range(4):
        B.rows0[:, COLS[n]] = pick(B.hot_s[...], B.hidden[:, COLS[n]])
    ffn_gain = B.ffn_gain[...].astype(F32)
    ffn_shift = B.ffn_shift[...].astype(F32)
    up_bias = B.up_bias[...].astype(F32)
    down_bias = B.down_bias[...].astype(F32)

    def expert_norm(rows_ref, low_ref, j):
        for e in range(2):
            g, s = ffn_gain[e, j : j + 1], ffn_shift[e, j : j + 1]

            def block(i, carry, e=e, g=g, s=s):
                rows = rows32(e * 4 + i)
                n, _ = unit(rows_ref[rows])
                low_ref[rows] = (n * g + s).astype(BF)
                return carry

            lax.fori_loop(0, 4, block, 0, unroll=2)

    def gelu_parts(v):
        t = jnp.tanh(ROOT * (v + 0.044715 * (v * v * v)))
        cdf = 0.5 * (1.0 + t)
        slope = cdf + (0.5 * ROOT) * v * (1.0 - t * t) * (1.0 + (3.0 * 0.044715) * (v * v))
        return v * cdf, slope

    def half(e):
        return pl.ds(e * 128, 128)

    expert_norm(B.rows0, B.n0, 0)
    s0u = Shared(here, "a", B.gs0u, sems).start(B.n0)
    for cp in experts:
        cp.wait()
    for e in range(2):
        for n in range(4):
            pre = nn(B.n0[half(e)], B.wup[e, :, COLS[n]]) + up_bias[e, 0:1, n * 256 : n * 256 + 256]
            act, slope = gelu_parts(pre)
            B.act0[half(e), COLS[n]] = act.astype(BF)
            B.slope0[half(e), COLS[n]] = slope

    def down(act_ref):
        def make(n):
            return jnp.concatenate(
                [nn(act_ref[half(e)], B.wdn[e, :, COLS[n]]) for e in range(2)], axis=0
            )

        return make

    first = TensorSum(here, sems, B.pa, B.lca, B.lxa.at[1], B.rows1, odd)
    first.send(down(B.act0))
    experts = fetch_experts(1)
    m0w = Moved(here, "b", 256, B.ys, B.gy0, sems).start(B.act0)
    gate_row = down_rows(B.hot_t[...].astype(F32) * B.gating[...])
    gate_col = column(gate_row)
    B.gates[here.b] = jnp.broadcast_to(jnp.where(c == 0, gate_row[:, :128], gate_row[:, 128:]), (8, 128))
    mine = B.gates.at[here.b]
    gate_cps = [sems.copy(mine, mine, here.ring("b", step)) for step in (1, 3, 2)]
    for n in range(4):
        g = gate_col * B.grows[:, COLS[n]]
        B.grows[:, COLS[n]] = g
        B.go1[:, COLS[n]] = g.astype(BF)
    for e in range(2):
        vec[DOWN_B + e * 2 + 1 : DOWN_B + e * 2 + 2] = down_rows(B.go1[half(e)].astype(F32))
    for cp in experts:
        cp.wait()
    for e in range(2):
        for n in range(4):
            B.gwork[half(e), COLS[n]] = nt(B.go1[half(e)], B.wdn[e, COLS[n], :])
    for n in range(3):
        first.third(n)
    s0u.relay()
    first.end()

    sq = jnp.zeros((8, 1024), F32)
    for e in range(2):
        bias = down_bias[e, 0:1]

        def rows1_block(i, carry, e=e, bias=bias):
            rows = rows32(e * 4 + i)
            r1 = B.rows0[rows] + (B.rows1[rows] + bias)
            B.rows1[rows] = r1
            return carry + fold(r1 * r1 * B.filled[rows])

        sq = lax.fori_loop(0, 4, rows1_block, sq, unroll=2)
    stat(1, total(sq))
    expert_norm(B.rows1, B.n1, 1)
    s1u = Shared(here, "a", B.gs1u, sems).start(B.n1)
    for e in range(2):
        for n in range(4):
            pre = nn(B.n1[half(e)], B.wup[e, :, COLS[n]]) + up_bias[e, 1:2, n * 256 : n * 256 + 256]
            act, slope = gelu_parts(pre)
            B.act1[half(e), COLS[n]] = act.astype(BF)
            gp = (B.gwork[half(e), COLS[n]] * slope).astype(BF)
            B.gp1[half(e), COLS[n]] = gp
            vec[UP_B + e * 2 + 1 : UP_B + e * 2 + 2, COLS[n]] = down_rows(gp.astype(F32))

    def normed_grad(gp_ref):
        def make(n):
            return jnp.concatenate(
                [nt(gp_ref[half(e)], B.wup[e, COLS[n], :]) for e in range(2)], axis=0
            )

        return make

    back1 = TensorSum(here, sems, B.pa, B.lca, B.lxa.at[0], B.gwork, even)
    back1.send(normed_grad(B.gp1))
    m1u = Moved(here, "a", 0, B.ys, B.gy1, sems).start(B.gp1)
    second = TensorSum(here, sems, B.pb, B.lcb, B.lxb, B.rows2, [sems.block(4) for _ in range(3)])
    second.send(down(B.act1))
    experts = fetch_experts(0)
    m0w.sent()
    m1w = Moved(here, "b", 256, B.ys, B.gy1, sems).start(B.act1)
    back1.end()

    def expert_norm_back(rows_ref, j, go_ref):
        for e in range(2):
            g = ffn_gain[e, j : j + 1]

            def block(i, carry, e=e, g=g):
                rows = rows32(e * 4 + i)
                n, r = unit(rows_ref[rows])
                gn = B.gwork[rows]
                new = B.grows[rows] + unit_back(gn, g, n, r)
                B.grows[rows] = new
                out = [carry[0] + fold(gn * n), carry[1] + fold(gn)]
                if go_ref is not None:
                    low = new.astype(BF)
                    go_ref[rows] = low
                    out.append(carry[2] + fold(low.astype(F32)))
                return tuple(out)

            zero = jnp.zeros((8, 1024), F32)
            sums = lax.fori_loop(0, 4, block, (zero,) * (2 if go_ref is None else 3), unroll=2)
            at = e * 2 + j
            vec[GAIN + at : GAIN + at + 1] = down_rows(sums[0])
            vec[SHIFT + at : SHIFT + at + 1] = down_rows(sums[1])
            if go_ref is not None:
                vec[DOWN_B + e * 2 : DOWN_B + e * 2 + 1] = down_rows(sums[2])

    expert_norm_back(B.rows1, 1, B.go0)
    s0w = Shared(here, "b", B.gs0w, sems).start(B.go0)
    for cp in experts:
        cp.wait()
    for e in range(2):
        for n in range(4):
            ga = nt(B.go0[half(e)], B.wdn[e, COLS[n], :])
            gp = (ga * B.slope0[half(e), COLS[n]]).astype(BF)
            B.gp0[half(e), COLS[n]] = gp
            vec[UP_B + e * 2 : UP_B + e * 2 + 1, COLS[n]] = down_rows(gp.astype(F32))
    back0 = TensorSum(here, sems, B.pa, B.lca, B.lxa.at[1], B.gwork, odd)
    back0.send(normed_grad(B.gp0))
    state = {}
    def slot_gates():
        for cp in gate_cps:
            cp.wait_recv()
        eye = down_i[:128, :128] == along_i[:128, :128]
        return [
            jnp.sum(jnp.where(eye, B.gates[p, 0:1], 0.0), axis=1, keepdims=True) for p in range(4)
        ]

    eg1 = [
        ExpertGrads(here, m, (s1u, s1w)[m], (m1u, m1w)[m], B.right, (B.partu, B.partw)[m],
                    two(B.l1.at[m]), two(B.l2.at[m]), B.lx.at[0, m], B.land.at[0, m], sems,
                    gates=(None, slot_gates)[m])
        for m in range(2)
    ]
    m0u = Moved(here, "a", 0, B.ys, B.gy0, sems)
    wide = [pl.ds(0, 512), pl.ds(512, 512)]
    eg0 = [
        ExpertGrads(here, m, (s0u, s0w)[m], (m0u, m0w)[m], B.right, (B.ys, B.gy1)[m],
                    [B.slope0.at[pl.ds(128 * k, 128), wide[m]] for k in range(2)],
                    [(B.hidden, B.rows2)[m].at[:, wide[k]] for k in range(2)],
                    B.lx.at[1, m], B.land.at[1, m], sems)
        for m in range(2)
    ]
    lefts = (B.normed, B.normed, B.normed, B.gbranch)
    rights = (B.gq, B.gk, B.gv, B.mixed)
    apart = (B.gs1u, B.gs1w)
    rings, rings2, swaps = {}, {}, {}
    gather = Totals(here, B.vb, sems)

    def move_gp0():
        m1u.sent()
        m0u.start(B.gp0)

    def result():
        sq = jnp.zeros((8, 1024), F32)
        for e in range(2):
            bias = down_bias[e, 1:2]

            def rows2_block(i, carry, e=e, bias=bias):
                rows = rows32(e * 4 + i)
                r2 = B.rows1[rows] + (B.rows2[rows] + bias)
                B.rows2[rows] = r2
                return carry + fold(r2 * r2 * B.filled[rows])

            sq = lax.fori_loop(0, 4, rows2_block, sq, unroll=2)
        stat(2, total(sq))
        gate_grad = jnp.zeros((256, 1), F32)
        result_sq = jnp.zeros((256, 1), F32)
        for n in range(4):
            comb = pick(B.hot_t[...], B.rows2[:, COLS[n]])
            res = B.hidden[:, COLS[n]] + B.gating[...] * comb
            B.result[:, COLS[n]] = res.astype(BF)
            result_sq = result_sq + jnp.sum(res * res, axis=-1, keepdims=True)
            gate_grad = gate_grad + jnp.sum(B.cot[:, COLS[n]].astype(F32) * comb, axis=-1, keepdims=True)
        stat(3, total(result_sq * B.valid[...]))
        B.gating[...] = gate_grad * B.sig[...] * (1.0 - B.sig[...]) * B.valid[...]

        def gate_block(i, carry):
            rows = rows32(i)
            gl, second_route = B.gating[rows], B.route[rows] == 1.0
            B.ghidden[rows] = B.cot[rows].astype(F32) + gl * jnp.where(second_route, cent[1:2], cent[0:1])
            v = gl * B.hidden[rows]
            return (
                carry[0] + fold(jnp.where(second_route, 0.0, v)),
                carry[1] + fold(jnp.where(second_route, v, 0.0)),
            )

        zero = jnp.zeros((8, 1024), F32)
        sums = lax.fori_loop(0, 8, gate_block, (zero, zero), unroll=2)
        for e in range(2):
            vec[CENT + e : CENT + e + 1] = down_rows(sums[e])
        for k, axis in enumerate(("b", "a")):
            for step in (1, 3):
                pl.semaphore_signal(
                    B.free.at[k], inc=1, device_id=here.ring(axis, step), device_id_type=MESH
                )

    def attention_back():
        expert_norm_back(B.rows0, 0, None)
        for n in range(4):
            g = B.ghidden[:, COLS[n]] + pick(B.hot_t[...], B.grows[:, COLS[n]])
            B.ghidden[:, COLS[n]] = g
            low = g.astype(BF)
            B.gbranch[:, COLS[n]] = low
            vec[OUT_BIAS : OUT_BIAS + 1, COLS[n]] = down_rows(low.astype(F32))
        gm = nt(B.gbranch[...], B.wout[...]).astype(BF)
        gq = jnp.zeros((256, 256), F32)
        gk = jnp.zeros((256, 256), F32)
        gv = jnp.zeros((256, 256), F32)
        for hh in range(4):
            probs = B.probs[hh]
            gp = nt(one_head(gm, hh).astype(BF), B.v[...])
            gv = gv + one_head(tn(probs.astype(BF), gm), hh)
            gs = (probs * (gp - jnp.sum(probs * gp, axis=-1, keepdims=True))).astype(BF)
            gq = gq + one_head(nn(gs, B.k[...]), hh)
            gk = gk + one_head(tn(gs, B.q[...]), hh)
        B.gq[...] = (gq * SCALE).astype(BF)
        B.gk[...] = (gk * SCALE).astype(BF)
        B.gv[...] = gv.astype(BF)
        vec[QV_B : QV_B + 1, 0:256] = down_rows(B.gq[...].astype(F32))
        vec[QV_B : QV_B + 1, 256:512] = down_rows(B.gv[...].astype(F32))
        state["back"] = back = TensorSum(here, sems, B.pa, B.lca, B.lxa.at[0], B.gwork, even)
        grads = (B.gq, B.gk, B.gv)
        back.send(lambda n: sum(nt(grads[s][...], B.wqkv[s, COLS[n], :]) for s in range(3)))


    def first_sublayer(m):
        if m == 0:
            m1w.sent()
            m0u.sent()
        pl.semaphore_wait(B.free.at[m], 2)
        eg0[m].multiply()

    def attention_grads(m):
        (s1u, s1w)[m].done()
        last_y = (m + c) % 2
        for j in range(2):

            def block(k, carry, m=m, last_y=last_y, left=lefts[2 * m + j], right=rights[2 * m + j], j=j):
                lanes = pl.ds(pl.multiple_of(k * 128, 128), 128)
                res = tn(left[:, lanes], right[...])
                for z in range(4):
                    at = (k // 4) * 32 + (k % 4) * (256 - 192 * last_y) + z * (64 + 192 * last_y)
                    apart[m][pl.ds(pl.multiple_of(at, 32), 32), j * 256 : j * 256 + 256] = res[
                        z * 32 : z * 32 + 32
                    ]
                return carry

            lax.fori_loop(0, 8, block, 0)
        rings[m] = RingSum(here, "ab"[m], apart[m], 0, 256, two(B.a1.at[m]), two(B.a2.at[m]), sems)
        rings[m].start()

    def tokens_back():
        state["back"].end()
        zero = jnp.zeros((8, 1024), F32)

        def last_block(i, carry):
            rows = rows32(i)
            n, r = unit(B.tok[rows].astype(F32))
            gn = B.gwork[rows]
            B.tokens_grad[rows] = (B.ghidden[rows] + unit_back(gn, gain, n, r)).astype(BF)
            return carry[0] + fold(gn * n), carry[1] + fold(gn)

        sums = lax.fori_loop(0, 8, last_block, (zero, zero), unroll=2)
        vec[LN_GAIN : LN_GAIN + 1] = down_rows(sums[0])
        vec[LN_SHIFT : LN_SHIFT + 1] = down_rows(sums[1])
        gather.ring_y()

    def second_ring(m):
        rings[m].arrive()
        base = rings[m].p * 256
        b1, b2 = two(B.b1.at[m]), two(B.b2.at[m])
        rings2[m] = RingSum(here, "ba"[m], apart[m], base, 64, b1, b2, sems)
        rings2[m].start()

    def attention_swap(m):
        rings2[m].arrive()
        base = rings2[m].base + rings2[m].p * 64
        away = pl.ds(pl.multiple_of(base + (1 - x) * 32, 32), 32)
        swaps[m] = sems.copy(apart[m].at[away], B.ax.at[m], here.dev(x=1 - x))

    def attention_out(m):
        swaps[m].wait_recv()
        base = rings2[m].base + rings2[m].p * 64
        mine = apart[m][pl.ds(pl.multiple_of(base + x * 32, 32), 32)] + B.ax[m]
        if m == 0:
            B.qkv_grad[0] = mine[:, :256]
            B.qkv_grad[1] = mine[:, 256:]
        else:
            B.qkv_grad[2] = mine[:, :256]
            B.out_grad[...] = mine[:, 256:]

    s1u.relay()
    move_gp0()
    eg1[0].multiply()
    back0.third(0)
    s0w.relay()
    eg1[1].multiply()
    second.end()
    result()
    first_sublayer(0)
    back0.third(1)
    first_sublayer(1)
    back0.third(2)
    back0.end()
    attention_back()
    eg1[0].ring.middle()
    eg0[0].ring.middle()
    eg1[1].ring.middle()
    eg1[0].across()
    state["back"].third(0)
    eg0[1].ring.middle()
    state["back"].third(1)
    attention_grads(1)
    eg0[1].across()
    state["back"].third(2)
    tokens_back()
    rings[1].middle()
    eg1[1].across()
    attention_grads(0)
    eg0[0].across()
    gather.ring_z()
    rings[0].middle()
    second_ring(1)
    eg0[1].spread()
    second_ring(0)
    rings2[1].middle()
    gather.pair()
    eg1[1].spread()
    rings2[0].middle()
    eg0[0].spread()
    eg1[0].spread()
    gather.finish(B.sums)
    attention_swap(1)
    attention_swap(0)
    eg0[0].finish((B.up_grad, B.down_grad)[0], 0)
    eg0[1].finish((B.up_grad, B.down_grad)[1], 0)
    attention_out(1)
    eg1[0].finish((B.up_grad, B.down_grad)[0], 1)
    eg1[1].finish((B.up_grad, B.down_grad)[1], 1)
    attention_out(0)
    assert sems.n == N_SEMS, sems.n
    for job in (s0u, s0w, gather, *rings.values(), *rings2.values()):
        job.done()
    for cp in [*swaps.values(), *gate_cps]:
        cp.wait_send()


def finish_kernel(*refs):
    big_in, sums, big_out = refs[:6], refs[6], refs[7:13]
    gain, shift, out_b, cent, ffn_g, ffn_s, down_b, up_b, qv_b, rms, sem = refs[13:]
    cps = [pltpu.make_async_copy(a, b, sem.at[k]) for k, (a, b) in enumerate(zip(big_in, big_out))]
    for cp in cps:
        cp.start()
    d = lax.axis_index("dp")
    near = sums[:, pl.ds(pl.multiple_of((d // 4) * 128, 128), 128)]
    share = near[:, :32]
    for k in range(1, 4):
        share = jnp.where(d % 4 == k, near[:, k * 32 : k * 32 + 32], share)
    for ref, at in ((gain, LN_GAIN), (shift, LN_SHIFT), (out_b, OUT_BIAS)):
        ref[...] = share[at : at + 1]
    cent[...] = share[CENT : CENT + 2]
    for ref, at in ((ffn_g, GAIN), (ffn_s, SHIFT), (down_b, DOWN_B)):
        for e in range(2):
            ref[e] = share[at + e * 2 : at + e * 2 + 2]
    for e in range(2):
        up_b[e] = sums[UP_B + e * 2 : UP_B + e * 2 + 2]
    qv_b[0:1] = sums[QV_B : QV_B + 1, 0:256]
    qv_b[1:2] = sums[QV_B : QV_B + 1, 256:512]
    totals = sums[STATS : STATS + 1, 0:128]
    rms[...] = jnp.sqrt(totals[:, :4] / (totals[:, 4:5] * 1024.0))
    for cp in cps:
        cp.wait()


SMALL = [(1, 32), (1, 32), (1, 32), (2, 32), (2, 2, 32), (2, 2, 32), (2, 2, 32), (2, 2, 1024), (2, 256), (1, 4)]


def local(
    tokens, segments, routes, slot_table, ln_gain, ln_shift, qkv_proj, qv_bias, out_proj, out_bias,
    centroids, ffn_gain, ffn_shift, up_proj, up_bias, down_proj, down_bias, cotangent,
):
    in_specs = [
        pl.BlockSpec(memory_space=pl.ANY if name in IN_HBM else VM) for name in INPUTS
    ]
    outs = pl.pallas_call(
        layer_kernel,
        out_shape=tuple(jax.ShapeDtypeStruct(*spec) for spec in OUTPUTS.values()),
        in_specs=in_specs,
        out_specs=[pl.BlockSpec(memory_space=VM)] * len(OUTPUTS),
        scratch_shapes=[VM(*spec) for spec in SCRATCH.values()]
        + [pltpu.SemaphoreType.DMA((N_SEMS,)), pltpu.SemaphoreType.DMA((N_SEMS,)), pltpu.SemaphoreType.DMA((6,)), pltpu.SemaphoreType.REGULAR((2,))],
        compiler_params=pltpu.CompilerParams(
            collective_id=0, has_side_effects=True, vmem_limit_bytes=VMEM_LIMIT
        ),
    )(
        tokens, segments.reshape(1, 256), routes.reshape(1, 256), slot_table,
        ln_gain, ln_shift, qkv_proj, qv_bias, out_proj,
        out_bias, centroids, ffn_gain, ffn_shift, up_proj, up_bias, down_proj,
        down_bias, cotangent,
    )
    anywhere = pl.BlockSpec(memory_space=pl.ANY)
    near = pl.BlockSpec(memory_space=VM)
    (
        result, tokens_grad, qkv_grad, out_grad, up_grad, down_grad,
        gain, shift, out_b, cent, ffn_g, ffn_s, down_b, up_b, qv_b, rms,
    ) = pl.pallas_call(
        finish_kernel,
        out_shape=tuple(jax.ShapeDtypeStruct(a.shape, a.dtype) for a in outs[:6])
        + tuple(jax.ShapeDtypeStruct(shape, F32) for shape in SMALL),
        in_specs=[near] * 7,
        out_specs=[anywhere] * 6 + [near] * len(SMALL),
        scratch_shapes=[pltpu.SemaphoreType.DMA((6,))],
    )(*outs)
    return (
        result,
        tokens_grad,
        gain.reshape(32),
        shift.reshape(32),
        qkv_grad,
        qv_b,
        out_grad.T,
        out_b.reshape(32),
        cent,
        ffn_g,
        ffn_s,
        up_grad,
        up_b,
        jnp.swapaxes(down_grad, 2, 3),
        down_b,
        rms.reshape(4),
    )


VMEM_LIMIT = 63 * 2**20


def solution(mesh):
    return jax.shard_map(
        local,
        mesh=mesh,
        in_specs=(
            P("dp", None),
            P("dp"),
            P("dp"),
            P("dp", None, None),
            P(),
            P(),
            P(None, None, "tensor"),
            P(None, "tensor"),
            P("tensor", None),
            P(),
            P(),
            P(),
            P(),
            P(None, None, None, "tensor"),
            P(None, None, "tensor"),
            P(None, None, "tensor", None),
            P(),
            P("dp", None),
        ),
        out_specs=(
            P("dp", None),
            P("dp", None),
            P("dp"),
            P("dp"),
            P(None, "dp", "tensor"),
            P(None, "tensor"),
            P("tensor", "dp"),
            P("dp"),
            P(None, "dp"),
            P(None, None, "dp"),
            P(None, None, "dp"),
            P(None, None, "dp", "tensor"),
            P(None, None, "tensor"),
            P(None, None, "tensor", "dp"),
            P(None, None, "dp"),
            P(),
        ),
        check_vma=False,
    )
```

```python
import math

import jax
import jax.numpy as jnp
from jax import lax
from jax.experimental import pallas as pl
from jax.experimental.pallas import tpu as pltpu
from jax.sharding import PartitionSpec as P

HD = 64
MESH = pl.DeviceIdType.MESH
OTHER = {"a": "b", "b": "a"}
VM = pltpu.VMEM
F32 = jnp.float32
BF = jnp.bfloat16
EPS = 1e-05
SCALE = HD ** (-0.5)
ROOT = math.sqrt(2.0 / math.pi)
COLS = [pl.ds(n * 256, 256) for n in range(4)]
LN_GAIN, LN_SHIFT, OUT_BIAS, CENT, GAIN, SHIFT, DOWN_B, UP_B, QV_B, STATS = (
    0, 1, 2, 3, 5, 9, 13, 17, 21, 22,
)


class Here:
    def __init__(self):
        d = lax.axis_index("dp")
        t = lax.axis_index("tensor")
        self.x, self.y, self.z = d // 16, (d // 4) % 4, d % 4
        self.h, self.c = t // 2, t % 2
        self.a = self.y * (1 - self.c) + self.z * self.c
        self.b = self.z * (1 - self.c) + self.y * self.c

    def dev(self, x=None, y=None, z=None, h=None, c=None):
        x = self.x if x is None else x
        y = self.y if y is None else y
        z = self.z if z is None else z
        h = self.h if h is None else h
        c = self.c if c is None else c
        return (x * 16 + y * 4 + z, h * 2 + c)

    def ring(self, axis, step, c=None):
        on_y = {"y": 1, "z": 0, "a": 1 - self.c, "b": self.c}[axis]
        y, z = (self.y + step * on_y) % 4, (self.z + step * (1 - on_y)) % 4
        return self.dev(y=y, z=z, c=c)


def here_not(flag):
    return not flag if isinstance(flag, bool) else jnp.logical_not(flag)


class Sems:
    def __init__(self, send, recv):
        self.send, self.recv, self.n = send, recv, 0

    def block(self, n):
        self.n += n
        return self.n - n

    def all_recv(self, k, view):
        pltpu.make_async_copy(view, view, self.recv.at[k]).wait()

    def all_sent(self, k, view):
        pltpu.make_async_copy(view, view, self.send.at[k]).wait()

    def copy(self, src, dst, dev, k=None):
        if k is None:
            k = self.block(1)
        cp = pltpu.make_async_remote_copy(
            src_ref=src,
            dst_ref=dst,
            send_sem=self.send.at[k],
            recv_sem=self.recv.at[k],
            device_id=dev,
            device_id_type=MESH,
        )
        cp.start()
        return cp


def nn(a, b):
    return jnp.dot(a, b, preferred_element_type=F32)


def nt(a, b):
    return lax.dot_general(a, b, (((1,), (1,)), ((), ())), preferred_element_type=F32)


def tn(a, b):
    return lax.dot_general(a, b, (((0,), (0,)), ((), ())), preferred_element_type=F32)


def pick(hot, v):
    a = v.astype(BF)
    rest = v - a.astype(F32)
    b = rest.astype(BF)
    c = (rest - b.astype(F32)).astype(BF)
    return nn(hot, a) + nn(hot, b) + nn(hot, c)


def unit(v):
    center = v - jnp.mean(v, axis=-1, keepdims=True)
    r = lax.rsqrt(jnp.mean(center * center, axis=-1, keepdims=True) + EPS)
    return center * r, r


def unit_back(grad, gain, n, r):
    u = grad * gain
    return r * (u - jnp.mean(u, axis=-1, keepdims=True) - n * jnp.mean(u * n, axis=-1, keepdims=True))


def fold(v):
    return jnp.sum(v.reshape(v.shape[0] // 8, 8, v.shape[1]), axis=0)


def down_rows(v):
    return jnp.sum(v, axis=0, keepdims=True)


def rows32(i):
    return pl.ds(pl.multiple_of(i * 32, 32), 32)


class TensorSum:
    def __init__(self, here, sems, p, lc, lx, out, at):
        self.sems, self.p, self.lc, self.lx, self.out, self.at = sems, p, lc, lx, out, at
        self.core = here.dev(c=1 - here.c)
        self.across = here.dev(h=1 - here.h)
        self.mine = pl.ds(pl.multiple_of(here.c * 128, 128), 128)
        self.other = pl.ds(pl.multiple_of((1 - here.c) * 128, 128), 128)
        self.a, self.b, self.d = [], [], []

    def first(self, n):
        cp = self.sems.copy(self.p.at[n, self.other], self.lc.at[n], self.core, self.at[0] + n)
        self.a.append(cp)

    def second(self, n):
        self.a[n].wait_recv()
        self.p[n, self.mine] = self.p[n, self.mine] + self.lc[n]
        cp = self.sems.copy(self.p.at[n, self.mine], self.lx.at[n], self.across, self.at[1] + n)
        self.b.append(cp)

    def third(self, n):
        self.b[n].wait_recv()
        self.out[self.mine, COLS[n]] = self.p[n, self.mine] + self.lx[n]
        spot = self.out.at[self.mine, COLS[n]]
        self.d.append(self.sems.copy(spot, spot, self.core, self.at[2] + n))

    def send(self, make):
        for n in range(4):
            self.p[n] = make(n)
            self.first(n)
            if n:
                self.second(n - 1)
        self.second(3)

    def end(self):
        for n in range(len(self.d), 4):
            self.third(n)
        for cp in self.d:
            cp.wait_recv()
        for cp in self.a + self.b + self.d:
            cp.wait_send()


class RingSum:
    def __init__(self, here, axis, buf, base, rows, l1, l2, sems):
        self.p = getattr(here, axis)
        self.buf, self.base, self.rows = buf, base, rows
        self.l1, self.l2, self.sems = l1, l2, sems
        self.plus, self.minus = here.ring(axis, 1), here.ring(axis, 3)
        self.cps = []

    def part(self, step, half):
        n = self.rows // 2
        at = self.base + ((self.p + step) % 4) * self.rows + half * n
        return pl.ds(pl.multiple_of(at, n), n)

    def own(self):
        at = self.base + self.p * self.rows
        return pl.ds(pl.multiple_of(at, self.rows), self.rows)

    def start(self):
        n, buf, sems = self.rows // 2, self.buf, self.sems
        lo, hi = pl.ds(0, n), pl.ds(n, n)
        self.a = sems.copy(buf.at[self.part(2, 0)], self.l1[0], self.plus)
        self.b = sems.copy(buf.at[self.part(2, 1)], self.l1[1], self.minus)
        self.cps.append(sems.copy(buf.at[self.part(1, 1)], self.l2[0].at[hi], self.plus))
        self.cps.append(sems.copy(buf.at[self.part(3, 0)], self.l2[1].at[lo], self.minus))
        return self

    def middle(self):
        n, buf, sems = self.rows // 2, self.buf, self.sems
        lo, hi = pl.ds(0, n), pl.ds(n, n)
        up, dn = self.part(1, 0), self.part(3, 1)
        self.a.wait_recv()
        buf[up] = buf[up] + self.l1[0][...]
        self.cps.append(sems.copy(buf.at[up], self.l2[0].at[lo], self.plus))
        self.b.wait_recv()
        buf[dn] = buf[dn] + self.l1[1][...]
        self.cps.append(sems.copy(buf.at[dn], self.l2[1].at[hi], self.minus))

    def arrive(self):
        for cp in self.cps:
            cp.wait_recv()
        own = self.own()
        self.buf[own] = self.buf[own] + self.l2[0][...] + self.l2[1][...]

    def done(self):
        for cp in [self.a, self.b] + self.cps:
            cp.wait_send()


class Shared:
    def __init__(self, here, axis, buf, sems):
        self.here, self.axis, self.buf, self.sems = here, axis, buf, sems
        self.p = getattr(here, axis)

    def spot(self, step, half=None):
        at = ((self.p + step) % 4) * 256
        if half is None:
            return pl.ds(pl.multiple_of(at, 256), 256)
        return pl.ds(pl.multiple_of(at + half * 128, 128), 128)

    def start(self, src):
        rows = pl.ds(pl.multiple_of(self.here.c * 128, 128), 128)
        for half in range(2):
            part = src[rows, half * 512 : half * 512 + 512]
            self.buf[self.spot(0, half)] = part.astype(F32)
        mine = self.buf.at[self.spot(0)]
        self.near = [self.sems.copy(mine, mine, self.here.ring(self.axis, s)) for s in (1, 3)]
        return self

    def relay(self):
        self.far = []
        for cp, frm, to, half in ((self.near[0], 3, 1, 0), (self.near[1], 1, 3, 1)):
            cp.wait_recv()
            part = self.buf.at[self.spot(frm, half)]
            self.far.append(self.sems.copy(part, part, self.here.ring(self.axis, to)))

    def arrive(self):
        for cp in self.far:
            cp.wait_recv()

    def done(self):
        for cp in self.near + self.far:
            cp.wait_send()


class Moved:
    def __init__(self, here, axis, lane, ys, gy, sems):
        self.here, self.axis, self.ys, self.gy, self.sems = here, axis, ys, gy, sems
        self.lanes = pl.ds(lane, 256)

    def start(self, src):
        here, ys, gy, lanes = self.here, self.ys, self.gy, self.lanes
        c = here.c
        for q in range(4):
            ys[q * 256 : q * 256 + 256, lanes] = src[:, q * 256 : q * 256 + 256].astype(F32)
        self.k = self.sems.block(1)
        for step in (1, 3, 2, 0):
            for dc in range(2):
                axis = self.axis if dc == 0 else OTHER[self.axis]
                p, e = getattr(here, axis), (c + dc) % 2
                q = (p + step) % 4
                spot = pl.ds(pl.multiple_of(p * 256 + c * 128, 128), 128)
                rows = pl.ds(pl.multiple_of(q * 256 + e * 128, 128), 128)
                if step == 0 and dc == 0:
                    gy[spot, lanes] = ys[rows, lanes]
                    continue
                to = here.ring(axis, step, c=e)
                self.sems.copy(ys.at[rows, lanes], gy.at[spot, lanes], to, self.k)
        return self

    def sent(self):
        self.sems.all_sent(self.k, self.ys.at[pl.ds(0, 896), self.lanes])

    def arrive(self):
        self.sems.all_recv(self.k, self.gy.at[pl.ds(0, 896), self.lanes])


class ExpertGrads:
    def __init__(self, here, m, shared, moved, right, part, l1, l2, lx, land, sems, gates=None):
        self.here, self.m, self.shared, self.moved, self.right = here, m, shared, moved, right
        self.part, self.lx, self.land, self.sems, self.gates = part, lx, land, sems, gates
        self.axis = "ab"[m]
        self.ring = RingSum(here, OTHER[self.axis], part, 0, 256, l1, l2, sems)

    def multiply(self):
        self.shared.arrive()
        self.moved.arrive()
        gs, gy, lanes = self.shared.buf, self.moved.gy, self.moved.lanes
        for p in range(4):
            for k in range(2):
                rows = pl.ds(p * 256 + k * 128, 128)
                self.right[p * 128 : p * 128 + 128, k * 256 : k * 256 + 256] = gy[rows, lanes].astype(BF)
        gates = self.gates() if self.gates else None
        ring_on_y = (self.m + self.here.c) % 2
        per_y, per_z = 32 + 224 * ring_on_y, 256 - 224 * ring_on_y

        def block(k, carry):
            lanes = pl.ds(pl.multiple_of((k % 4) * 128, 128), 128)
            left = []
            for p in range(4):
                v = gs[pl.ds(pl.multiple_of(p * 256 + (k // 4) * 128, 128), 128), lanes]
                left.append((v if gates is None else gates[p] * v).astype(BF))
            res = tn(jnp.concatenate(left, axis=0), self.right[...])
            for z in range(4):
                at = (k // 4) * 128 + (k % 4) * per_y + z * per_z
                self.part[pl.ds(pl.multiple_of(at, 32), 32)] = res[z * 32 : z * 32 + 32]
            return carry

        lax.fori_loop(0, 8, block, 0)
        self.ring.start()

    def send_x(self, base, rows):
        here = self.here
        away = pl.ds(pl.multiple_of(base + (1 - here.x) * rows, rows), rows)
        self.swap = self.sems.copy(self.part.at[away], self.lx, here.dev(x=1 - here.x))

    def add_x(self, base, rows):
        self.swap.wait_recv()
        mine = pl.ds(pl.multiple_of(base + self.here.x * rows, rows), rows)
        self.part[mine] = self.part[mine] + self.lx[...]

    def across(self):
        self.ring.arrive()
        self.send_x(self.ring.p * 256, 128)

    def spread(self):
        here = self.here
        self.add_x(self.ring.p * 256, 128)
        base = self.ring.p * 256 + here.x * 128
        p, c = getattr(here, self.axis), here.c
        self.k = self.sems.block(1)
        for step in (1, 3, 2, 0):
            for dc in range(2):
                q, k = (p + step) % 4, (c + dc) % 2
                rows = pl.ds(pl.multiple_of(base + q * 32, 32), 32)
                lanes = pl.ds(pl.multiple_of(k * 256, 256), 256)
                if step == 0 and dc == 0:
                    self.land[p, c] = self.part[rows, lanes]
                    continue
                to = here.ring(self.axis, step, c=k)
                self.sems.copy(self.part.at[rows, lanes], self.land.at[p, c], to, self.k)

    def finish(self, out, j):
        seven = self.part.at[pl.ds(0, 224), pl.ds(0, 256)]
        self.sems.all_recv(self.k, seven)
        for e in range(2):
            for q in range(4):
                out[e, j, :, q * 256 : q * 256 + 256] = self.land[q, e]
        self.sems.all_sent(self.k, seven)
        self.swap.wait_send()
        self.ring.done()


INPUTS = (
    "tok", "seg", "routes", "slots", "ln_gain", "ln_shift", "qkv_w", "qv_bias", "out_w", "out_bias",
    "cent", "ffn_gain", "ffn_shift", "up_w", "up_bias", "down_w", "down_bias", "cot",
)
OUT_HBM = ("result", "tokens_grad")
IN_HBM = ("up_w", "down_w", "qkv_w", "out_w")
OUTPUTS = {
    "result": ((256, 1024), BF),
    "tokens_grad": ((256, 1024), BF),
    "qkv_grad": ((3, 32, 256), F32),
    "out_grad": ((32, 256), F32),
    "up_grad": ((2, 2, 32, 1024), F32),
    "down_grad": ((2, 2, 32, 1024), F32),
    "sums": ((24, 1024), F32),
}
PART = ((1024, 512), F32)
SQUARE = ((256, 1024), F32)
LOW = ((256, 1024), BF)
SCRATCH = {
    "wqkv": ((3, 1024, 256), BF), "wout": ((256, 1024), BF),
    "wup": ((2, 1024, 1024), BF), "wdn": ((2, 1024, 1024), BF),
    "normed": LOW, "q": ((256, 256), BF), "k": ((256, 256), BF), "v": ((256, 256), BF),
    "mixed": ((256, 256), BF), "probs": ((4, 256, 256), F32),
    "gq": ((256, 256), BF), "gk": ((256, 256), BF), "gv": ((256, 256), BF),
    "hot_s": ((256, 256), BF), "hot_t": ((256, 256), BF),
    "valid": ((256, 1), F32), "filled": ((256, 1), F32), "route": ((256, 1), F32),
    "sig": ((256, 1), F32), "gating": ((256, 1), F32), "segc": ((256, 1), F32),
    "hidden": SQUARE, "rows0": SQUARE, "rows1": SQUARE, "rows2": SQUARE,
    "slope0": SQUARE, "gwork": SQUARE, "grows": SQUARE, "ghidden": SQUARE,
    "n": LOW, "act": LOW, "go": LOW, "gp": LOW,
    "pa": ((4, 256, 256), F32), "lca": ((4, 128, 256), F32), "lxa": ((2, 4, 128, 256), F32),
    "pb": ((4, 256, 256), F32), "lcb": ((4, 128, 256), F32), "lxb": ((4, 128, 256), F32),
    "gs0u": PART, "gs0w": PART, "gs1u": PART, "gs1w": PART,
    "ys": PART, "gy0": PART, "gy1": PART,
    "right": ((512, 512), BF),
    "partu": PART, "partw": PART,
    "l1": ((2, 2, 128, 512), F32), "l2": ((2, 2, 256, 512), F32),
    "lx": ((2, 2, 128, 512), F32), "gates": ((4, 8, 128), F32), "land": ((2, 2, 4, 2, 32, 256), F32),
    "a1": ((2, 2, 128, 384), F32), "a2": ((2, 2, 256, 384), F32),
    "b1": ((2, 32, 256), F32), "b2": ((2, 64, 256), F32), "ax": ((32, 256), F32),
    "gsn": PART, "gyn": ((512, 384), F32), "lxn": ((128, 384), F32), "landn": ((2, 2, 32, 384), F32),
    "vb": ((10, 24, 1024), F32), "low_out": LOW,
}
N_SEMS = 116


class QkvGrads:
    def __init__(self, here, shared, ys, gy, right, part, l1, l2, lx, land, sems):
        self.here, self.shared, self.ys, self.gy, self.right = here, shared, ys, gy, right
        self.part, self.lx, self.land, self.sems = part, lx, land, sems
        self.ring = RingSum(here, "b", part, 0, 256, l1, l2, sems)
        self.stays = here.a // 2 == here.c

    def move(self, grads):
        here, ys, gy, c = self.here, self.ys, self.gy, self.here.c
        for n, g in enumerate(grads):
            ys[:, COLS[n]] = g[...].astype(F32)
        self.k = self.sems.block(1)
        for dc in range(2):
            axis, e = "ab"[dc], (c + dc) % 2
            p = getattr(here, axis)
            spot = gy.at[pl.ds(pl.multiple_of(p * 128, 128), 128)]
            for q in range(2):
                to = 2 * c + q
                block = ys.at[
                    pl.ds(pl.multiple_of(e * 128, 128), 128), q * 384 : q * 384 + 384
                ]

                def send(block=block, spot=spot, to=to, axis=axis, e=e, p=p):
                    self.sems.copy(block, spot, here.ring(axis, to - p + 4, c=e), self.k)

                if dc:
                    send()
                    continue

                def keep(block=block, spot=spot):
                    spot[...] = block[...]

                pl.when(to == p)(keep)
                pl.when(to != p)(send)

    def settle(self, wait, rows):
        view = self.gy
        pl.when(self.stays)(lambda: wait(view.at[pl.ds(0, 3 * rows)]))
        pl.when(here_not(self.stays))(lambda: wait(view.at[pl.ds(0, 4 * rows)]))

    def multiply(self):
        self.shared.arrive()
        self.settle(lambda view: self.sems.all_recv(self.k, view), 128)
        self.right[:, 0:384] = self.gy[...].astype(BF)
        c = self.here.c
        per_y, per_z = 32 + 224 * c, 256 - 224 * c

        def block(k, carry):
            lanes = pl.ds(pl.multiple_of((k % 4) * 128, 128), 128)
            left = [
                self.shared.buf[
                    pl.ds(pl.multiple_of(p * 256 + (k // 4) * 128, 128), 128), lanes
                ].astype(BF)
                for p in range(4)
            ]
            res = tn(jnp.concatenate(left, axis=0), self.right[:, 0:384])
            for z in range(4):
                at = (k // 4) * 128 + (k % 4) * per_y + z * per_z
                self.part[pl.ds(pl.multiple_of(at, 32), 32)] = res[z * 32 : z * 32 + 32]
            return carry

        lax.fori_loop(0, 8, block, 0)
        self.ring.start()

    def across(self):
        here = self.here
        self.ring.arrive()
        away = pl.multiple_of(self.ring.p * 256 + (1 - here.x) * 128, 128)
        self.swap = self.sems.copy(self.part.at[pl.ds(away, 128)], self.lx, here.dev(x=1 - here.x))

    def spread(self):
        here = self.here
        self.swap.wait_recv()
        base = self.ring.p * 256 + here.x * 128
        mine = pl.ds(pl.multiple_of(base, 128), 128)
        self.part[mine] = self.part[mine] + self.lx[...]
        self.k2 = self.sems.block(1)
        p, owner = here.a, here.a // 2
        spot = self.land.at[p % 2, here.c]
        for step in (1, 3, 2, 0):
            block = self.part.at[pl.ds(pl.multiple_of(base + ((p + step) % 4) * 32, 32), 32)]

            def send(block=block, step=step):
                self.sems.copy(block, spot, here.ring("a", step, c=owner), self.k2)

            if step:
                send()
                continue

            def keep(block=block):
                spot[...] = block[...]

            pl.when(self.stays)(keep)
            pl.when(here_not(self.stays))(send)

    def finish(self, out):
        self.settle(lambda view: self.sems.all_recv(self.k2, view), 32)
        left, right = (self.land[half, 0] + self.land[half, 1] for half in range(2))
        out[0] = left[:, 0:256]
        out[1, :, 0:128] = left[:, 256:384]
        out[1, :, 128:256] = right[:, 0:128]
        out[2] = right[:, 128:384]

    def done(self):
        self.settle(lambda view: self.sems.all_sent(self.k, view), 128)
        self.settle(lambda view: self.sems.all_sent(self.k2, view), 32)
        self.swap.wait_send()
        self.ring.done()


class Totals:
    def __init__(self, here, buf, sems):
        self.here, self.buf, self.sems, self.cps, self.wait = here, buf, sems, [], []

    def send(self, at, to, devices):
        spots = self.buf.at[at], self.buf.at[to]
        self.wait = [self.sems.copy(*spots, dev) for dev in devices]
        self.cps += self.wait

    def four(self, at):
        for cp in self.wait:
            cp.wait_recv()
        buf = self.buf
        return (buf[at] + buf[at + 1]) + (buf[at + 2] + buf[at + 3])

    def ring_y(self):
        at = 1 + self.here.y
        self.buf[at] = self.buf[0]
        self.send(at, at, [self.here.ring("y", step) for step in (1, 3, 2)])

    def ring_z(self):
        at = 5 + self.here.z
        self.buf[at] = self.four(1)
        self.send(at, at, [self.here.ring("z", step) for step in (1, 3, 2)])

    def pair(self):
        self.buf[0] = self.four(5)
        self.send(0, 9, [self.here.dev(x=1 - self.here.x)])

    def finish(self, out):
        self.wait[0].wait_recv()
        out[...] = self.buf[0] + self.buf[9]

    def done(self):
        for cp in self.cps:
            cp.wait_send()


class Bag:
    pass


def two(ref):
    return [ref.at[0], ref.at[1]]


def layer_kernel(*refs):
    B = Bag()
    for name, ref in zip([*INPUTS, *OUTPUTS, *SCRATCH, "ss", "rs", "ws", "free"], refs):
        setattr(B, name, ref)
    B.n0 = B.n1 = B.gbranch = B.n
    B.act0 = B.act1 = B.act
    B.go0 = B.go1 = B.go
    B.gp0 = B.gp1 = B.gp
    here = Here()
    sems = Sems(B.ss, B.rs)
    x, c = here.x, here.c
    vec = B.vb.at[0]
    even = [sems.block(4) for _ in range(3)]
    odd = [even[0], sems.block(4), even[2]]

    peers = [here.dev(c=1 - c), here.dev(h=1 - here.h), here.dev(x=1 - x)]
    for axis in ("y", "z"):
        for step in (1, 2, 3):
            for dc in range(2):
                peers.append(here.ring(axis, step, c=(c + dc) % 2))
    bar = pltpu.get_barrier_semaphore()
    for dev in peers:
        pl.semaphore_signal(bar, inc=1, device_id=dev, device_id_type=MESH)

    def fetch(pairs, at):
        cps = [pltpu.make_async_copy(s, t, B.ws.at[at + k]) for k, (s, t) in enumerate(pairs)]
        for cp in cps:
            cp.start()
        return cps

    def fetch_experts(j):
        return fetch(
            [(B.up_w.at[e, j], B.wup.at[e]) for e in range(2)]
            + [(B.down_w.at[e, j], B.wdn.at[e]) for e in range(2)],
            2,
        )

    heads = fetch([(B.qkv_w, B.wqkv), (B.out_w, B.wout)], 0)
    experts = fetch_experts(0)

    B.vb[0] = jnp.zeros((24, 1024), F32)
    lane1024 = lax.broadcasted_iota(jnp.int32, (1, 1024), 1)

    def stat(k, total):
        row = jnp.where(lane1024 == k, total, 0.0)
        vec[STATS : STATS + 1] = vec[STATS : STATS + 1] + row

    def total(v):
        return jnp.sum(jnp.sum(v, axis=1, keepdims=True), axis=0, keepdims=True)

    down_i = lax.broadcasted_iota(jnp.int32, (256, 256), 0)
    along_i = lax.broadcasted_iota(jnp.int32, (256, 256), 1)

    def column(row):
        return jnp.sum(jnp.where(down_i == along_i, row, 0.0), axis=1, keepdims=True)

    seg_row = B.seg[...].astype(F32)
    B.segc[...] = column(seg_row)
    B.valid[...] = (B.segc[...] != 0.0).astype(F32)

    def allowed():
        return (B.segc[...] == seg_row) & (along_i <= down_i) & (B.segc[...] != 0.0)

    head_of = along_i // HD

    gain = B.ln_gain[...].astype(F32).reshape(1, 1024)
    shift = B.ln_shift[...].astype(F32).reshape(1, 1024)

    def norm_block(i, carry):
        n, _ = unit(B.tok[rows32(i)].astype(F32))
        B.normed[rows32(i)] = (n * gain + shift).astype(BF)
        return carry

    lax.fori_loop(0, 8, norm_block, 0, unroll=2)
    for cp in heads:
        cp.wait()
    qv_bias = B.qv_bias[...].astype(F32)
    B.q[...] = (nn(B.normed[...], B.wqkv[0]) + qv_bias[0:1]).astype(BF)
    B.k[...] = nn(B.normed[...], B.wqkv[1]).astype(BF)
    B.v[...] = (nn(B.normed[...], B.wqkv[2]) + qv_bias[1:2]).astype(BF)

    def one_head(value, hh):
        return jnp.where(head_of == hh, value.astype(F32), 0.0)

    mixed = jnp.zeros((256, 256), F32)
    for hh in range(4):
        s = nt(one_head(B.q[...], hh).astype(BF), B.k[...]) * SCALE
        ok = allowed()
        s = jnp.where(ok, s, -1e30)
        e = jnp.where(ok, jnp.exp(s - jnp.max(s, axis=-1, keepdims=True)), 0.0)
        probs = e / (jnp.sum(e, axis=-1, keepdims=True) + (1.0 - B.valid[...]))
        B.probs[hh] = probs
        mixed = mixed + one_head(nn(probs.astype(BF), B.v[...]), hh)
    B.mixed[...] = mixed.astype(BF)

    pl.semaphore_wait(bar, len(peers))
    sn = Shared(here, "a", B.gsn, sems).start(B.normed)
    branch = TensorSum(here, sems, B.pa, B.lca, B.lxa.at[0], B.hidden, even)
    branch.send(lambda n: nn(B.mixed[...], B.wout[:, COLS[n]]))
    slot_row = jnp.concatenate([B.slots[0, 0:1], B.slots[0, 1:2]], axis=1)
    slot_col = column(slot_row.astype(F32))
    B.hot_s[...] = jnp.where(slot_col == along_i.astype(F32), 1.0, 0.0).astype(BF)
    for n in range(4):
        B.grows[:, COLS[n]] = nn(B.hot_s[...], B.cot[:, COLS[n]])
    s1w = Shared(here, "b", B.gs1w, sems).start(B.grows)
    B.route[...] = column(B.routes[...].astype(F32))
    B.filled[...] = (slot_col < 256.0).astype(F32)
    B.hot_t[...] = jnp.where(slot_row == down_i, 1.0, 0.0).astype(BF)
    stat(4, total(B.valid[...]))
    for n in range(2):
        branch.third(n)
    sn.relay()
    branch.third(2)
    s1w.relay()
    branch.end()

    out_bias = B.out_bias[...].astype(F32).reshape(1, 1024)
    cent = B.cent[...].astype(F32)

    def hidden_block(i, carry):
        rows = rows32(i)
        h = B.tok[rows].astype(F32) + (B.hidden[rows] + out_bias)
        B.hidden[rows] = h
        scores = [jnp.sum(h * cent[e : e + 1], axis=-1, keepdims=True) for e in range(2)]
        logits = jnp.where(B.route[rows] == 1.0, scores[1], scores[0])
        sig = 1.0 / (1.0 + jnp.exp(-logits))
        B.sig[rows] = sig
        B.gating[rows] = sig * B.valid[rows]
        return carry + fold(h * h * B.valid[rows])

    stat(0, total(lax.fori_loop(0, 8, hidden_block, jnp.zeros((8, 1024), F32), unroll=2)))
    for n in range(4):
        B.rows0[:, COLS[n]] = pick(B.hot_s[...], B.hidden[:, COLS[n]])
    ffn_gain = B.ffn_gain[...].astype(F32)
    ffn_shift = B.ffn_shift[...].astype(F32)
    up_bias = B.up_bias[...].astype(F32)
    down_bias = B.down_bias[...].astype(F32)

    def expert_norm(rows_ref, low_ref, j):
        for e in range(2):
            g, s = ffn_gain[e, j : j + 1], ffn_shift[e, j : j + 1]

            def block(i, carry, e=e, g=g, s=s):
                rows = rows32(e * 4 + i)
                n, _ = unit(rows_ref[rows])
                low_ref[rows] = (n * g + s).astype(BF)
                return carry

            lax.fori_loop(0, 4, block, 0, unroll=2)

    def gelu_parts(v):
        t = jnp.tanh(ROOT * (v + 0.044715 * (v * v * v)))
        cdf = 0.5 * (1.0 + t)
        slope = cdf + (0.5 * ROOT) * v * (1.0 - t * t) * (1.0 + (3.0 * 0.044715) * (v * v))
        return v * cdf, slope

    def half(e):
        return pl.ds(e * 128, 128)

    expert_norm(B.rows0, B.n0, 0)
    s0u = Shared(here, "a", B.gs0u, sems).start(B.n0)
    for cp in experts:
        cp.wait()
    for e in range(2):
        for n in range(4):
            pre = nn(B.n0[half(e)], B.wup[e, :, COLS[n]]) + up_bias[e, 0:1, n * 256 : n * 256 + 256]
            act, slope = gelu_parts(pre)
            B.act0[half(e), COLS[n]] = act.astype(BF)
            B.slope0[half(e), COLS[n]] = slope

    def down(act_ref):
        def make(n):
            return jnp.concatenate(
                [nn(act_ref[half(e)], B.wdn[e, :, COLS[n]]) for e in range(2)], axis=0
            )

        return make

    first = TensorSum(here, sems, B.pa, B.lca, B.lxa.at[1], B.rows1, odd)
    first.send(down(B.act0))
    experts = fetch_experts(1)
    m0w = Moved(here, "b", 256, B.ys, B.gy0, sems).start(B.act0)
    gate_row = down_rows(B.hot_t[...].astype(F32) * B.gating[...])
    gate_col = column(gate_row)
    B.gates[here.b] = jnp.broadcast_to(jnp.where(c == 0, gate_row[:, :128], gate_row[:, 128:]), (8, 128))
    mine = B.gates.at[here.b]
    gate_cps = [sems.copy(mine, mine, here.ring("b", step)) for step in (1, 3, 2)]
    for n in range(4):
        g = gate_col * B.grows[:, COLS[n]]
        B.grows[:, COLS[n]] = g
        B.go1[:, COLS[n]] = g.astype(BF)
    for e in range(2):
        vec[DOWN_B + e * 2 + 1 : DOWN_B + e * 2 + 2] = down_rows(B.go1[half(e)].astype(F32))
    for cp in experts:
        cp.wait()
    for e in range(2):
        for n in range(4):
            B.gwork[half(e), COLS[n]] = nt(B.go1[half(e)], B.wdn[e, COLS[n], :])
    for n in range(3):
        first.third(n)
    s0u.relay()
    first.end()

    sq = jnp.zeros((8, 1024), F32)
    for e in range(2):
        bias = down_bias[e, 0:1]

        def rows1_block(i, carry, e=e, bias=bias):
            rows = rows32(e * 4 + i)
            r1 = B.rows0[rows] + (B.rows1[rows] + bias)
            B.rows1[rows] = r1
            return carry + fold(r1 * r1 * B.filled[rows])

        sq = lax.fori_loop(0, 4, rows1_block, sq, unroll=2)
    stat(1, total(sq))
    expert_norm(B.rows1, B.n1, 1)
    s1u = Shared(here, "a", B.gs1u, sems).start(B.n1)
    for e in range(2):
        for n in range(4):
            pre = nn(B.n1[half(e)], B.wup[e, :, COLS[n]]) + up_bias[e, 1:2, n * 256 : n * 256 + 256]
            act, slope = gelu_parts(pre)
            B.act1[half(e), COLS[n]] = act.astype(BF)
            gp = (B.gwork[half(e), COLS[n]] * slope).astype(BF)
            B.gp1[half(e), COLS[n]] = gp
            vec[UP_B + e * 2 + 1 : UP_B + e * 2 + 2, COLS[n]] = down_rows(gp.astype(F32))

    def normed_grad(gp_ref):
        def make(n):
            return jnp.concatenate(
                [nt(gp_ref[half(e)], B.wup[e, COLS[n], :]) for e in range(2)], axis=0
            )

        return make

    back1 = TensorSum(here, sems, B.pa, B.lca, B.lxa.at[0], B.gwork, even)
    back1.send(normed_grad(B.gp1))
    m1u = Moved(here, "a", 0, B.ys, B.gy1, sems).start(B.gp1)
    second = TensorSum(here, sems, B.pb, B.lcb, B.lxb, B.rows2, [sems.block(4) for _ in range(3)])
    second.send(down(B.act1))
    experts = fetch_experts(0)
    m0w.sent()
    m1w = Moved(here, "b", 256, B.ys, B.gy1, sems).start(B.act1)
    back1.end()

    def expert_norm_back(rows_ref, j, go_ref):
        for e in range(2):
            g = ffn_gain[e, j : j + 1]

            def block(i, carry, e=e, g=g):
                rows = rows32(e * 4 + i)
                n, r = unit(rows_ref[rows])
                gn = B.gwork[rows]
                new = B.grows[rows] + unit_back(gn, g, n, r)
                B.grows[rows] = new
                out = [carry[0] + fold(gn * n), carry[1] + fold(gn)]
                if go_ref is not None:
                    low = new.astype(BF)
                    go_ref[rows] = low
                    out.append(carry[2] + fold(low.astype(F32)))
                return tuple(out)

            zero = jnp.zeros((8, 1024), F32)
            sums = lax.fori_loop(0, 4, block, (zero,) * (2 if go_ref is None else 3), unroll=2)
            at = e * 2 + j
            vec[GAIN + at : GAIN + at + 1] = down_rows(sums[0])
            vec[SHIFT + at : SHIFT + at + 1] = down_rows(sums[1])
            if go_ref is not None:
                vec[DOWN_B + e * 2 : DOWN_B + e * 2 + 1] = down_rows(sums[2])

    expert_norm_back(B.rows1, 1, B.go0)
    s0w = Shared(here, "b", B.gs0w, sems).start(B.go0)
    for cp in experts:
        cp.wait()
    for e in range(2):
        for n in range(4):
            ga = nt(B.go0[half(e)], B.wdn[e, COLS[n], :])
            gp = (ga * B.slope0[half(e), COLS[n]]).astype(BF)
            B.gp0[half(e), COLS[n]] = gp
            vec[UP_B + e * 2 : UP_B + e * 2 + 1, COLS[n]] = down_rows(gp.astype(F32))
    back0 = TensorSum(here, sems, B.pa, B.lca, B.lxa.at[1], B.gwork, odd)
    back0.send(normed_grad(B.gp0))
    state = {}
    def slot_gates():
        for cp in gate_cps:
            cp.wait_recv()
        eye = down_i[:128, :128] == along_i[:128, :128]
        return [
            jnp.sum(jnp.where(eye, B.gates[p, 0:1], 0.0), axis=1, keepdims=True) for p in range(4)
        ]

    eg1 = [
        ExpertGrads(here, m, (s1u, s1w)[m], (m1u, m1w)[m], B.right, (B.partu, B.partw)[m],
                    two(B.l1.at[m]), two(B.l2.at[m]), B.lx.at[0, m], B.land.at[0, m], sems,
                    gates=(None, slot_gates)[m])
        for m in range(2)
    ]
    m0u = Moved(here, "a", 0, B.ys, B.gy0, sems)
    wide = [pl.ds(0, 512), pl.ds(512, 512)]
    eg0 = [
        ExpertGrads(here, m, (s0u, s0w)[m], (m0u, m0w)[m], B.right, (B.ys, B.gy1)[m],
                    [B.slope0.at[pl.ds(128 * k, 128), wide[m]] for k in range(2)],
                    [(B.hidden, B.rows2)[m].at[:, wide[k]] for k in range(2)],
                    B.lx.at[1, m], B.land.at[1, m], sems)
        for m in range(2)
    ]
    low, few = pl.ds(0, 256), pl.ds(0, 384)
    apart = (None, B.gs1w.at[:, low])
    qkv = QkvGrads(
        here, sn, B.rows0, B.gyn, B.right, B.gs1u.at[:, few],
        two(B.a1.at[0]), two(B.a2.at[0]), B.lxn, B.landn, sems,
    )
    rings, rings2, swaps = {}, {}, {}
    gather = Totals(here, B.vb, sems)

    def move_gp0():
        m1u.sent()
        m0u.start(B.gp0)

    def result():
        sq = jnp.zeros((8, 1024), F32)
        for e in range(2):
            bias = down_bias[e, 1:2]

            def rows2_block(i, carry, e=e, bias=bias):
                rows = rows32(e * 4 + i)
                r2 = B.rows1[rows] + (B.rows2[rows] + bias)
                B.rows2[rows] = r2
                return carry + fold(r2 * r2 * B.filled[rows])

            sq = lax.fori_loop(0, 4, rows2_block, sq, unroll=2)
        stat(2, total(sq))
        gate_grad = jnp.zeros((256, 1), F32)
        result_sq = jnp.zeros((256, 1), F32)
        for n in range(4):
            comb = pick(B.hot_t[...], B.rows2[:, COLS[n]])
            res = B.hidden[:, COLS[n]] + B.gating[...] * comb
            B.low_out[:, COLS[n]] = res.astype(BF)
            result_sq = result_sq + jnp.sum(res * res, axis=-1, keepdims=True)
            gate_grad = gate_grad + jnp.sum(B.cot[:, COLS[n]].astype(F32) * comb, axis=-1, keepdims=True)
        state["out"] = pltpu.make_async_copy(B.low_out, B.result, B.ws.at[0])
        state["out"].start()
        stat(3, total(result_sq * B.valid[...]))
        B.gating[...] = gate_grad * B.sig[...] * (1.0 - B.sig[...]) * B.valid[...]

        def gate_block(i, carry):
            rows = rows32(i)
            gl, second_route = B.gating[rows], B.route[rows] == 1.0
            B.ghidden[rows] = B.cot[rows].astype(F32) + gl * jnp.where(second_route, cent[1:2], cent[0:1])
            v = gl * B.hidden[rows]
            return (
                carry[0] + fold(jnp.where(second_route, 0.0, v)),
                carry[1] + fold(jnp.where(second_route, v, 0.0)),
            )

        zero = jnp.zeros((8, 1024), F32)
        sums = lax.fori_loop(0, 8, gate_block, (zero, zero), unroll=2)
        for e in range(2):
            vec[CENT + e : CENT + e + 1] = down_rows(sums[e])
        for k, axis in enumerate(("b", "a")):
            for step in (1, 3):
                pl.semaphore_signal(
                    B.free.at[k], inc=1, device_id=here.ring(axis, step), device_id_type=MESH
                )

    def attention_back():
        expert_norm_back(B.rows0, 0, None)
        for n in range(4):
            g = B.ghidden[:, COLS[n]] + pick(B.hot_t[...], B.grows[:, COLS[n]])
            B.ghidden[:, COLS[n]] = g
            low = g.astype(BF)
            B.gbranch[:, COLS[n]] = low
            vec[OUT_BIAS : OUT_BIAS + 1, COLS[n]] = down_rows(low.astype(F32))
        gm = nt(B.gbranch[...], B.wout[...]).astype(BF)
        gq = jnp.zeros((256, 256), F32)
        gk = jnp.zeros((256, 256), F32)
        gv = jnp.zeros((256, 256), F32)
        for hh in range(4):
            probs = B.probs[hh]
            gp = nt(one_head(gm, hh).astype(BF), B.v[...])
            gv = gv + one_head(tn(probs.astype(BF), gm), hh)
            gs = (probs * (gp - jnp.sum(probs * gp, axis=-1, keepdims=True))).astype(BF)
            gq = gq + one_head(nn(gs, B.k[...]), hh)
            gk = gk + one_head(tn(gs, B.q[...]), hh)
        B.gq[...] = (gq * SCALE).astype(BF)
        B.gk[...] = (gk * SCALE).astype(BF)
        B.gv[...] = gv.astype(BF)
        vec[QV_B : QV_B + 1, 0:256] = down_rows(B.gq[...].astype(F32))
        vec[QV_B : QV_B + 1, 256:512] = down_rows(B.gv[...].astype(F32))
        state["back"] = back = TensorSum(here, sems, B.pa, B.lca, B.lxa.at[0], B.gwork, even)
        grads = (B.gq, B.gk, B.gv)
        back.send(lambda n: sum(nt(grads[s][...], B.wqkv[s, COLS[n], :]) for s in range(3)))


    def first_sublayer(m):
        if m == 0:
            m1w.sent()
            m0u.sent()
        pl.semaphore_wait(B.free.at[m], 2)
        eg0[m].multiply()

    def qkv_multiply():
        s1u.done()
        qkv.multiply()

    def attention_grads(m):
        s1w.done()
        last_y = (m + c) % 2

        def block(k, carry):
            lanes = pl.ds(pl.multiple_of(k * 128, 128), 128)
            res = tn(B.gbranch[:, lanes], B.mixed[...])
            for z in range(4):
                at = (k // 4) * 32 + (k % 4) * (256 - 192 * last_y) + z * (64 + 192 * last_y)
                apart[m][pl.ds(pl.multiple_of(at, 32), 32)] = res[z * 32 : z * 32 + 32]
            return carry

        lax.fori_loop(0, 8, block, 0)
        l1 = [B.a1.at[m, k, :, low] for k in range(2)]
        l2 = [B.a2.at[m, k, :, low] for k in range(2)]
        rings[m] = RingSum(here, "ab"[m], apart[m], 0, 256, l1, l2, sems)
        rings[m].start()

    def tokens_back():
        state["back"].end()
        state["out"].wait()
        zero = jnp.zeros((8, 1024), F32)

        def last_block(i, carry):
            rows = rows32(i)
            n, r = unit(B.tok[rows].astype(F32))
            gn = B.gwork[rows]
            B.low_out[rows] = (B.ghidden[rows] + unit_back(gn, gain, n, r)).astype(BF)
            return carry[0] + fold(gn * n), carry[1] + fold(gn)

        sums = lax.fori_loop(0, 8, last_block, (zero, zero), unroll=2)
        vec[LN_GAIN : LN_GAIN + 1] = down_rows(sums[0])
        vec[LN_SHIFT : LN_SHIFT + 1] = down_rows(sums[1])
        state["out"] = pltpu.make_async_copy(B.low_out, B.tokens_grad, B.ws.at[0])
        state["out"].start()
        gather.ring_y()

    def second_ring(m):
        rings[m].arrive()
        base = rings[m].p * 256
        b1, b2 = two(B.b1), two(B.b2)
        rings2[m] = RingSum(here, "ba"[m], apart[m], base, 64, b1, b2, sems)
        rings2[m].start()

    def attention_swap(m):
        rings2[m].arrive()
        base = rings2[m].base + rings2[m].p * 64
        away = pl.ds(pl.multiple_of(base + (1 - x) * 32, 32), 32)
        swaps[m] = sems.copy(apart[m].at[away], B.ax, here.dev(x=1 - x))

    def attention_out(m):
        swaps[m].wait_recv()
        base = rings2[m].base + rings2[m].p * 64
        B.out_grad[...] = apart[m][pl.ds(pl.multiple_of(base + x * 32, 32), 32)] + B.ax[...]

    s1u.relay()
    move_gp0()
    s0w.relay()
    second.end()
    eg1[1].multiply()
    back0.third(0)
    result()
    back0.third(1)
    back0.third(2)
    eg1[0].multiply()
    back0.end()
    first_sublayer(1)
    attention_back()
    eg1[1].ring.middle()
    first_sublayer(0)
    eg1[0].ring.middle()
    qkv.move((B.gq, B.gk, B.gv))
    eg1[0].across()
    eg0[0].ring.middle()
    eg1[1].across()
    state["back"].third(0)
    state["back"].third(1)
    state["back"].third(2)
    tokens_back()
    eg0[1].ring.middle()
    qkv_multiply()
    eg0[0].across()
    attention_grads(1)
    gather.ring_z()
    qkv.ring.middle()
    eg0[1].across()
    rings[1].middle()
    eg0[0].spread()
    eg1[1].spread()
    qkv.across()
    second_ring(1)
    eg0[1].spread()
    gather.pair()
    rings2[1].middle()
    eg1[0].spread()
    eg0[0].finish((B.up_grad, B.down_grad)[0], 0)
    qkv.spread()
    attention_swap(1)
    qkv.finish(B.qkv_grad)
    eg1[0].finish((B.up_grad, B.down_grad)[0], 1)
    attention_out(1)
    eg0[1].finish((B.up_grad, B.down_grad)[1], 0)
    gather.finish(B.sums)
    eg1[1].finish((B.up_grad, B.down_grad)[1], 1)
    state["out"].wait()
    assert sems.n == N_SEMS, sems.n
    for job in (sn, s0u, s0w, gather, qkv, *rings.values(), *rings2.values()):
        job.done()
    for cp in [*swaps.values(), *gate_cps]:
        cp.wait_send()


def finish_kernel(*refs):
    big_in, sums, big_out = refs[:6], refs[6], refs[7:13]
    gain, shift, out_b, cent, ffn_g, ffn_s, down_b, up_b, qv_b, rms, sem = refs[13:]
    cps = [pltpu.make_async_copy(a, b, sem.at[k]) for k, (a, b) in enumerate(zip(big_in, big_out))]
    for cp in cps:
        cp.start()
    d = lax.axis_index("dp")
    near = sums[:, pl.ds(pl.multiple_of((d // 4) * 128, 128), 128)]
    share = near[:, :32]
    for k in range(1, 4):
        share = jnp.where(d % 4 == k, near[:, k * 32 : k * 32 + 32], share)
    for ref, at in ((gain, LN_GAIN), (shift, LN_SHIFT), (out_b, OUT_BIAS)):
        ref[...] = share[at : at + 1]
    cent[...] = share[CENT : CENT + 2]
    for ref, at in ((ffn_g, GAIN), (ffn_s, SHIFT), (down_b, DOWN_B)):
        for e in range(2):
            ref[e] = share[at + e * 2 : at + e * 2 + 2]
    for e in range(2):
        up_b[e] = sums[UP_B + e * 2 : UP_B + e * 2 + 2]
    qv_b[0:1] = sums[QV_B : QV_B + 1, 0:256]
    qv_b[1:2] = sums[QV_B : QV_B + 1, 256:512]
    totals = sums[STATS : STATS + 1, 0:128]
    rms[...] = jnp.sqrt(totals[:, :4] / (totals[:, 4:5] * 1024.0))
    for cp in cps:
        cp.wait()


SMALL = [(1, 32), (1, 32), (1, 32), (2, 32), (2, 2, 32), (2, 2, 32), (2, 2, 32), (2, 2, 1024), (2, 256), (1, 4)]


def local(
    tokens, segments, routes, slot_table, ln_gain, ln_shift, qkv_proj, qv_bias, out_proj, out_bias,
    centroids, ffn_gain, ffn_shift, up_proj, up_bias, down_proj, down_bias, cotangent,
):
    in_specs = [
        pl.BlockSpec(memory_space=pl.ANY if name in IN_HBM else VM) for name in INPUTS
    ]
    outs = pl.pallas_call(
        layer_kernel,
        out_shape=tuple(jax.ShapeDtypeStruct(*spec) for spec in OUTPUTS.values()),
        in_specs=in_specs,
        out_specs=[
            pl.BlockSpec(memory_space=pl.ANY if name in OUT_HBM else VM) for name in OUTPUTS
        ],
        scratch_shapes=[VM(*spec) for spec in SCRATCH.values()]
        + [pltpu.SemaphoreType.DMA((N_SEMS,)), pltpu.SemaphoreType.DMA((N_SEMS,)), pltpu.SemaphoreType.DMA((6,)), pltpu.SemaphoreType.REGULAR((2,))],
        compiler_params=pltpu.CompilerParams(
            collective_id=0, has_side_effects=True, vmem_limit_bytes=VMEM_LIMIT
        ),
    )(
        tokens, segments.reshape(1, 256), routes.reshape(1, 256), slot_table,
        ln_gain, ln_shift, qkv_proj, qv_bias, out_proj,
        out_bias, centroids, ffn_gain, ffn_shift, up_proj, up_bias, down_proj,
        down_bias, cotangent,
    )
    anywhere = pl.BlockSpec(memory_space=pl.ANY)
    near = pl.BlockSpec(memory_space=VM)
    (
        result, tokens_grad, qkv_grad, out_grad, up_grad, down_grad,
        gain, shift, out_b, cent, ffn_g, ffn_s, down_b, up_b, qv_b, rms,
    ) = pl.pallas_call(
        finish_kernel,
        out_shape=tuple(jax.ShapeDtypeStruct(a.shape, a.dtype) for a in outs[:6])
        + tuple(jax.ShapeDtypeStruct(shape, F32) for shape in SMALL),
        in_specs=[near] * 7,
        out_specs=[anywhere] * 6 + [near] * len(SMALL),
        scratch_shapes=[pltpu.SemaphoreType.DMA((6,))],
    )(*outs)
    return (
        result,
        tokens_grad,
        gain.reshape(32),
        shift.reshape(32),
        qkv_grad,
        qv_b,
        out_grad.T,
        out_b.reshape(32),
        cent,
        ffn_g,
        ffn_s,
        up_grad,
        up_b,
        jnp.swapaxes(down_grad, 2, 3),
        down_b,
        rms.reshape(4),
    )


VMEM_LIMIT = 63 * 2**20


def solution(mesh):
    return jax.shard_map(
        local,
        mesh=mesh,
        in_specs=(
            P("dp", None),
            P("dp"),
            P("dp"),
            P("dp", None, None),
            P(),
            P(),
            P(None, None, "tensor"),
            P(None, "tensor"),
            P("tensor", None),
            P(),
            P(),
            P(),
            P(),
            P(None, None, None, "tensor"),
            P(None, None, "tensor"),
            P(None, None, "tensor", None),
            P(),
            P("dp", None),
        ),
        out_specs=(
            P("dp", None),
            P("dp", None),
            P("dp"),
            P("dp"),
            P(None, "dp", "tensor"),
            P(None, "tensor"),
            P("tensor", "dp"),
            P("dp"),
            P(None, "dp"),
            P(None, None, "dp"),
            P(None, None, "dp"),
            P(None, None, "dp", "tensor"),
            P(None, None, "tensor"),
            P(None, None, "tensor", "dp"),
            P(None, None, "dp"),
            P(),
        ),
        check_vma=False,
    )
```

```python
import math

import jax
import jax.numpy as jnp
from jax import lax
from jax.experimental import pallas as pl
from jax.experimental.pallas import tpu as pltpu
from jax.sharding import PartitionSpec as P

HD = 64
MESH = pl.DeviceIdType.MESH
OTHER = {"a": "b", "b": "a"}
VM = pltpu.VMEM
F32 = jnp.float32
BF = jnp.bfloat16
EPS = 1e-05
SCALE = HD ** (-0.5)
ROOT = math.sqrt(2.0 / math.pi)
COLS = [pl.ds(n * 256, 256) for n in range(4)]
LN_GAIN, LN_SHIFT, OUT_BIAS, CENT, GAIN, SHIFT, DOWN_B, UP_B, QV_B, STATS = (
    0, 1, 2, 3, 5, 9, 13, 17, 21, 22,
)


class Here:
    def __init__(self):
        d = lax.axis_index("dp")
        t = lax.axis_index("tensor")
        self.x, self.y, self.z = d // 16, (d // 4) % 4, d % 4
        self.h, self.c = t // 2, t % 2
        self.a = self.y * (1 - self.c) + self.z * self.c
        self.b = self.z * (1 - self.c) + self.y * self.c

    def dev(self, x=None, y=None, z=None, h=None, c=None):
        x = self.x if x is None else x
        y = self.y if y is None else y
        z = self.z if z is None else z
        h = self.h if h is None else h
        c = self.c if c is None else c
        return (x * 16 + y * 4 + z, h * 2 + c)

    def ring(self, axis, step, c=None):
        on_y = {"y": 1, "z": 0, "a": 1 - self.c, "b": self.c}[axis]
        y, z = (self.y + step * on_y) % 4, (self.z + step * (1 - on_y)) % 4
        return self.dev(y=y, z=z, c=c)


def here_not(flag):
    return not flag if isinstance(flag, bool) else jnp.logical_not(flag)


class Sems:
    def __init__(self, send, recv):
        self.send, self.recv, self.n = send, recv, 0

    def block(self, n):
        self.n += n
        return self.n - n

    def all_recv(self, k, view):
        pltpu.make_async_copy(view, view, self.recv.at[k]).wait()

    def all_sent(self, k, view):
        pltpu.make_async_copy(view, view, self.send.at[k]).wait()

    def copy(self, src, dst, dev, k=None):
        if k is None:
            k = self.block(1)
        cp = pltpu.make_async_remote_copy(
            src_ref=src,
            dst_ref=dst,
            send_sem=self.send.at[k],
            recv_sem=self.recv.at[k],
            device_id=dev,
            device_id_type=MESH,
        )
        cp.start()
        return cp


def nn(a, b):
    return jnp.dot(a, b, preferred_element_type=F32)


def nt(a, b):
    return lax.dot_general(a, b, (((1,), (1,)), ((), ())), preferred_element_type=F32)


def tn(a, b):
    return lax.dot_general(a, b, (((0,), (0,)), ((), ())), preferred_element_type=F32)


def pick(hot, v):
    a = v.astype(BF)
    rest = v - a.astype(F32)
    b = rest.astype(BF)
    c = (rest - b.astype(F32)).astype(BF)
    return nn(hot, a) + nn(hot, b) + nn(hot, c)


def unit(v):
    center = v - jnp.mean(v, axis=-1, keepdims=True)
    r = lax.rsqrt(jnp.mean(center * center, axis=-1, keepdims=True) + EPS)
    return center * r, r


def unit_back(grad, gain, n, r):
    u = grad * gain
    return r * (u - jnp.mean(u, axis=-1, keepdims=True) - n * jnp.mean(u * n, axis=-1, keepdims=True))


def fold(v):
    return jnp.sum(v.reshape(v.shape[0] // 8, 8, v.shape[1]), axis=0)


def down_rows(v):
    return jnp.sum(v, axis=0, keepdims=True)


def rows32(i):
    return pl.ds(pl.multiple_of(i * 32, 32), 32)


class TensorSum:
    def __init__(self, here, sems, p, lc, lx, out, at):
        self.sems, self.p, self.lc, self.lx, self.out, self.at = sems, p, lc, lx, out, at
        self.core = here.dev(c=1 - here.c)
        self.across = here.dev(h=1 - here.h)
        self.mine = pl.ds(pl.multiple_of(here.c * 128, 128), 128)
        self.other = pl.ds(pl.multiple_of((1 - here.c) * 128, 128), 128)
        self.a, self.b, self.d = [], [], []

    def first(self, n):
        cp = self.sems.copy(self.p.at[n, self.other], self.lc.at[n], self.core, self.at[0] + n)
        self.a.append(cp)

    def second(self, n):
        self.a[n].wait_recv()
        self.p[n, self.mine] = self.p[n, self.mine] + self.lc[n]
        cp = self.sems.copy(self.p.at[n, self.mine], self.lx.at[n], self.across, self.at[1] + n)
        self.b.append(cp)

    def third(self, n):
        self.b[n].wait_recv()
        self.out[self.mine, COLS[n]] = self.p[n, self.mine] + self.lx[n]
        spot = self.out.at[self.mine, COLS[n]]
        self.d.append(self.sems.copy(spot, spot, self.core, self.at[2] + n))

    def send(self, make):
        for n in range(4):
            self.p[n] = make(n)
            self.first(n)
            if n:
                self.second(n - 1)
        self.second(3)

    def end(self):
        for n in range(len(self.d), 4):
            self.third(n)
        for cp in self.d:
            cp.wait_recv()
        for cp in self.a + self.b + self.d:
            cp.wait_send()


class RingSum:
    def __init__(self, here, axis, buf, base, rows, l1, l2, sems):
        self.p = getattr(here, axis)
        self.buf, self.base, self.rows = buf, base, rows
        self.l1, self.l2, self.sems = l1, l2, sems
        self.plus, self.minus = here.ring(axis, 1), here.ring(axis, 3)
        self.cps = []

    def part(self, step, half):
        n = self.rows // 2
        at = self.base + ((self.p + step) % 4) * self.rows + half * n
        return pl.ds(pl.multiple_of(at, n), n)

    def own(self):
        at = self.base + self.p * self.rows
        return pl.ds(pl.multiple_of(at, self.rows), self.rows)

    def start(self):
        n, buf, sems = self.rows // 2, self.buf, self.sems
        lo, hi = pl.ds(0, n), pl.ds(n, n)
        self.a = sems.copy(buf.at[self.part(2, 0)], self.l1[0], self.plus)
        self.b = sems.copy(buf.at[self.part(2, 1)], self.l1[1], self.minus)
        self.cps.append(sems.copy(buf.at[self.part(1, 1)], self.l2[0].at[hi], self.plus))
        self.cps.append(sems.copy(buf.at[self.part(3, 0)], self.l2[1].at[lo], self.minus))
        return self

    def middle(self):
        n, buf, sems = self.rows // 2, self.buf, self.sems
        lo, hi = pl.ds(0, n), pl.ds(n, n)
        up, dn = self.part(1, 0), self.part(3, 1)
        self.a.wait_recv()
        buf[up] = buf[up] + self.l1[0][...]
        self.cps.append(sems.copy(buf.at[up], self.l2[0].at[lo], self.plus))
        self.b.wait_recv()
        buf[dn] = buf[dn] + self.l1[1][...]
        self.cps.append(sems.copy(buf.at[dn], self.l2[1].at[hi], self.minus))

    def arrive(self):
        for cp in self.cps:
            cp.wait_recv()
        own = self.own()
        self.buf[own] = self.buf[own] + self.l2[0][...] + self.l2[1][...]

    def done(self):
        for cp in [self.a, self.b] + self.cps:
            cp.wait_send()


class Shared:
    def __init__(self, here, axis, buf, sems):
        self.here, self.axis, self.buf, self.sems = here, axis, buf, sems
        self.p = getattr(here, axis)

    def spot(self, step, half=None):
        at = ((self.p + step) % 4) * 256
        if half is None:
            return pl.ds(pl.multiple_of(at, 256), 256)
        return pl.ds(pl.multiple_of(at + half * 128, 128), 128)

    def start(self, src):
        rows = pl.ds(pl.multiple_of(self.here.c * 128, 128), 128)
        for half in range(2):
            part = src[rows, half * 512 : half * 512 + 512]
            self.buf[self.spot(0, half)] = part.astype(F32)
        mine = self.buf.at[self.spot(0)]
        self.near = [self.sems.copy(mine, mine, self.here.ring(self.axis, s)) for s in (1, 3)]
        return self

    def relay(self):
        self.far = []
        for cp, frm, to, half in ((self.near[0], 3, 1, 0), (self.near[1], 1, 3, 1)):
            cp.wait_recv()
            part = self.buf.at[self.spot(frm, half)]
            self.far.append(self.sems.copy(part, part, self.here.ring(self.axis, to)))

    def arrive(self):
        for cp in self.far:
            cp.wait_recv()

    def done(self):
        for cp in self.near + self.far:
            cp.wait_send()


class Moved:
    def __init__(self, here, axis, lane, ys, gy, sems):
        self.here, self.axis, self.ys, self.gy, self.sems = here, axis, ys, gy, sems
        self.lanes = pl.ds(lane, 256)

    def start(self, src):
        here, ys, gy, lanes = self.here, self.ys, self.gy, self.lanes
        c = here.c
        for q in range(4):
            ys[q * 256 : q * 256 + 256, lanes] = src[:, q * 256 : q * 256 + 256].astype(F32)
        self.k = self.sems.block(1)
        for step in (1, 3, 2, 0):
            for dc in range(2):
                axis = self.axis if dc == 0 else OTHER[self.axis]
                p, e = getattr(here, axis), (c + dc) % 2
                q = (p + step) % 4
                spot = pl.ds(pl.multiple_of(p * 256 + c * 128, 128), 128)
                rows = pl.ds(pl.multiple_of(q * 256 + e * 128, 128), 128)
                if step == 0 and dc == 0:
                    gy[spot, lanes] = ys[rows, lanes]
                    continue
                to = here.ring(axis, step, c=e)
                self.sems.copy(ys.at[rows, lanes], gy.at[spot, lanes], to, self.k)
        return self

    def sent(self):
        self.sems.all_sent(self.k, self.ys.at[pl.ds(0, 896), self.lanes])

    def arrive(self):
        self.sems.all_recv(self.k, self.gy.at[pl.ds(0, 896), self.lanes])


class ExpertGrads:
    def __init__(self, here, m, shared, moved, right, part, l1, l2, lx, land, sems, gates=None):
        self.here, self.m, self.shared, self.moved, self.right = here, m, shared, moved, right
        self.part, self.lx, self.land, self.sems, self.gates = part, lx, land, sems, gates
        self.axis = "ab"[m]
        self.ring = RingSum(here, OTHER[self.axis], part, 0, 256, l1, l2, sems)

    def multiply(self):
        self.shared.arrive()
        self.moved.arrive()
        gs, gy, lanes = self.shared.buf, self.moved.gy, self.moved.lanes
        for p in range(4):
            for k in range(2):
                rows = pl.ds(p * 256 + k * 128, 128)
                self.right[p * 128 : p * 128 + 128, k * 256 : k * 256 + 256] = gy[rows, lanes].astype(BF)
        gates = self.gates() if self.gates else None
        ring_on_y = (self.m + self.here.c) % 2
        per_y, per_z = 32 + 224 * ring_on_y, 256 - 224 * ring_on_y

        def block(k, carry):
            lanes = pl.ds(pl.multiple_of((k % 4) * 128, 128), 128)
            left = []
            for p in range(4):
                v = gs[pl.ds(pl.multiple_of(p * 256 + (k // 4) * 128, 128), 128), lanes]
                left.append((v if gates is None else gates[p] * v).astype(BF))
            res = tn(jnp.concatenate(left, axis=0), self.right[...])
            for z in range(4):
                at = (k // 4) * 128 + (k % 4) * per_y + z * per_z
                self.part[pl.ds(pl.multiple_of(at, 32), 32)] = res[z * 32 : z * 32 + 32]
            return carry

        lax.fori_loop(0, 8, block, 0)
        self.ring.start()

    def send_x(self, base, rows):
        here = self.here
        away = pl.ds(pl.multiple_of(base + (1 - here.x) * rows, rows), rows)
        self.swap = self.sems.copy(self.part.at[away], self.lx, here.dev(x=1 - here.x))

    def add_x(self, base, rows):
        self.swap.wait_recv()
        mine = pl.ds(pl.multiple_of(base + self.here.x * rows, rows), rows)
        self.part[mine] = self.part[mine] + self.lx[...]

    def across(self):
        self.ring.arrive()
        self.send_x(self.ring.p * 256, 128)

    def spread(self):
        here = self.here
        self.add_x(self.ring.p * 256, 128)
        base = self.ring.p * 256 + here.x * 128
        p, c = getattr(here, self.axis), here.c
        self.k = self.sems.block(1)
        for step in (1, 3, 2, 0):
            for dc in range(2):
                q, k = (p + step) % 4, (c + dc) % 2
                rows = pl.ds(pl.multiple_of(base + q * 32, 32), 32)
                lanes = pl.ds(pl.multiple_of(k * 256, 256), 256)
                if step == 0 and dc == 0:
                    self.land[p, c] = self.part[rows, lanes]
                    continue
                to = here.ring(self.axis, step, c=k)
                self.sems.copy(self.part.at[rows, lanes], self.land.at[p, c], to, self.k)

    def finish(self, out, j):
        seven = self.part.at[pl.ds(0, 224), pl.ds(0, 256)]
        self.sems.all_recv(self.k, seven)
        for e in range(2):
            for q in range(4):
                out[e, j, :, q * 256 : q * 256 + 256] = self.land[q, e]
        self.sems.all_sent(self.k, seven)
        self.swap.wait_send()
        self.ring.done()


INPUTS = (
    "tok", "seg", "routes", "slots", "ln_gain", "ln_shift", "qkv_w", "qv_bias", "out_w", "out_bias",
    "cent", "ffn_gain", "ffn_shift", "up_w", "up_bias", "down_w", "down_bias", "cot",
)
OUT_HBM = ("result", "tokens_grad")
IN_HBM = ("up_w", "down_w", "qkv_w", "out_w")
OUTPUTS = {
    "result": ((256, 1024), BF),
    "tokens_grad": ((256, 1024), BF),
    "qkv_grad": ((3, 32, 256), F32),
    "out_grad": ((32, 256), F32),
    "up_grad": ((2, 2, 32, 1024), F32),
    "down_grad": ((2, 2, 32, 1024), F32),
    "sums": ((24, 1024), F32),
}
PART = ((1024, 512), F32)
SQUARE = ((256, 1024), F32)
LOW = ((256, 1024), BF)
SCRATCH = {
    "wqkv": ((3, 1024, 256), BF), "wout": ((256, 1024), BF),
    "wup": ((2, 1024, 1024), BF), "wdn": ((2, 1024, 1024), BF),
    "normed": LOW, "q": ((256, 256), BF), "k": ((256, 256), BF), "v": ((256, 256), BF),
    "mixed": ((256, 256), BF), "probs": ((4, 256, 256), F32),
    "gq": ((256, 256), BF), "gk": ((256, 256), BF), "gv": ((256, 256), BF),
    "hot_s": ((256, 256), BF), "hot_t": ((256, 256), BF),
    "valid": ((256, 1), F32), "filled": ((256, 1), F32), "route": ((256, 1), F32),
    "sig": ((256, 1), F32), "gating": ((256, 1), F32), "segc": ((256, 1), F32),
    "hidden": SQUARE, "rows0": SQUARE, "rows1": SQUARE, "rows2": SQUARE,
    "slope0": SQUARE, "gwork": SQUARE, "grows": SQUARE, "ghidden": SQUARE,
    "n": LOW, "act": LOW, "go": LOW, "gp": LOW,
    "pa": ((4, 256, 256), F32), "lca": ((4, 128, 256), F32), "lxa": ((2, 4, 128, 256), F32),
    "pb": ((4, 256, 256), F32), "lcb": ((4, 128, 256), F32), "lxb": ((4, 128, 256), F32),
    "gs0u": PART, "gs0w": PART, "gs1u": PART, "gs1w": PART,
    "ys": PART, "gy0": PART, "gy1": PART,
    "right": ((512, 512), BF),
    "partu": PART, "partw": PART,
    "l1": ((2, 2, 128, 512), F32), "l2": ((2, 2, 256, 512), F32),
    "lx": ((2, 2, 128, 512), F32), "gates": ((4, 8, 128), F32), "land": ((2, 2, 4, 2, 32, 256), F32),
    "a1": ((2, 2, 128, 384), F32), "a2": ((2, 2, 256, 384), F32),
    "b1": ((2, 32, 256), F32), "b2": ((2, 64, 256), F32), "ax": ((32, 256), F32),
    "gsn": PART, "gyn": ((512, 384), F32), "lxn": ((128, 384), F32), "landn": ((2, 2, 32, 384), F32),
    "vb": ((10, 24, 1024), F32), "low_out": LOW,
}
N_SEMS = 116


class QkvGrads:
    def __init__(self, here, shared, ys, gy, right, part, l1, l2, lx, land, sems):
        self.here, self.shared, self.ys, self.gy, self.right = here, shared, ys, gy, right
        self.part, self.lx, self.land, self.sems = part, lx, land, sems
        self.ring = RingSum(here, "b", part, 0, 256, l1, l2, sems)
        self.stays = here.a // 2 == here.c

    def move(self, grads):
        here, ys, gy, c = self.here, self.ys, self.gy, self.here.c
        for n, g in enumerate(grads):
            ys[:, COLS[n]] = g[...].astype(F32)
        self.k = self.sems.block(1)
        for dc in range(2):
            axis, e = "ab"[dc], (c + dc) % 2
            p = getattr(here, axis)
            spot = gy.at[pl.ds(pl.multiple_of(p * 128, 128), 128)]
            for q in range(2):
                to = 2 * c + q
                block = ys.at[
                    pl.ds(pl.multiple_of(e * 128, 128), 128), q * 384 : q * 384 + 384
                ]

                def send(block=block, spot=spot, to=to, axis=axis, e=e, p=p):
                    self.sems.copy(block, spot, here.ring(axis, to - p + 4, c=e), self.k)

                if dc:
                    send()
                    continue

                def keep(block=block, spot=spot):
                    spot[...] = block[...]

                pl.when(to == p)(keep)
                pl.when(to != p)(send)

    def settle(self, wait, rows):
        view = self.gy
        pl.when(self.stays)(lambda: wait(view.at[pl.ds(0, 3 * rows)]))
        pl.when(here_not(self.stays))(lambda: wait(view.at[pl.ds(0, 4 * rows)]))

    def multiply(self):
        self.shared.arrive()
        self.settle(lambda view: self.sems.all_recv(self.k, view), 128)
        self.right[:, 0:384] = self.gy[...].astype(BF)
        c = self.here.c
        per_y, per_z = 32 + 224 * c, 256 - 224 * c

        def block(k, carry):
            lanes = pl.ds(pl.multiple_of((k % 4) * 128, 128), 128)
            left = [
                self.shared.buf[
                    pl.ds(pl.multiple_of(p * 256 + (k // 4) * 128, 128), 128), lanes
                ].astype(BF)
                for p in range(4)
            ]
            res = tn(jnp.concatenate(left, axis=0), self.right[:, 0:384])
            for z in range(4):
                at = (k // 4) * 128 + (k % 4) * per_y + z * per_z
                self.part[pl.ds(pl.multiple_of(at, 32), 32)] = res[z * 32 : z * 32 + 32]
            return carry

        lax.fori_loop(0, 8, block, 0)
        self.ring.start()

    def across(self):
        here = self.here
        self.ring.arrive()
        away = pl.multiple_of(self.ring.p * 256 + (1 - here.x) * 128, 128)
        self.swap = self.sems.copy(self.part.at[pl.ds(away, 128)], self.lx, here.dev(x=1 - here.x))

    def spread(self):
        here = self.here
        self.swap.wait_recv()
        base = self.ring.p * 256 + here.x * 128
        mine = pl.ds(pl.multiple_of(base, 128), 128)
        self.part[mine] = self.part[mine] + self.lx[...]
        self.k2 = self.sems.block(1)
        p, owner = here.a, here.a // 2
        spot = self.land.at[p % 2, here.c]
        for step in (1, 3, 2, 0):
            block = self.part.at[pl.ds(pl.multiple_of(base + ((p + step) % 4) * 32, 32), 32)]

            def send(block=block, step=step):
                self.sems.copy(block, spot, here.ring("a", step, c=owner), self.k2)

            if step:
                send()
                continue

            def keep(block=block):
                spot[...] = block[...]

            pl.when(self.stays)(keep)
            pl.when(here_not(self.stays))(send)

    def finish(self, out):
        self.settle(lambda view: self.sems.all_recv(self.k2, view), 32)
        left, right = (self.land[half, 0] + self.land[half, 1] for half in range(2))
        out[0] = left[:, 0:256]
        out[1, :, 0:128] = left[:, 256:384]
        out[1, :, 128:256] = right[:, 0:128]
        out[2] = right[:, 128:384]

    def done(self):
        self.settle(lambda view: self.sems.all_sent(self.k, view), 128)
        self.settle(lambda view: self.sems.all_sent(self.k2, view), 32)
        self.swap.wait_send()
        self.ring.done()


class Totals:
    def __init__(self, here, buf, sems):
        self.here, self.buf, self.sems, self.cps, self.wait = here, buf, sems, [], []

    def send(self, at, to, devices):
        spots = self.buf.at[at], self.buf.at[to]
        self.wait = [self.sems.copy(*spots, dev) for dev in devices]
        self.cps += self.wait

    def four(self, at):
        for cp in self.wait:
            cp.wait_recv()
        buf = self.buf
        return (buf[at] + buf[at + 1]) + (buf[at + 2] + buf[at + 3])

    def ring_y(self):
        at = 1 + self.here.y
        self.buf[at] = self.buf[0]
        self.send(at, at, [self.here.ring("y", step) for step in (1, 3, 2)])

    def ring_z(self):
        at = 5 + self.here.z
        self.buf[at] = self.four(1)
        self.send(at, at, [self.here.ring("z", step) for step in (1, 3, 2)])

    def pair(self):
        self.buf[0] = self.four(5)
        self.send(0, 9, [self.here.dev(x=1 - self.here.x)])

    def finish(self, out):
        self.wait[0].wait_recv()
        out[...] = self.buf[0] + self.buf[9]

    def done(self):
        for cp in self.cps:
            cp.wait_send()


class Bag:
    pass


def two(ref):
    return [ref.at[0], ref.at[1]]


def layer_kernel(*refs):
    B = Bag()
    for name, ref in zip([*INPUTS, *OUTPUTS, *SCRATCH, "ss", "rs", "ws", "free"], refs):
        setattr(B, name, ref)
    B.n0 = B.n1 = B.gbranch = B.n
    B.act0 = B.act1 = B.act
    B.go0 = B.go1 = B.go
    B.gp0 = B.gp1 = B.gp
    here = Here()
    sems = Sems(B.ss, B.rs)
    x, c = here.x, here.c
    vec = B.vb.at[0]
    even = [sems.block(4) for _ in range(3)]
    odd = [even[0], sems.block(4), even[2]]

    peers = [here.dev(c=1 - c), here.dev(h=1 - here.h), here.dev(x=1 - x)]
    for axis in ("y", "z"):
        for step in (1, 2, 3):
            for dc in range(2):
                peers.append(here.ring(axis, step, c=(c + dc) % 2))
    bar = pltpu.get_barrier_semaphore()
    for dev in peers:
        pl.semaphore_signal(bar, inc=1, device_id=dev, device_id_type=MESH)

    def fetch(pairs, at):
        cps = [pltpu.make_async_copy(s, t, B.ws.at[at + k]) for k, (s, t) in enumerate(pairs)]
        for cp in cps:
            cp.start()
        return cps

    def fetch_experts(j):
        return fetch(
            [(B.up_w.at[e, j], B.wup.at[e]) for e in range(2)]
            + [(B.down_w.at[e, j], B.wdn.at[e]) for e in range(2)],
            2,
        )

    heads = fetch([(B.qkv_w, B.wqkv), (B.out_w, B.wout)], 0)
    experts = fetch_experts(0)

    B.vb[0] = jnp.zeros((24, 1024), F32)
    lane1024 = lax.broadcasted_iota(jnp.int32, (1, 1024), 1)

    def stat(k, total):
        row = jnp.where(lane1024 == k, total, 0.0)
        vec[STATS : STATS + 1] = vec[STATS : STATS + 1] + row

    def total(v):
        return jnp.sum(jnp.sum(v, axis=1, keepdims=True), axis=0, keepdims=True)

    down_i = lax.broadcasted_iota(jnp.int32, (256, 256), 0)
    along_i = lax.broadcasted_iota(jnp.int32, (256, 256), 1)

    def column(row):
        return jnp.sum(jnp.where(down_i == along_i, row, 0.0), axis=1, keepdims=True)

    seg_row = B.seg[...].astype(F32)
    B.segc[...] = column(seg_row)
    B.valid[...] = (B.segc[...] != 0.0).astype(F32)

    def allowed():
        return (B.segc[...] == seg_row) & (along_i <= down_i) & (B.segc[...] != 0.0)

    head_of = along_i // HD

    gain = B.ln_gain[...].astype(F32).reshape(1, 1024)
    shift = B.ln_shift[...].astype(F32).reshape(1, 1024)

    def norm_block(i, carry):
        n, _ = unit(B.tok[rows32(i)].astype(F32))
        B.normed[rows32(i)] = (n * gain + shift).astype(BF)
        return carry

    lax.fori_loop(0, 8, norm_block, 0, unroll=2)
    for cp in heads:
        cp.wait()
    qv_bias = B.qv_bias[...].astype(F32)
    B.q[...] = (nn(B.normed[...], B.wqkv[0]) + qv_bias[0:1]).astype(BF)
    B.k[...] = nn(B.normed[...], B.wqkv[1]).astype(BF)
    B.v[...] = (nn(B.normed[...], B.wqkv[2]) + qv_bias[1:2]).astype(BF)

    def one_head(value, hh):
        return jnp.where(head_of == hh, value.astype(F32), 0.0)

    mixed = jnp.zeros((256, 256), F32)
    for hh in range(4):
        s = nt(one_head(B.q[...], hh).astype(BF), B.k[...]) * SCALE
        ok = allowed()
        s = jnp.where(ok, s, -1e30)
        e = jnp.where(ok, jnp.exp(s - jnp.max(s, axis=-1, keepdims=True)), 0.0)
        probs = e / (jnp.sum(e, axis=-1, keepdims=True) + (1.0 - B.valid[...]))
        B.probs[hh] = probs
        mixed = mixed + one_head(nn(probs.astype(BF), B.v[...]), hh)
    B.mixed[...] = mixed.astype(BF)

    pl.semaphore_wait(bar, len(peers))
    sn = Shared(here, "a", B.gsn, sems).start(B.normed)
    branch = TensorSum(here, sems, B.pa, B.lca, B.lxa.at[0], B.hidden, even)
    branch.send(lambda n: nn(B.mixed[...], B.wout[:, COLS[n]]))
    slot_row = jnp.concatenate([B.slots[0, 0:1], B.slots[0, 1:2]], axis=1)
    slot_col = column(slot_row.astype(F32))
    B.hot_s[...] = jnp.where(slot_col == along_i.astype(F32), 1.0, 0.0).astype(BF)
    for n in range(4):
        B.grows[:, COLS[n]] = nn(B.hot_s[...], B.cot[:, COLS[n]])
    s1w = Shared(here, "b", B.gs1w, sems).start(B.grows)
    B.route[...] = column(B.routes[...].astype(F32))
    B.filled[...] = (slot_col < 256.0).astype(F32)
    B.hot_t[...] = jnp.where(slot_row == down_i, 1.0, 0.0).astype(BF)
    stat(4, total(B.valid[...]))
    for n in range(2):
        branch.third(n)
    sn.relay()
    branch.third(2)
    s1w.relay()
    branch.end()

    out_bias = B.out_bias[...].astype(F32).reshape(1, 1024)
    cent = B.cent[...].astype(F32)

    def hidden_block(i, carry):
        rows = rows32(i)
        h = B.tok[rows].astype(F32) + (B.hidden[rows] + out_bias)
        B.hidden[rows] = h
        scores = [jnp.sum(h * cent[e : e + 1], axis=-1, keepdims=True) for e in range(2)]
        logits = jnp.where(B.route[rows] == 1.0, scores[1], scores[0])
        sig = 1.0 / (1.0 + jnp.exp(-logits))
        B.sig[rows] = sig
        B.gating[rows] = sig * B.valid[rows]
        return carry + fold(h * h * B.valid[rows])

    stat(0, total(lax.fori_loop(0, 8, hidden_block, jnp.zeros((8, 1024), F32), unroll=2)))
    for n in range(4):
        B.rows0[:, COLS[n]] = pick(B.hot_s[...], B.hidden[:, COLS[n]])
    ffn_gain = B.ffn_gain[...].astype(F32)
    ffn_shift = B.ffn_shift[...].astype(F32)
    up_bias = B.up_bias[...].astype(F32)
    down_bias = B.down_bias[...].astype(F32)

    def expert_norm(rows_ref, low_ref, j):
        for e in range(2):
            g, s = ffn_gain[e, j : j + 1], ffn_shift[e, j : j + 1]

            def block(i, carry, e=e, g=g, s=s):
                rows = rows32(e * 4 + i)
                n, _ = unit(rows_ref[rows])
                low_ref[rows] = (n * g + s).astype(BF)
                return carry

            lax.fori_loop(0, 4, block, 0, unroll=2)

    def gelu_parts(v):
        t = jnp.tanh(ROOT * (v + 0.044715 * (v * v * v)))
        cdf = 0.5 * (1.0 + t)
        slope = cdf + (0.5 * ROOT) * v * (1.0 - t * t) * (1.0 + (3.0 * 0.044715) * (v * v))
        return v * cdf, slope

    def half(e):
        return pl.ds(e * 128, 128)

    expert_norm(B.rows0, B.n0, 0)
    s0u = Shared(here, "a", B.gs0u, sems).start(B.n0)
    for cp in experts:
        cp.wait()
    for e in range(2):
        for n in range(4):
            pre = nn(B.n0[half(e)], B.wup[e, :, COLS[n]]) + up_bias[e, 0:1, n * 256 : n * 256 + 256]
            act, slope = gelu_parts(pre)
            B.act0[half(e), COLS[n]] = act.astype(BF)
            B.slope0[half(e), COLS[n]] = slope

    def down(act_ref):
        def make(n):
            return jnp.concatenate(
                [nn(act_ref[half(e)], B.wdn[e, :, COLS[n]]) for e in range(2)], axis=0
            )

        return make

    first = TensorSum(here, sems, B.pa, B.lca, B.lxa.at[1], B.rows1, odd)
    first.send(down(B.act0))
    experts = fetch_experts(1)
    m0w = Moved(here, "b", 256, B.ys, B.gy0, sems).start(B.act0)
    gate_row = down_rows(B.hot_t[...].astype(F32) * B.gating[...])
    gate_col = column(gate_row)
    B.gates[here.b] = jnp.broadcast_to(jnp.where(c == 0, gate_row[:, :128], gate_row[:, 128:]), (8, 128))
    mine = B.gates.at[here.b]
    gate_cps = [sems.copy(mine, mine, here.ring("b", step)) for step in (1, 3, 2)]
    for n in range(4):
        g = gate_col * B.grows[:, COLS[n]]
        B.grows[:, COLS[n]] = g
        B.go1[:, COLS[n]] = g.astype(BF)
    for e in range(2):
        vec[DOWN_B + e * 2 + 1 : DOWN_B + e * 2 + 2] = down_rows(B.go1[half(e)].astype(F32))
    for cp in experts:
        cp.wait()
    for e in range(2):
        for n in range(4):
            B.gwork[half(e), COLS[n]] = nt(B.go1[half(e)], B.wdn[e, COLS[n], :])
    for n in range(3):
        first.third(n)
    s0u.relay()
    first.end()

    sq = jnp.zeros((8, 1024), F32)
    for e in range(2):
        bias = down_bias[e, 0:1]

        def rows1_block(i, carry, e=e, bias=bias):
            rows = rows32(e * 4 + i)
            r1 = B.rows0[rows] + (B.rows1[rows] + bias)
            B.rows1[rows] = r1
            return carry + fold(r1 * r1 * B.filled[rows])

        sq = lax.fori_loop(0, 4, rows1_block, sq, unroll=2)
    stat(1, total(sq))
    expert_norm(B.rows1, B.n1, 1)
    s1u = Shared(here, "a", B.gs1u, sems).start(B.n1)
    for e in range(2):
        for n in range(4):
            pre = nn(B.n1[half(e)], B.wup[e, :, COLS[n]]) + up_bias[e, 1:2, n * 256 : n * 256 + 256]
            act, slope = gelu_parts(pre)
            B.act1[half(e), COLS[n]] = act.astype(BF)
            gp = (B.gwork[half(e), COLS[n]] * slope).astype(BF)
            B.gp1[half(e), COLS[n]] = gp
            vec[UP_B + e * 2 + 1 : UP_B + e * 2 + 2, COLS[n]] = down_rows(gp.astype(F32))

    def normed_grad(gp_ref):
        def make(n):
            return jnp.concatenate(
                [nt(gp_ref[half(e)], B.wup[e, COLS[n], :]) for e in range(2)], axis=0
            )

        return make

    back1 = TensorSum(here, sems, B.pa, B.lca, B.lxa.at[0], B.gwork, even)
    back1.send(normed_grad(B.gp1))
    m1u = Moved(here, "a", 0, B.ys, B.gy1, sems).start(B.gp1)
    second = TensorSum(here, sems, B.pb, B.lcb, B.lxb, B.rows2, [sems.block(4) for _ in range(3)])
    second.send(down(B.act1))
    experts = fetch_experts(0)
    m0w.sent()
    m1w = Moved(here, "b", 256, B.ys, B.gy1, sems).start(B.act1)
    back1.end()

    def expert_norm_back(rows_ref, j, go_ref):
        for e in range(2):
            g = ffn_gain[e, j : j + 1]

            def block(i, carry, e=e, g=g):
                rows = rows32(e * 4 + i)
                n, r = unit(rows_ref[rows])
                gn = B.gwork[rows]
                new = B.grows[rows] + unit_back(gn, g, n, r)
                B.grows[rows] = new
                out = [carry[0] + fold(gn * n), carry[1] + fold(gn)]
                if go_ref is not None:
                    low = new.astype(BF)
                    go_ref[rows] = low
                    out.append(carry[2] + fold(low.astype(F32)))
                return tuple(out)

            zero = jnp.zeros((8, 1024), F32)
            sums = lax.fori_loop(0, 4, block, (zero,) * (2 if go_ref is None else 3), unroll=2)
            at = e * 2 + j
            vec[GAIN + at : GAIN + at + 1] = down_rows(sums[0])
            vec[SHIFT + at : SHIFT + at + 1] = down_rows(sums[1])
            if go_ref is not None:
                vec[DOWN_B + e * 2 : DOWN_B + e * 2 + 1] = down_rows(sums[2])

    expert_norm_back(B.rows1, 1, B.go0)
    s0w = Shared(here, "b", B.gs0w, sems).start(B.go0)
    for cp in experts:
        cp.wait()
    for e in range(2):
        for n in range(4):
            ga = nt(B.go0[half(e)], B.wdn[e, COLS[n], :])
            gp = (ga * B.slope0[half(e), COLS[n]]).astype(BF)
            B.gp0[half(e), COLS[n]] = gp
            vec[UP_B + e * 2 : UP_B + e * 2 + 1, COLS[n]] = down_rows(gp.astype(F32))
    back0 = TensorSum(here, sems, B.pa, B.lca, B.lxa.at[1], B.gwork, odd)
    back0.send(normed_grad(B.gp0))
    state = {}
    def slot_gates():
        for cp in gate_cps:
            cp.wait_recv()
        eye = down_i[:128, :128] == along_i[:128, :128]
        return [
            jnp.sum(jnp.where(eye, B.gates[p, 0:1], 0.0), axis=1, keepdims=True) for p in range(4)
        ]

    eg1 = [
        ExpertGrads(here, m, (s1u, s1w)[m], (m1u, m1w)[m], B.right, (B.partu, B.partw)[m],
                    two(B.l1.at[m]), two(B.l2.at[m]), B.lx.at[0, m], B.land.at[0, m], sems,
                    gates=(None, slot_gates)[m])
        for m in range(2)
    ]
    m0u = Moved(here, "a", 0, B.ys, B.gy0, sems)
    wide = [pl.ds(0, 512), pl.ds(512, 512)]
    eg0 = [
        ExpertGrads(here, m, (s0u, s0w)[m], (m0u, m0w)[m], B.right, (B.ys, B.gy1)[m],
                    [B.slope0.at[pl.ds(128 * k, 128), wide[m]] for k in range(2)],
                    [(B.hidden, B.rows2)[m].at[:, wide[k]] for k in range(2)],
                    B.lx.at[1, m], B.land.at[1, m], sems)
        for m in range(2)
    ]
    low, few = pl.ds(0, 256), pl.ds(0, 384)
    apart = (None, B.gs1w.at[:, low])
    qkv = QkvGrads(
        here, sn, B.rows0, B.gyn, B.right, B.gs1u.at[:, few],
        two(B.a1.at[0]), two(B.a2.at[0]), B.lxn, B.landn, sems,
    )
    rings, rings2, swaps = {}, {}, {}
    gather = Totals(here, B.vb, sems)

    def move_gp0():
        m1u.sent()
        m0u.start(B.gp0)

    def result():
        sq = jnp.zeros((8, 1024), F32)
        for e in range(2):
            bias = down_bias[e, 1:2]

            def rows2_block(i, carry, e=e, bias=bias):
                rows = rows32(e * 4 + i)
                r2 = B.rows1[rows] + (B.rows2[rows] + bias)
                B.rows2[rows] = r2
                return carry + fold(r2 * r2 * B.filled[rows])

            sq = lax.fori_loop(0, 4, rows2_block, sq, unroll=2)
        stat(2, total(sq))
        gate_grad = jnp.zeros((256, 1), F32)
        result_sq = jnp.zeros((256, 1), F32)
        for n in range(4):
            comb = pick(B.hot_t[...], B.rows2[:, COLS[n]])
            res = B.hidden[:, COLS[n]] + B.gating[...] * comb
            B.low_out[:, COLS[n]] = res.astype(BF)
            result_sq = result_sq + jnp.sum(res * res, axis=-1, keepdims=True)
            gate_grad = gate_grad + jnp.sum(B.cot[:, COLS[n]].astype(F32) * comb, axis=-1, keepdims=True)
        state["out"] = pltpu.make_async_copy(B.low_out, B.result, B.ws.at[0])
        state["out"].start()
        stat(3, total(result_sq * B.valid[...]))
        B.gating[...] = gate_grad * B.sig[...] * (1.0 - B.sig[...]) * B.valid[...]

        def gate_block(i, carry):
            rows = rows32(i)
            gl, second_route = B.gating[rows], B.route[rows] == 1.0
            B.ghidden[rows] = B.cot[rows].astype(F32) + gl * jnp.where(second_route, cent[1:2], cent[0:1])
            v = gl * B.hidden[rows]
            return (
                carry[0] + fold(jnp.where(second_route, 0.0, v)),
                carry[1] + fold(jnp.where(second_route, v, 0.0)),
            )

        zero = jnp.zeros((8, 1024), F32)
        sums = lax.fori_loop(0, 8, gate_block, (zero, zero), unroll=2)
        for e in range(2):
            vec[CENT + e : CENT + e + 1] = down_rows(sums[e])
        for k, axis in enumerate(("b", "a")):
            for step in (1, 3):
                pl.semaphore_signal(
                    B.free.at[k], inc=1, device_id=here.ring(axis, step), device_id_type=MESH
                )

    def attention_back():
        expert_norm_back(B.rows0, 0, None)
        for n in range(4):
            g = B.ghidden[:, COLS[n]] + pick(B.hot_t[...], B.grows[:, COLS[n]])
            B.ghidden[:, COLS[n]] = g
            low = g.astype(BF)
            B.gbranch[:, COLS[n]] = low
            vec[OUT_BIAS : OUT_BIAS + 1, COLS[n]] = down_rows(low.astype(F32))
        gm = nt(B.gbranch[...], B.wout[...]).astype(BF)
        gq = jnp.zeros((256, 256), F32)
        gk = jnp.zeros((256, 256), F32)
        gv = jnp.zeros((256, 256), F32)
        for hh in range(4):
            probs = B.probs[hh]
            gp = nt(one_head(gm, hh).astype(BF), B.v[...])
            gv = gv + one_head(tn(probs.astype(BF), gm), hh)
            gs = (probs * (gp - jnp.sum(probs * gp, axis=-1, keepdims=True))).astype(BF)
            gq = gq + one_head(nn(gs, B.k[...]), hh)
            gk = gk + one_head(tn(gs, B.q[...]), hh)
        B.gq[...] = (gq * SCALE).astype(BF)
        B.gk[...] = (gk * SCALE).astype(BF)
        B.gv[...] = gv.astype(BF)
        vec[QV_B : QV_B + 1, 0:256] = down_rows(B.gq[...].astype(F32))
        vec[QV_B : QV_B + 1, 256:512] = down_rows(B.gv[...].astype(F32))
        state["back"] = back = TensorSum(here, sems, B.pa, B.lca, B.lxa.at[0], B.gwork, even)
        grads = (B.gq, B.gk, B.gv)
        back.send(lambda n: sum(nt(grads[s][...], B.wqkv[s, COLS[n], :]) for s in range(3)))


    def first_sublayer(m):
        if m == 0:
            m1w.sent()
            m0u.sent()
        pl.semaphore_wait(B.free.at[m], 2)
        eg0[m].multiply()

    def qkv_multiply():
        s1u.done()
        qkv.multiply()

    def attention_grads(m):
        s1w.done()
        last_y = (m + c) % 2

        def block(k, carry):
            lanes = pl.ds(pl.multiple_of(k * 128, 128), 128)
            res = tn(B.gbranch[:, lanes], B.mixed[...])
            for z in range(4):
                at = (k // 4) * 32 + (k % 4) * (256 - 192 * last_y) + z * (64 + 192 * last_y)
                apart[m][pl.ds(pl.multiple_of(at, 32), 32)] = res[z * 32 : z * 32 + 32]
            return carry

        lax.fori_loop(0, 8, block, 0)
        l1 = [B.a1.at[m, k, :, low] for k in range(2)]
        l2 = [B.a2.at[m, k, :, low] for k in range(2)]
        rings[m] = RingSum(here, "ab"[m], apart[m], 0, 256, l1, l2, sems)
        rings[m].start()

    def tokens_back():
        state["back"].end()
        state["out"].wait()
        zero = jnp.zeros((8, 1024), F32)

        def last_block(i, carry):
            rows = rows32(i)
            n, r = unit(B.tok[rows].astype(F32))
            gn = B.gwork[rows]
            B.low_out[rows] = (B.ghidden[rows] + unit_back(gn, gain, n, r)).astype(BF)
            return carry[0] + fold(gn * n), carry[1] + fold(gn)

        sums = lax.fori_loop(0, 8, last_block, (zero, zero), unroll=2)
        vec[LN_GAIN : LN_GAIN + 1] = down_rows(sums[0])
        vec[LN_SHIFT : LN_SHIFT + 1] = down_rows(sums[1])
        state["out"] = pltpu.make_async_copy(B.low_out, B.tokens_grad, B.ws.at[0])
        state["out"].start()
        gather.ring_y()

    def second_ring(m):
        rings[m].arrive()
        base = rings[m].p * 256
        b1, b2 = two(B.b1), two(B.b2)
        rings2[m] = RingSum(here, "ba"[m], apart[m], base, 64, b1, b2, sems)
        rings2[m].start()

    def attention_swap(m):
        rings2[m].arrive()
        base = rings2[m].base + rings2[m].p * 64
        away = pl.ds(pl.multiple_of(base + (1 - x) * 32, 32), 32)
        swaps[m] = sems.copy(apart[m].at[away], B.ax, here.dev(x=1 - x))

    def attention_out(m):
        swaps[m].wait_recv()
        base = rings2[m].base + rings2[m].p * 64
        B.out_grad[...] = apart[m][pl.ds(pl.multiple_of(base + x * 32, 32), 32)] + B.ax[...]

    s1u.relay()
    move_gp0()
    eg1[1].multiply()
    second.end()
    s0w.relay()
    back0.third(0)
    result()
    eg1[0].multiply()
    back0.third(1)
    back0.third(2)
    back0.end()
    first_sublayer(0)
    eg1[1].ring.middle()
    attention_back()
    qkv.move((B.gq, B.gk, B.gv))
    first_sublayer(1)
    state["back"].third(0)
    eg1[1].across()
    state["back"].third(1)
    eg0[0].ring.middle()
    state["back"].third(2)
    eg0[1].ring.middle()
    tokens_back()
    eg1[0].ring.middle()
    qkv_multiply()
    eg0[0].across()
    attention_grads(1)
    eg0[1].across()
    gather.ring_z()
    eg1[0].across()
    qkv.ring.middle()
    rings[1].middle()
    eg1[1].spread()
    qkv.across()
    eg0[0].spread()
    second_ring(1)
    eg1[0].spread()
    rings2[1].middle()
    eg0[1].spread()
    gather.pair()
    eg0[0].finish((B.up_grad, B.down_grad)[0], 0)
    qkv.spread()
    attention_swap(1)
    attention_out(1)
    qkv.finish(B.qkv_grad)
    gather.finish(B.sums)
    eg1[1].finish((B.up_grad, B.down_grad)[1], 1)
    eg0[1].finish((B.up_grad, B.down_grad)[1], 0)
    eg1[0].finish((B.up_grad, B.down_grad)[0], 1)
    state["out"].wait()
    assert sems.n == N_SEMS, sems.n
    for job in (sn, s0u, s0w, gather, qkv, *rings.values(), *rings2.values()):
        job.done()
    for cp in [*swaps.values(), *gate_cps]:
        cp.wait_send()


def finish_kernel(*refs):
    big_in, sums, big_out = refs[:6], refs[6], refs[7:13]
    gain, shift, out_b, cent, ffn_g, ffn_s, down_b, up_b, qv_b, rms, sem = refs[13:]
    cps = [pltpu.make_async_copy(a, b, sem.at[k]) for k, (a, b) in enumerate(zip(big_in, big_out))]
    for cp in cps:
        cp.start()
    d = lax.axis_index("dp")
    near = sums[:, pl.ds(pl.multiple_of((d // 4) * 128, 128), 128)]
    share = near[:, :32]
    for k in range(1, 4):
        share = jnp.where(d % 4 == k, near[:, k * 32 : k * 32 + 32], share)
    for ref, at in ((gain, LN_GAIN), (shift, LN_SHIFT), (out_b, OUT_BIAS)):
        ref[...] = share[at : at + 1]
    cent[...] = share[CENT : CENT + 2]
    for ref, at in ((ffn_g, GAIN), (ffn_s, SHIFT), (down_b, DOWN_B)):
        for e in range(2):
            ref[e] = share[at + e * 2 : at + e * 2 + 2]
    for e in range(2):
        up_b[e] = sums[UP_B + e * 2 : UP_B + e * 2 + 2]
    qv_b[0:1] = sums[QV_B : QV_B + 1, 0:256]
    qv_b[1:2] = sums[QV_B : QV_B + 1, 256:512]
    totals = sums[STATS : STATS + 1, 0:128]
    rms[...] = jnp.sqrt(totals[:, :4] / (totals[:, 4:5] * 1024.0))
    for cp in cps:
        cp.wait()


SMALL = [(1, 32), (1, 32), (1, 32), (2, 32), (2, 2, 32), (2, 2, 32), (2, 2, 32), (2, 2, 1024), (2, 256), (1, 4)]


def local(
    tokens, segments, routes, slot_table, ln_gain, ln_shift, qkv_proj, qv_bias, out_proj, out_bias,
    centroids, ffn_gain, ffn_shift, up_proj, up_bias, down_proj, down_bias, cotangent,
):
    in_specs = [
        pl.BlockSpec(memory_space=pl.ANY if name in IN_HBM else VM) for name in INPUTS
    ]
    outs = pl.pallas_call(
        layer_kernel,
        out_shape=tuple(jax.ShapeDtypeStruct(*spec) for spec in OUTPUTS.values()),
        in_specs=in_specs,
        out_specs=[
            pl.BlockSpec(memory_space=pl.ANY if name in OUT_HBM else VM) for name in OUTPUTS
        ],
        scratch_shapes=[VM(*spec) for spec in SCRATCH.values()]
        + [pltpu.SemaphoreType.DMA((N_SEMS,)), pltpu.SemaphoreType.DMA((N_SEMS,)), pltpu.SemaphoreType.DMA((6,)), pltpu.SemaphoreType.REGULAR((2,))],
        compiler_params=pltpu.CompilerParams(
            collective_id=0, has_side_effects=True, vmem_limit_bytes=VMEM_LIMIT
        ),
    )(
        tokens, segments.reshape(1, 256), routes.reshape(1, 256), slot_table,
        ln_gain, ln_shift, qkv_proj, qv_bias, out_proj,
        out_bias, centroids, ffn_gain, ffn_shift, up_proj, up_bias, down_proj,
        down_bias, cotangent,
    )
    anywhere = pl.BlockSpec(memory_space=pl.ANY)
    near = pl.BlockSpec(memory_space=VM)
    (
        result, tokens_grad, qkv_grad, out_grad, up_grad, down_grad,
        gain, shift, out_b, cent, ffn_g, ffn_s, down_b, up_b, qv_b, rms,
    ) = pl.pallas_call(
        finish_kernel,
        out_shape=tuple(jax.ShapeDtypeStruct(a.shape, a.dtype) for a in outs[:6])
        + tuple(jax.ShapeDtypeStruct(shape, F32) for shape in SMALL),
        in_specs=[near] * 7,
        out_specs=[anywhere] * 6 + [near] * len(SMALL),
        scratch_shapes=[pltpu.SemaphoreType.DMA((6,))],
    )(*outs)
    return (
        result,
        tokens_grad,
        gain.reshape(32),
        shift.reshape(32),
        qkv_grad,
        qv_b,
        out_grad.T,
        out_b.reshape(32),
        cent,
        ffn_g,
        ffn_s,
        up_grad,
        up_b,
        jnp.swapaxes(down_grad, 2, 3),
        down_b,
        rms.reshape(4),
    )


VMEM_LIMIT = 63 * 2**20


def solution(mesh):
    return jax.shard_map(
        local,
        mesh=mesh,
        in_specs=(
            P("dp", None),
            P("dp"),
            P("dp"),
            P("dp", None, None),
            P(),
            P(),
            P(None, None, "tensor"),
            P(None, "tensor"),
            P("tensor", None),
            P(),
            P(),
            P(),
            P(),
            P(None, None, None, "tensor"),
            P(None, None, "tensor"),
            P(None, None, "tensor", None),
            P(),
            P("dp", None),
        ),
        out_specs=(
            P("dp", None),
            P("dp", None),
            P("dp"),
            P("dp"),
            P(None, "dp", "tensor"),
            P(None, "tensor"),
            P("tensor", "dp"),
            P("dp"),
            P(None, "dp"),
            P(None, None, "dp"),
            P(None, None, "dp"),
            P(None, None, "dp", "tensor"),
            P(None, None, "tensor"),
            P(None, None, "tensor", "dp"),
            P(None, None, "dp"),
            P(),
        ),
        check_vma=False,
    )
```

```python
import math

import jax
import jax.numpy as jnp
from jax import lax
from jax.experimental import pallas as pl
from jax.experimental.pallas import tpu as pltpu
from jax.sharding import PartitionSpec as P

HD = 64
MESH = pl.DeviceIdType.MESH
OTHER = {"a": "b", "b": "a"}
VM = pltpu.VMEM
F32 = jnp.float32
BF = jnp.bfloat16
EPS = 1e-05
SCALE = HD ** (-0.5)
ROOT = math.sqrt(2.0 / math.pi)
COLS = [pl.ds(n * 256, 256) for n in range(4)]
LN_GAIN, LN_SHIFT, OUT_BIAS, CENT, GAIN, SHIFT, DOWN_B, UP_B, QV_B, STATS = (
    0, 1, 2, 3, 5, 9, 13, 17, 21, 22,
)


class Here:
    def __init__(self):
        d = lax.axis_index("dp")
        t = lax.axis_index("tensor")
        self.x, self.y, self.z = d // 16, (d // 4) % 4, d % 4
        self.h, self.c = t // 2, t % 2
        self.a = self.y * (1 - self.c) + self.z * self.c
        self.b = self.z * (1 - self.c) + self.y * self.c

    def dev(self, x=None, y=None, z=None, h=None, c=None):
        x = self.x if x is None else x
        y = self.y if y is None else y
        z = self.z if z is None else z
        h = self.h if h is None else h
        c = self.c if c is None else c
        return (x * 16 + y * 4 + z, h * 2 + c)

    def ring(self, axis, step, c=None):
        on_y = {"y": 1, "z": 0, "a": 1 - self.c, "b": self.c}[axis]
        y, z = (self.y + step * on_y) % 4, (self.z + step * (1 - on_y)) % 4
        return self.dev(y=y, z=z, c=c)


def here_not(flag):
    return not flag if isinstance(flag, bool) else jnp.logical_not(flag)


class Sems:
    def __init__(self, send, recv):
        self.send, self.recv, self.n = send, recv, 0

    def block(self, n):
        self.n += n
        return self.n - n

    def all_recv(self, k, view):
        pltpu.make_async_copy(view, view, self.recv.at[k]).wait()

    def all_sent(self, k, view):
        pltpu.make_async_copy(view, view, self.send.at[k]).wait()

    def copy(self, src, dst, dev, k=None):
        if k is None:
            k = self.block(1)
        cp = pltpu.make_async_remote_copy(
            src_ref=src,
            dst_ref=dst,
            send_sem=self.send.at[k],
            recv_sem=self.recv.at[k],
            device_id=dev,
            device_id_type=MESH,
        )
        cp.start()
        return cp


def nn(a, b):
    return jnp.dot(a, b, preferred_element_type=F32)


def nt(a, b):
    return lax.dot_general(a, b, (((1,), (1,)), ((), ())), preferred_element_type=F32)


def tn(a, b):
    return lax.dot_general(a, b, (((0,), (0,)), ((), ())), preferred_element_type=F32)


def pick(hot, v):
    a = v.astype(BF)
    rest = v - a.astype(F32)
    b = rest.astype(BF)
    c = (rest - b.astype(F32)).astype(BF)
    return nn(hot, a) + nn(hot, b) + nn(hot, c)


def unit(v):
    center = v - jnp.mean(v, axis=-1, keepdims=True)
    r = lax.rsqrt(jnp.mean(center * center, axis=-1, keepdims=True) + EPS)
    return center * r, r


def unit_back(grad, gain, n, r):
    u = grad * gain
    return r * (u - jnp.mean(u, axis=-1, keepdims=True) - n * jnp.mean(u * n, axis=-1, keepdims=True))


def fold(v):
    return jnp.sum(v.reshape(v.shape[0] // 8, 8, v.shape[1]), axis=0)


def down_rows(v):
    return jnp.sum(v, axis=0, keepdims=True)


def rows32(i):
    return pl.ds(pl.multiple_of(i * 32, 32), 32)


class TensorSum:
    def __init__(self, here, sems, p, lc, lx, out, at):
        self.sems, self.p, self.lc, self.lx, self.out, self.at = sems, p, lc, lx, out, at
        self.core = here.dev(c=1 - here.c)
        self.across = here.dev(h=1 - here.h)
        self.mine = pl.ds(pl.multiple_of(here.c * 128, 128), 128)
        self.other = pl.ds(pl.multiple_of((1 - here.c) * 128, 128), 128)
        self.a, self.b, self.d = [], [], []

    def first(self, n):
        cp = self.sems.copy(self.p.at[n, self.other], self.lc.at[n], self.core, self.at[0] + n)
        self.a.append(cp)

    def second(self, n):
        self.a[n].wait_recv()
        self.p[n, self.mine] = self.p[n, self.mine] + self.lc[n]
        cp = self.sems.copy(self.p.at[n, self.mine], self.lx.at[n], self.across, self.at[1] + n)
        self.b.append(cp)

    def third(self, n):
        self.b[n].wait_recv()
        self.out[self.mine, COLS[n]] = self.p[n, self.mine] + self.lx[n]
        spot = self.out.at[self.mine, COLS[n]]
        self.d.append(self.sems.copy(spot, spot, self.core, self.at[2] + n))

    def send(self, make):
        for n in range(4):
            self.p[n] = make(n)
            self.first(n)
            if n:
                self.second(n - 1)
        self.second(3)

    def end(self):
        for n in range(len(self.d), 4):
            self.third(n)
        for cp in self.d:
            cp.wait_recv()
        for cp in self.a + self.b + self.d:
            cp.wait_send()


class RingSum:
    def __init__(self, here, axis, buf, base, rows, l1, l2, sems):
        self.p = getattr(here, axis)
        self.buf, self.base, self.rows = buf, base, rows
        self.l1, self.l2, self.sems = l1, l2, sems
        self.plus, self.minus = here.ring(axis, 1), here.ring(axis, 3)
        self.cps = []

    def part(self, step, half):
        n = self.rows // 2
        at = self.base + ((self.p + step) % 4) * self.rows + half * n
        return pl.ds(pl.multiple_of(at, n), n)

    def own(self):
        at = self.base + self.p * self.rows
        return pl.ds(pl.multiple_of(at, self.rows), self.rows)

    def start(self):
        n, buf, sems = self.rows // 2, self.buf, self.sems
        lo, hi = pl.ds(0, n), pl.ds(n, n)
        self.a = sems.copy(buf.at[self.part(2, 0)], self.l1[0], self.plus)
        self.b = sems.copy(buf.at[self.part(2, 1)], self.l1[1], self.minus)
        self.cps.append(sems.copy(buf.at[self.part(1, 1)], self.l2[0].at[hi], self.plus))
        self.cps.append(sems.copy(buf.at[self.part(3, 0)], self.l2[1].at[lo], self.minus))
        return self

    def middle(self):
        n, buf, sems = self.rows // 2, self.buf, self.sems
        lo, hi = pl.ds(0, n), pl.ds(n, n)
        up, dn = self.part(1, 0), self.part(3, 1)
        self.a.wait_recv()
        buf[up] = buf[up] + self.l1[0][...]
        self.cps.append(sems.copy(buf.at[up], self.l2[0].at[lo], self.plus))
        self.b.wait_recv()
        buf[dn] = buf[dn] + self.l1[1][...]
        self.cps.append(sems.copy(buf.at[dn], self.l2[1].at[hi], self.minus))

    def arrive(self):
        for cp in self.cps:
            cp.wait_recv()
        own = self.own()
        self.buf[own] = self.buf[own] + self.l2[0][...] + self.l2[1][...]

    def done(self):
        for cp in [self.a, self.b] + self.cps:
            cp.wait_send()


class Shared:
    def __init__(self, here, axis, buf, sems):
        self.here, self.axis, self.buf, self.sems = here, axis, buf, sems
        self.p = getattr(here, axis)

    def spot(self, step, half=None):
        at = ((self.p + step) % 4) * 256
        if half is None:
            return pl.ds(pl.multiple_of(at, 256), 256)
        return pl.ds(pl.multiple_of(at + half * 128, 128), 128)

    def start(self, src):
        rows = pl.ds(pl.multiple_of(self.here.c * 128, 128), 128)
        for half in range(2):
            part = src[rows, half * 512 : half * 512 + 512]
            self.buf[self.spot(0, half)] = part.astype(F32)
        mine = self.buf.at[self.spot(0)]
        self.near = [self.sems.copy(mine, mine, self.here.ring(self.axis, s)) for s in (1, 3)]
        return self

    def relay(self):
        self.far = []
        for cp, frm, to, half in ((self.near[0], 3, 1, 0), (self.near[1], 1, 3, 1)):
            cp.wait_recv()
            part = self.buf.at[self.spot(frm, half)]
            self.far.append(self.sems.copy(part, part, self.here.ring(self.axis, to)))

    def arrive(self):
        for cp in self.far:
            cp.wait_recv()

    def done(self):
        for cp in self.near + self.far:
            cp.wait_send()


class Moved:
    def __init__(self, here, axis, lane, ys, gy, sems):
        self.here, self.axis, self.ys, self.gy, self.sems = here, axis, ys, gy, sems
        self.lanes = pl.ds(lane, 256)

    def start(self, src):
        here, ys, gy, lanes = self.here, self.ys, self.gy, self.lanes
        c = here.c
        for q in range(4):
            ys[q * 256 : q * 256 + 256, lanes] = src[:, q * 256 : q * 256 + 256].astype(F32)
        self.k = self.sems.block(1)
        for step in (1, 3, 2, 0):
            for dc in range(2):
                axis = self.axis if dc == 0 else OTHER[self.axis]
                p, e = getattr(here, axis), (c + dc) % 2
                q = (p + step) % 4
                spot = pl.ds(pl.multiple_of(p * 256 + c * 128, 128), 128)
                rows = pl.ds(pl.multiple_of(q * 256 + e * 128, 128), 128)
                if step == 0 and dc == 0:
                    gy[spot, lanes] = ys[rows, lanes]
                    continue
                to = here.ring(axis, step, c=e)
                self.sems.copy(ys.at[rows, lanes], gy.at[spot, lanes], to, self.k)
        return self

    def sent(self):
        self.sems.all_sent(self.k, self.ys.at[pl.ds(0, 896), self.lanes])

    def arrive(self):
        self.sems.all_recv(self.k, self.gy.at[pl.ds(0, 896), self.lanes])


class ExpertGrads:
    def __init__(self, here, m, shared, moved, right, part, l1, l2, lx, land, sems, gates=None):
        self.here, self.m, self.shared, self.moved, self.right = here, m, shared, moved, right
        self.part, self.lx, self.land, self.sems, self.gates = part, lx, land, sems, gates
        self.axis = "ab"[m]
        self.ring = RingSum(here, OTHER[self.axis], part, 0, 256, l1, l2, sems)

    def multiply(self):
        self.shared.arrive()
        self.moved.arrive()
        gs, gy, lanes = self.shared.buf, self.moved.gy, self.moved.lanes
        for p in range(4):
            for k in range(2):
                rows = pl.ds(p * 256 + k * 128, 128)
                self.right[p * 128 : p * 128 + 128, k * 256 : k * 256 + 256] = gy[rows, lanes].astype(BF)
        gates = self.gates() if self.gates else None
        ring_on_y = (self.m + self.here.c) % 2
        per_y, per_z = 32 + 224 * ring_on_y, 256 - 224 * ring_on_y

        def block(k, carry):
            lanes = pl.ds(pl.multiple_of((k % 4) * 128, 128), 128)
            left = []
            for p in range(4):
                v = gs[pl.ds(pl.multiple_of(p * 256 + (k // 4) * 128, 128), 128), lanes]
                left.append((v if gates is None else gates[p] * v).astype(BF))
            res = tn(jnp.concatenate(left, axis=0), self.right[...])
            for z in range(4):
                at = (k // 4) * 128 + (k % 4) * per_y + z * per_z
                self.part[pl.ds(pl.multiple_of(at, 32), 32)] = res[z * 32 : z * 32 + 32]
            return carry

        lax.fori_loop(0, 8, block, 0)
        self.ring.start()

    def send_x(self, base, rows):
        here = self.here
        away = pl.ds(pl.multiple_of(base + (1 - here.x) * rows, rows), rows)
        self.swap = self.sems.copy(self.part.at[away], self.lx, here.dev(x=1 - here.x))

    def add_x(self, base, rows):
        self.swap.wait_recv()
        mine = pl.ds(pl.multiple_of(base + self.here.x * rows, rows), rows)
        self.part[mine] = self.part[mine] + self.lx[...]

    def across(self):
        self.ring.arrive()
        self.send_x(self.ring.p * 256, 128)

    def spread(self):
        here = self.here
        self.add_x(self.ring.p * 256, 128)
        base = self.ring.p * 256 + here.x * 128
        p, c = getattr(here, self.axis), here.c
        self.k = self.sems.block(1)
        for step in (1, 3, 2, 0):
            for dc in range(2):
                q, k = (p + step) % 4, (c + dc) % 2
                rows = pl.ds(pl.multiple_of(base + q * 32, 32), 32)
                lanes = pl.ds(pl.multiple_of(k * 256, 256), 256)
                if step == 0 and dc == 0:
                    self.land[p, c] = self.part[rows, lanes]
                    continue
                to = here.ring(self.axis, step, c=k)
                self.sems.copy(self.part.at[rows, lanes], self.land.at[p, c], to, self.k)

    def finish(self, out, j):
        seven = self.part.at[pl.ds(0, 224), pl.ds(0, 256)]
        self.sems.all_recv(self.k, seven)
        for e in range(2):
            for q in range(4):
                out[e, j, :, q * 256 : q * 256 + 256] = self.land[q, e]
        self.sems.all_sent(self.k, seven)
        self.swap.wait_send()
        self.ring.done()


INPUTS = (
    "tok", "seg", "routes", "slots", "ln_gain", "ln_shift", "qkv_w", "qv_bias", "out_w", "out_bias",
    "cent", "ffn_gain", "ffn_shift", "up_w", "up_bias", "down_w", "down_bias", "cot",
)
OUT_HBM = ("result", "tokens_grad")
IN_HBM = ("up_w", "down_w", "qkv_w", "out_w")
OUTPUTS = {
    "result": ((256, 1024), BF),
    "tokens_grad": ((256, 1024), BF),
    "qkv_grad": ((3, 32, 256), F32),
    "out_grad": ((32, 256), F32),
    "up_grad": ((2, 2, 32, 1024), F32),
    "down_grad": ((2, 2, 32, 1024), F32),
    "sums": ((24, 1024), F32),
}
PART = ((1024, 512), F32)
SQUARE = ((256, 1024), F32)
LOW = ((256, 1024), BF)
SCRATCH = {
    "wqkv": ((3, 1024, 256), BF), "wout": ((256, 1024), BF),
    "wup": ((2, 1024, 1024), BF), "wdn": ((2, 1024, 1024), BF),
    "normed": LOW, "q": ((256, 256), BF), "k": ((256, 256), BF), "v": ((256, 256), BF),
    "mixed": ((256, 256), BF), "probs": ((4, 256, 256), F32),
    "gq": ((256, 256), BF), "gk": ((256, 256), BF), "gv": ((256, 256), BF),
    "hot_s": ((256, 256), BF), "hot_t": ((256, 256), BF),
    "valid": ((256, 1), F32), "filled": ((256, 1), F32), "route": ((256, 1), F32),
    "sig": ((256, 1), F32), "gating": ((256, 1), F32), "segc": ((256, 1), F32),
    "hidden": SQUARE, "rows0": SQUARE, "rows1": SQUARE, "rows2": SQUARE,
    "slope0": SQUARE, "gwork": SQUARE, "grows": SQUARE, "ghidden": SQUARE,
    "n": LOW, "act": LOW, "go": LOW, "gp": LOW,
    "pa": ((4, 256, 256), F32), "lca": ((4, 128, 256), F32), "lxa": ((2, 4, 128, 256), F32),
    "pb": ((4, 256, 256), F32), "lcb": ((4, 128, 256), F32), "lxb": ((4, 128, 256), F32),
    "gs0u": PART, "gs0w": PART, "gs1u": PART, "gs1w": PART,
    "ys": PART, "gy0": PART, "gy1": PART,
    "right": ((512, 512), BF),
    "partu": PART, "partw": PART,
    "l1": ((2, 2, 128, 512), F32), "l2": ((2, 2, 256, 512), F32),
    "lx": ((2, 2, 128, 512), F32), "gates": ((4, 8, 128), F32), "land": ((2, 2, 4, 2, 32, 256), F32),
    "a1": ((2, 2, 128, 384), F32), "a2": ((2, 2, 256, 384), F32),
    "b1": ((2, 32, 256), F32), "b2": ((2, 64, 256), F32), "ax": ((32, 256), F32),
    "gsn": PART, "gyn": ((512, 384), F32), "lxn": ((128, 384), F32), "landn": ((2, 2, 32, 384), F32),
    "vb": ((10, 24, 1024), F32), "low_out": LOW,
}
N_SEMS = 116


class QkvGrads:
    def __init__(self, here, shared, ys, gy, right, part, l1, l2, lx, land, sems):
        self.here, self.shared, self.ys, self.gy, self.right = here, shared, ys, gy, right
        self.part, self.lx, self.land, self.sems = part, lx, land, sems
        self.ring = RingSum(here, "b", part, 0, 256, l1, l2, sems)
        self.stays = here.a // 2 == here.c

    def move(self, grads):
        here, ys, gy, c = self.here, self.ys, self.gy, self.here.c
        for n, g in enumerate(grads):
            ys[:, COLS[n]] = g[...].astype(F32)
        self.k = self.sems.block(1)
        for dc in range(2):
            axis, e = "ab"[dc], (c + dc) % 2
            p = getattr(here, axis)
            spot = gy.at[pl.ds(pl.multiple_of(p * 128, 128), 128)]
            for q in range(2):
                to = 2 * c + q
                block = ys.at[
                    pl.ds(pl.multiple_of(e * 128, 128), 128), q * 384 : q * 384 + 384
                ]

                def send(block=block, spot=spot, to=to, axis=axis, e=e, p=p):
                    self.sems.copy(block, spot, here.ring(axis, to - p + 4, c=e), self.k)

                if dc:
                    send()
                    continue

                def keep(block=block, spot=spot):
                    spot[...] = block[...]

                pl.when(to == p)(keep)
                pl.when(to != p)(send)

    def settle(self, wait, rows):
        view = self.gy
        pl.when(self.stays)(lambda: wait(view.at[pl.ds(0, 3 * rows)]))
        pl.when(here_not(self.stays))(lambda: wait(view.at[pl.ds(0, 4 * rows)]))

    def multiply(self):
        self.shared.arrive()
        self.settle(lambda view: self.sems.all_recv(self.k, view), 128)
        self.right[:, 0:384] = self.gy[...].astype(BF)
        c = self.here.c
        per_y, per_z = 32 + 224 * c, 256 - 224 * c

        def block(k, carry):
            lanes = pl.ds(pl.multiple_of((k % 4) * 128, 128), 128)
            left = [
                self.shared.buf[
                    pl.ds(pl.multiple_of(p * 256 + (k // 4) * 128, 128), 128), lanes
                ].astype(BF)
                for p in range(4)
            ]
            res = tn(jnp.concatenate(left, axis=0), self.right[:, 0:384])
            for z in range(4):
                at = (k // 4) * 128 + (k % 4) * per_y + z * per_z
                self.part[pl.ds(pl.multiple_of(at, 32), 32)] = res[z * 32 : z * 32 + 32]
            return carry

        lax.fori_loop(0, 8, block, 0)
        self.ring.start()

    def across(self):
        here = self.here
        self.ring.arrive()
        away = pl.multiple_of(self.ring.p * 256 + (1 - here.x) * 128, 128)
        self.swap = self.sems.copy(self.part.at[pl.ds(away, 128)], self.lx, here.dev(x=1 - here.x))

    def spread(self):
        here = self.here
        self.swap.wait_recv()
        base = self.ring.p * 256 + here.x * 128
        mine = pl.ds(pl.multiple_of(base, 128), 128)
        self.part[mine] = self.part[mine] + self.lx[...]
        self.k2 = self.sems.block(1)
        p, owner = here.a, here.a // 2
        spot = self.land.at[p % 2, here.c]
        for step in (1, 3, 2, 0):
            block = self.part.at[pl.ds(pl.multiple_of(base + ((p + step) % 4) * 32, 32), 32)]

            def send(block=block, step=step):
                self.sems.copy(block, spot, here.ring("a", step, c=owner), self.k2)

            if step:
                send()
                continue

            def keep(block=block):
                spot[...] = block[...]

            pl.when(self.stays)(keep)
            pl.when(here_not(self.stays))(send)

    def finish(self, out):
        self.settle(lambda view: self.sems.all_recv(self.k2, view), 32)
        left, right = (self.land[half, 0] + self.land[half, 1] for half in range(2))
        out[0] = left[:, 0:256]
        out[1, :, 0:128] = left[:, 256:384]
        out[1, :, 128:256] = right[:, 0:128]
        out[2] = right[:, 128:384]

    def done(self):
        self.settle(lambda view: self.sems.all_sent(self.k, view), 128)
        self.settle(lambda view: self.sems.all_sent(self.k2, view), 32)
        self.swap.wait_send()
        self.ring.done()


class Totals:
    def __init__(self, here, buf, sems):
        self.here, self.buf, self.sems, self.cps, self.wait = here, buf, sems, [], []

    def send(self, at, to, devices):
        spots = self.buf.at[at], self.buf.at[to]
        self.wait = [self.sems.copy(*spots, dev) for dev in devices]
        self.cps += self.wait

    def four(self, at):
        for cp in self.wait:
            cp.wait_recv()
        buf = self.buf
        return (buf[at] + buf[at + 1]) + (buf[at + 2] + buf[at + 3])

    def ring_y(self):
        at = 1 + self.here.y
        self.buf[at] = self.buf[0]
        self.send(at, at, [self.here.ring("y", step) for step in (1, 3, 2)])

    def ring_z(self):
        at = 5 + self.here.z
        self.buf[at] = self.four(1)
        self.send(at, at, [self.here.ring("z", step) for step in (1, 3, 2)])

    def pair(self):
        self.buf[0] = self.four(5)
        self.send(0, 9, [self.here.dev(x=1 - self.here.x)])

    def finish(self, out):
        self.wait[0].wait_recv()
        out[...] = self.buf[0] + self.buf[9]

    def done(self):
        for cp in self.cps:
            cp.wait_send()


class Bag:
    pass


def two(ref):
    return [ref.at[0], ref.at[1]]


def layer_kernel(*refs):
    B = Bag()
    for name, ref in zip([*INPUTS, *OUTPUTS, *SCRATCH, "ss", "rs", "ws", "free"], refs):
        setattr(B, name, ref)
    B.n0 = B.n1 = B.gbranch = B.n
    B.act0 = B.act1 = B.act
    B.go0 = B.go1 = B.go
    B.gp0 = B.gp1 = B.gp
    here = Here()
    sems = Sems(B.ss, B.rs)
    x, c = here.x, here.c
    vec = B.vb.at[0]
    even = [sems.block(4) for _ in range(3)]
    odd = [even[0], sems.block(4), even[2]]

    peers = [here.dev(c=1 - c), here.dev(h=1 - here.h), here.dev(x=1 - x)]
    for axis in ("y", "z"):
        for step in (1, 2, 3):
            for dc in range(2):
                peers.append(here.ring(axis, step, c=(c + dc) % 2))
    bar = pltpu.get_barrier_semaphore()
    for dev in peers:
        pl.semaphore_signal(bar, inc=1, device_id=dev, device_id_type=MESH)

    def fetch(pairs, at):
        cps = [pltpu.make_async_copy(s, t, B.ws.at[at + k]) for k, (s, t) in enumerate(pairs)]
        for cp in cps:
            cp.start()
        return cps

    def fetch_experts(j):
        return fetch(
            [(B.up_w.at[e, j], B.wup.at[e]) for e in range(2)]
            + [(B.down_w.at[e, j], B.wdn.at[e]) for e in range(2)],
            2,
        )

    heads = fetch([(B.qkv_w, B.wqkv), (B.out_w, B.wout)], 0)
    experts = fetch_experts(0)

    B.vb[0] = jnp.zeros((24, 1024), F32)
    lane1024 = lax.broadcasted_iota(jnp.int32, (1, 1024), 1)

    def stat(k, total):
        row = jnp.where(lane1024 == k, total, 0.0)
        vec[STATS : STATS + 1] = vec[STATS : STATS + 1] + row

    def total(v):
        return jnp.sum(jnp.sum(v, axis=1, keepdims=True), axis=0, keepdims=True)

    down_i = lax.broadcasted_iota(jnp.int32, (256, 256), 0)
    along_i = lax.broadcasted_iota(jnp.int32, (256, 256), 1)

    def column(row):
        return jnp.sum(jnp.where(down_i == along_i, row, 0.0), axis=1, keepdims=True)

    seg_row = B.seg[...].astype(F32)
    B.segc[...] = column(seg_row)
    B.valid[...] = (B.segc[...] != 0.0).astype(F32)

    def allowed():
        return (B.segc[...] == seg_row) & (along_i <= down_i) & (B.segc[...] != 0.0)

    head_of = along_i // HD

    gain = B.ln_gain[...].astype(F32).reshape(1, 1024)
    shift = B.ln_shift[...].astype(F32).reshape(1, 1024)

    def norm_block(i, carry):
        n, _ = unit(B.tok[rows32(i)].astype(F32))
        B.normed[rows32(i)] = (n * gain + shift).astype(BF)
        return carry

    lax.fori_loop(0, 8, norm_block, 0, unroll=2)
    for cp in heads:
        cp.wait()
    qv_bias = B.qv_bias[...].astype(F32)
    B.q[...] = (nn(B.normed[...], B.wqkv[0]) + qv_bias[0:1]).astype(BF)
    B.k[...] = nn(B.normed[...], B.wqkv[1]).astype(BF)
    B.v[...] = (nn(B.normed[...], B.wqkv[2]) + qv_bias[1:2]).astype(BF)

    def one_head(value, hh):
        return jnp.where(head_of == hh, value.astype(F32), 0.0)

    mixed = jnp.zeros((256, 256), F32)
    for hh in range(4):
        s = nt(one_head(B.q[...], hh).astype(BF), B.k[...]) * SCALE
        ok = allowed()
        s = jnp.where(ok, s, -1e30)
        e = jnp.where(ok, jnp.exp(s - jnp.max(s, axis=-1, keepdims=True)), 0.0)
        probs = e / (jnp.sum(e, axis=-1, keepdims=True) + (1.0 - B.valid[...]))
        B.probs[hh] = probs
        mixed = mixed + one_head(nn(probs.astype(BF), B.v[...]), hh)
    B.mixed[...] = mixed.astype(BF)

    pl.semaphore_wait(bar, len(peers))
    sn = Shared(here, "a", B.gsn, sems).start(B.normed)
    branch = TensorSum(here, sems, B.pa, B.lca, B.lxa.at[0], B.hidden, even)
    branch.send(lambda n: nn(B.mixed[...], B.wout[:, COLS[n]]))
    slot_row = jnp.concatenate([B.slots[0, 0:1], B.slots[0, 1:2]], axis=1)
    slot_col = column(slot_row.astype(F32))
    B.hot_s[...] = jnp.where(slot_col == along_i.astype(F32), 1.0, 0.0).astype(BF)
    for n in range(4):
        B.grows[:, COLS[n]] = nn(B.hot_s[...], B.cot[:, COLS[n]])
    s1w = Shared(here, "b", B.gs1w, sems).start(B.grows)
    B.route[...] = column(B.routes[...].astype(F32))
    B.filled[...] = (slot_col < 256.0).astype(F32)
    B.hot_t[...] = jnp.where(slot_row == down_i, 1.0, 0.0).astype(BF)
    stat(4, total(B.valid[...]))
    for n in range(2):
        branch.third(n)
    sn.relay()
    branch.third(2)
    s1w.relay()
    branch.end()

    out_bias = B.out_bias[...].astype(F32).reshape(1, 1024)
    cent = B.cent[...].astype(F32)

    def hidden_block(i, carry):
        rows = rows32(i)
        h = B.tok[rows].astype(F32) + (B.hidden[rows] + out_bias)
        B.hidden[rows] = h
        scores = [jnp.sum(h * cent[e : e + 1], axis=-1, keepdims=True) for e in range(2)]
        logits = jnp.where(B.route[rows] == 1.0, scores[1], scores[0])
        sig = 1.0 / (1.0 + jnp.exp(-logits))
        B.sig[rows] = sig
        B.gating[rows] = sig * B.valid[rows]
        return carry + fold(h * h * B.valid[rows])

    stat(0, total(lax.fori_loop(0, 8, hidden_block, jnp.zeros((8, 1024), F32), unroll=2)))
    for n in range(4):
        B.rows0[:, COLS[n]] = pick(B.hot_s[...], B.hidden[:, COLS[n]])
    ffn_gain = B.ffn_gain[...].astype(F32)
    ffn_shift = B.ffn_shift[...].astype(F32)
    up_bias = B.up_bias[...].astype(F32)
    down_bias = B.down_bias[...].astype(F32)

    def expert_norm(rows_ref, low_ref, j):
        for e in range(2):
            g, s = ffn_gain[e, j : j + 1], ffn_shift[e, j : j + 1]

            def block(i, carry, e=e, g=g, s=s):
                rows = rows32(e * 4 + i)
                n, _ = unit(rows_ref[rows])
                low_ref[rows] = (n * g + s).astype(BF)
                return carry

            lax.fori_loop(0, 4, block, 0, unroll=2)

    def gelu_parts(v):
        t = jnp.tanh(ROOT * (v + 0.044715 * (v * v * v)))
        cdf = 0.5 * (1.0 + t)
        slope = cdf + (0.5 * ROOT) * v * (1.0 - t * t) * (1.0 + (3.0 * 0.044715) * (v * v))
        return v * cdf, slope

    def half(e):
        return pl.ds(e * 128, 128)

    expert_norm(B.rows0, B.n0, 0)
    s0u = Shared(here, "a", B.gs0u, sems).start(B.n0)
    for cp in experts:
        cp.wait()
    for e in range(2):
        for n in range(4):
            pre = nn(B.n0[half(e)], B.wup[e, :, COLS[n]]) + up_bias[e, 0:1, n * 256 : n * 256 + 256]
            act, slope = gelu_parts(pre)
            B.act0[half(e), COLS[n]] = act.astype(BF)
            B.slope0[half(e), COLS[n]] = slope

    def down(act_ref):
        def make(n):
            return jnp.concatenate(
                [nn(act_ref[half(e)], B.wdn[e, :, COLS[n]]) for e in range(2)], axis=0
            )

        return make

    first = TensorSum(here, sems, B.pa, B.lca, B.lxa.at[1], B.rows1, odd)
    first.send(down(B.act0))
    experts = fetch_experts(1)
    m0w = Moved(here, "b", 256, B.ys, B.gy0, sems).start(B.act0)
    gate_row = down_rows(B.hot_t[...].astype(F32) * B.gating[...])
    gate_col = column(gate_row)
    B.gates[here.b] = jnp.broadcast_to(jnp.where(c == 0, gate_row[:, :128], gate_row[:, 128:]), (8, 128))
    mine = B.gates.at[here.b]
    gate_cps = [sems.copy(mine, mine, here.ring("b", step)) for step in (1, 3, 2)]
    for n in range(4):
        g = gate_col * B.grows[:, COLS[n]]
        B.grows[:, COLS[n]] = g
        B.go1[:, COLS[n]] = g.astype(BF)
    for e in range(2):
        vec[DOWN_B + e * 2 + 1 : DOWN_B + e * 2 + 2] = down_rows(B.go1[half(e)].astype(F32))
    for cp in experts:
        cp.wait()
    for e in range(2):
        for n in range(4):
            B.gwork[half(e), COLS[n]] = nt(B.go1[half(e)], B.wdn[e, COLS[n], :])
    for n in range(3):
        first.third(n)
    s0u.relay()
    first.end()

    sq = jnp.zeros((8, 1024), F32)
    for e in range(2):
        bias = down_bias[e, 0:1]

        def rows1_block(i, carry, e=e, bias=bias):
            rows = rows32(e * 4 + i)
            r1 = B.rows0[rows] + (B.rows1[rows] + bias)
            B.rows1[rows] = r1
            return carry + fold(r1 * r1 * B.filled[rows])

        sq = lax.fori_loop(0, 4, rows1_block, sq, unroll=2)
    stat(1, total(sq))
    expert_norm(B.rows1, B.n1, 1)
    s1u = Shared(here, "a", B.gs1u, sems).start(B.n1)
    for e in range(2):
        for n in range(4):
            pre = nn(B.n1[half(e)], B.wup[e, :, COLS[n]]) + up_bias[e, 1:2, n * 256 : n * 256 + 256]
            act, slope = gelu_parts(pre)
            B.act1[half(e), COLS[n]] = act.astype(BF)
            gp = (B.gwork[half(e), COLS[n]] * slope).astype(BF)
            B.gp1[half(e), COLS[n]] = gp
            vec[UP_B + e * 2 + 1 : UP_B + e * 2 + 2, COLS[n]] = down_rows(gp.astype(F32))

    def normed_grad(gp_ref):
        def make(n):
            return jnp.concatenate(
                [nt(gp_ref[half(e)], B.wup[e, COLS[n], :]) for e in range(2)], axis=0
            )

        return make

    back1 = TensorSum(here, sems, B.pa, B.lca, B.lxa.at[0], B.gwork, even)
    back1.send(normed_grad(B.gp1))
    m1u = Moved(here, "a", 0, B.ys, B.gy1, sems).start(B.gp1)
    second = TensorSum(here, sems, B.pb, B.lcb, B.lxb, B.rows2, [sems.block(4) for _ in range(3)])
    second.send(down(B.act1))
    experts = fetch_experts(0)
    m0w.sent()
    m1w = Moved(here, "b", 256, B.ys, B.gy1, sems).start(B.act1)
    back1.end()

    def expert_norm_back(rows_ref, j, go_ref):
        for e in range(2):
            g = ffn_gain[e, j : j + 1]

            def block(i, carry, e=e, g=g):
                rows = rows32(e * 4 + i)
                n, r = unit(rows_ref[rows])
                gn = B.gwork[rows]
                new = B.grows[rows] + unit_back(gn, g, n, r)
                B.grows[rows] = new
                out = [carry[0] + fold(gn * n), carry[1] + fold(gn)]
                if go_ref is not None:
                    low = new.astype(BF)
                    go_ref[rows] = low
                    out.append(carry[2] + fold(low.astype(F32)))
                return tuple(out)

            zero = jnp.zeros((8, 1024), F32)
            sums = lax.fori_loop(0, 4, block, (zero,) * (2 if go_ref is None else 3), unroll=2)
            at = e * 2 + j
            vec[GAIN + at : GAIN + at + 1] = down_rows(sums[0])
            vec[SHIFT + at : SHIFT + at + 1] = down_rows(sums[1])
            if go_ref is not None:
                vec[DOWN_B + e * 2 : DOWN_B + e * 2 + 1] = down_rows(sums[2])

    expert_norm_back(B.rows1, 1, B.go0)
    s0w = Shared(here, "b", B.gs0w, sems).start(B.go0)
    for cp in experts:
        cp.wait()
    for e in range(2):
        for n in range(4):
            ga = nt(B.go0[half(e)], B.wdn[e, COLS[n], :])
            gp = (ga * B.slope0[half(e), COLS[n]]).astype(BF)
            B.gp0[half(e), COLS[n]] = gp
            vec[UP_B + e * 2 : UP_B + e * 2 + 1, COLS[n]] = down_rows(gp.astype(F32))
    back0 = TensorSum(here, sems, B.pa, B.lca, B.lxa.at[1], B.gwork, odd)
    back0.send(normed_grad(B.gp0))
    state = {}
    def slot_gates():
        for cp in gate_cps:
            cp.wait_recv()
        eye = down_i[:128, :128] == along_i[:128, :128]
        return [
            jnp.sum(jnp.where(eye, B.gates[p, 0:1], 0.0), axis=1, keepdims=True) for p in range(4)
        ]

    eg1 = [
        ExpertGrads(here, m, (s1u, s1w)[m], (m1u, m1w)[m], B.right, (B.partu, B.partw)[m],
                    two(B.l1.at[m]), two(B.l2.at[m]), B.lx.at[0, m], B.land.at[0, m], sems,
                    gates=(None, slot_gates)[m])
        for m in range(2)
    ]
    m0u = Moved(here, "a", 0, B.ys, B.gy0, sems)
    wide = [pl.ds(0, 512), pl.ds(512, 512)]
    eg0 = [
        ExpertGrads(here, m, (s0u, s0w)[m], (m0u, m0w)[m], B.right, (B.ys, B.gy1)[m],
                    [B.slope0.at[pl.ds(128 * k, 128), wide[m]] for k in range(2)],
                    [(B.hidden, B.rows2)[m].at[:, wide[k]] for k in range(2)],
                    B.lx.at[1, m], B.land.at[1, m], sems)
        for m in range(2)
    ]
    low, few = pl.ds(0, 256), pl.ds(0, 384)
    apart = (None, B.gs1w.at[:, low])
    qkv = QkvGrads(
        here, sn, B.rows0, B.gyn, B.right, B.gs1u.at[:, few],
        two(B.a1.at[0]), two(B.a2.at[0]), B.lxn, B.landn, sems,
    )
    rings, rings2, swaps = {}, {}, {}
    gather = Totals(here, B.vb, sems)

    def move_gp0():
        m1u.sent()
        m0u.start(B.gp0)

    def result():
        sq = jnp.zeros((8, 1024), F32)
        for e in range(2):
            bias = down_bias[e, 1:2]

            def rows2_block(i, carry, e=e, bias=bias):
                rows = rows32(e * 4 + i)
                r2 = B.rows1[rows] + (B.rows2[rows] + bias)
                B.rows2[rows] = r2
                return carry + fold(r2 * r2 * B.filled[rows])

            sq = lax.fori_loop(0, 4, rows2_block, sq, unroll=2)
        stat(2, total(sq))
        gate_grad = jnp.zeros((256, 1), F32)
        result_sq = jnp.zeros((256, 1), F32)
        for n in range(4):
            comb = pick(B.hot_t[...], B.rows2[:, COLS[n]])
            res = B.hidden[:, COLS[n]] + B.gating[...] * comb
            B.low_out[:, COLS[n]] = res.astype(BF)
            result_sq = result_sq + jnp.sum(res * res, axis=-1, keepdims=True)
            gate_grad = gate_grad + jnp.sum(B.cot[:, COLS[n]].astype(F32) * comb, axis=-1, keepdims=True)
        state["out"] = pltpu.make_async_copy(B.low_out, B.result, B.ws.at[0])
        state["out"].start()
        stat(3, total(result_sq * B.valid[...]))
        B.gating[...] = gate_grad * B.sig[...] * (1.0 - B.sig[...]) * B.valid[...]

        def gate_block(i, carry):
            rows = rows32(i)
            gl, second_route = B.gating[rows], B.route[rows] == 1.0
            B.ghidden[rows] = B.cot[rows].astype(F32) + gl * jnp.where(second_route, cent[1:2], cent[0:1])
            v = gl * B.hidden[rows]
            return (
                carry[0] + fold(jnp.where(second_route, 0.0, v)),
                carry[1] + fold(jnp.where(second_route, v, 0.0)),
            )

        zero = jnp.zeros((8, 1024), F32)
        sums = lax.fori_loop(0, 8, gate_block, (zero, zero), unroll=2)
        for e in range(2):
            vec[CENT + e : CENT + e + 1] = down_rows(sums[e])
        for k, axis in enumerate(("b", "a")):
            for step in (1, 3):
                pl.semaphore_signal(
                    B.free.at[k], inc=1, device_id=here.ring(axis, step), device_id_type=MESH
                )

    def attention_back():
        expert_norm_back(B.rows0, 0, None)
        for n in range(4):
            g = B.ghidden[:, COLS[n]] + pick(B.hot_t[...], B.grows[:, COLS[n]])
            B.ghidden[:, COLS[n]] = g
            low = g.astype(BF)
            B.gbranch[:, COLS[n]] = low
            vec[OUT_BIAS : OUT_BIAS + 1, COLS[n]] = down_rows(low.astype(F32))
        gm = nt(B.gbranch[...], B.wout[...]).astype(BF)
        gq = jnp.zeros((256, 256), F32)
        gk = jnp.zeros((256, 256), F32)
        gv = jnp.zeros((256, 256), F32)
        for hh in range(4):
            probs = B.probs[hh]
            gp = nt(one_head(gm, hh).astype(BF), B.v[...])
            gv = gv + one_head(tn(probs.astype(BF), gm), hh)
            gs = (probs * (gp - jnp.sum(probs * gp, axis=-1, keepdims=True))).astype(BF)
            gq = gq + one_head(nn(gs, B.k[...]), hh)
            gk = gk + one_head(tn(gs, B.q[...]), hh)
        B.gq[...] = (gq * SCALE).astype(BF)
        B.gk[...] = (gk * SCALE).astype(BF)
        B.gv[...] = gv.astype(BF)
        vec[QV_B : QV_B + 1, 0:256] = down_rows(B.gq[...].astype(F32))
        vec[QV_B : QV_B + 1, 256:512] = down_rows(B.gv[...].astype(F32))
        state["back"] = back = TensorSum(here, sems, B.pa, B.lca, B.lxa.at[0], B.gwork, even)
        grads = (B.gq, B.gk, B.gv)
        back.send(lambda n: sum(nt(grads[s][...], B.wqkv[s, COLS[n], :]) for s in range(3)))


    def first_sublayer(m):
        if m == 0:
            m1w.sent()
            m0u.sent()
        pl.semaphore_wait(B.free.at[m], 2)
        eg0[m].multiply()

    def qkv_multiply():
        s1u.done()
        qkv.multiply()

    def attention_grads(m):
        s1w.done()
        last_y = (m + c) % 2

        def block(k, carry):
            lanes = pl.ds(pl.multiple_of(k * 128, 128), 128)
            res = tn(B.gbranch[:, lanes], B.mixed[...])
            for z in range(4):
                at = (k // 4) * 32 + (k % 4) * (256 - 192 * last_y) + z * (64 + 192 * last_y)
                apart[m][pl.ds(pl.multiple_of(at, 32), 32)] = res[z * 32 : z * 32 + 32]
            return carry

        lax.fori_loop(0, 8, block, 0)
        l1 = [B.a1.at[m, k, :, low] for k in range(2)]
        l2 = [B.a2.at[m, k, :, low] for k in range(2)]
        rings[m] = RingSum(here, "ab"[m], apart[m], 0, 256, l1, l2, sems)
        rings[m].start()

    def tokens_back():
        state["back"].end()
        state["out"].wait()
        zero = jnp.zeros((8, 1024), F32)

        def last_block(i, carry):
            rows = rows32(i)
            n, r = unit(B.tok[rows].astype(F32))
            gn = B.gwork[rows]
            B.low_out[rows] = (B.ghidden[rows] + unit_back(gn, gain, n, r)).astype(BF)
            return carry[0] + fold(gn * n), carry[1] + fold(gn)

        sums = lax.fori_loop(0, 8, last_block, (zero, zero), unroll=2)
        vec[LN_GAIN : LN_GAIN + 1] = down_rows(sums[0])
        vec[LN_SHIFT : LN_SHIFT + 1] = down_rows(sums[1])
        state["out"] = pltpu.make_async_copy(B.low_out, B.tokens_grad, B.ws.at[0])
        state["out"].start()
        gather.ring_y()

    def second_ring(m):
        rings[m].arrive()
        base = rings[m].p * 256
        b1, b2 = two(B.b1), two(B.b2)
        rings2[m] = RingSum(here, "ba"[m], apart[m], base, 64, b1, b2, sems)
        rings2[m].start()

    def attention_swap(m):
        rings2[m].arrive()
        base = rings2[m].base + rings2[m].p * 64
        away = pl.ds(pl.multiple_of(base + (1 - x) * 32, 32), 32)
        swaps[m] = sems.copy(apart[m].at[away], B.ax, here.dev(x=1 - x))

    def attention_out(m):
        swaps[m].wait_recv()
        base = rings2[m].base + rings2[m].p * 64
        B.out_grad[...] = apart[m][pl.ds(pl.multiple_of(base + x * 32, 32), 32)] + B.ax[...]

    s1u.relay()
    s0w.relay()
    eg1[1].multiply()
    back0.third(0)
    eg1[0].multiply()
    move_gp0()
    second.end()
    result()
    back0.third(1)
    first_sublayer(1)
    eg1[0].ring.middle()
    eg1[1].ring.middle()
    back0.third(2)
    back0.end()
    attention_back()
    first_sublayer(0)
    qkv.move((B.gq, B.gk, B.gv))
    eg1[0].across()
    state["back"].third(0)
    state["back"].third(1)
    eg1[1].across()
    state["back"].third(2)
    eg0[1].ring.middle()
    tokens_back()
    eg0[0].ring.middle()
    qkv_multiply()
    eg0[1].across()
    attention_grads(1)
    gather.ring_z()
    eg0[0].across()
    qkv.ring.middle()
    rings[1].middle()
    eg1[1].spread()
    eg0[1].spread()
    qkv.across()
    second_ring(1)
    eg1[0].spread()
    eg1[1].finish((B.up_grad, B.down_grad)[1], 1)
    gather.pair()
    rings2[1].middle()
    eg0[0].spread()
    eg1[0].finish((B.up_grad, B.down_grad)[0], 1)
    qkv.spread()
    eg0[1].finish((B.up_grad, B.down_grad)[1], 0)
    attention_swap(1)
    qkv.finish(B.qkv_grad)
    eg0[0].finish((B.up_grad, B.down_grad)[0], 0)
    gather.finish(B.sums)
    attention_out(1)
    state["out"].wait()
    assert sems.n == N_SEMS, sems.n
    for job in (sn, s0u, s0w, gather, qkv, *rings.values(), *rings2.values()):
        job.done()
    for cp in [*swaps.values(), *gate_cps]:
        cp.wait_send()


def finish_kernel(*refs):
    big_in, sums, big_out = refs[:6], refs[6], refs[7:13]
    gain, shift, out_b, cent, ffn_g, ffn_s, down_b, up_b, qv_b, rms, sem = refs[13:]
    cps = [pltpu.make_async_copy(a, b, sem.at[k]) for k, (a, b) in enumerate(zip(big_in, big_out))]
    for cp in cps:
        cp.start()
    d = lax.axis_index("dp")
    near = sums[:, pl.ds(pl.multiple_of((d // 4) * 128, 128), 128)]
    share = near[:, :32]
    for k in range(1, 4):
        share = jnp.where(d % 4 == k, near[:, k * 32 : k * 32 + 32], share)
    for ref, at in ((gain, LN_GAIN), (shift, LN_SHIFT), (out_b, OUT_BIAS)):
        ref[...] = share[at : at + 1]
    cent[...] = share[CENT : CENT + 2]
    for ref, at in ((ffn_g, GAIN), (ffn_s, SHIFT), (down_b, DOWN_B)):
        for e in range(2):
            ref[e] = share[at + e * 2 : at + e * 2 + 2]
    for e in range(2):
        up_b[e] = sums[UP_B + e * 2 : UP_B + e * 2 + 2]
    qv_b[0:1] = sums[QV_B : QV_B + 1, 0:256]
    qv_b[1:2] = sums[QV_B : QV_B + 1, 256:512]
    totals = sums[STATS : STATS + 1, 0:128]
    rms[...] = jnp.sqrt(totals[:, :4] / (totals[:, 4:5] * 1024.0))
    for cp in cps:
        cp.wait()


SMALL = [(1, 32), (1, 32), (1, 32), (2, 32), (2, 2, 32), (2, 2, 32), (2, 2, 32), (2, 2, 1024), (2, 256), (1, 4)]


def local(
    tokens, segments, routes, slot_table, ln_gain, ln_shift, qkv_proj, qv_bias, out_proj, out_bias,
    centroids, ffn_gain, ffn_shift, up_proj, up_bias, down_proj, down_bias, cotangent,
):
    in_specs = [
        pl.BlockSpec(memory_space=pl.ANY if name in IN_HBM else VM) for name in INPUTS
    ]
    outs = pl.pallas_call(
        layer_kernel,
        out_shape=tuple(jax.ShapeDtypeStruct(*spec) for spec in OUTPUTS.values()),
        in_specs=in_specs,
        out_specs=[
            pl.BlockSpec(memory_space=pl.ANY if name in OUT_HBM else VM) for name in OUTPUTS
        ],
        scratch_shapes=[VM(*spec) for spec in SCRATCH.values()]
        + [pltpu.SemaphoreType.DMA((N_SEMS,)), pltpu.SemaphoreType.DMA((N_SEMS,)), pltpu.SemaphoreType.DMA((6,)), pltpu.SemaphoreType.REGULAR((2,))],
        compiler_params=pltpu.CompilerParams(
            collective_id=0, has_side_effects=True, vmem_limit_bytes=VMEM_LIMIT
        ),
    )(
        tokens, segments.reshape(1, 256), routes.reshape(1, 256), slot_table,
        ln_gain, ln_shift, qkv_proj, qv_bias, out_proj,
        out_bias, centroids, ffn_gain, ffn_shift, up_proj, up_bias, down_proj,
        down_bias, cotangent,
    )
    anywhere = pl.BlockSpec(memory_space=pl.ANY)
    near = pl.BlockSpec(memory_space=VM)
    (
        result, tokens_grad, qkv_grad, out_grad, up_grad, down_grad,
        gain, shift, out_b, cent, ffn_g, ffn_s, down_b, up_b, qv_b, rms,
    ) = pl.pallas_call(
        finish_kernel,
        out_shape=tuple(jax.ShapeDtypeStruct(a.shape, a.dtype) for a in outs[:6])
        + tuple(jax.ShapeDtypeStruct(shape, F32) for shape in SMALL),
        in_specs=[near] * 7,
        out_specs=[anywhere] * 6 + [near] * len(SMALL),
        scratch_shapes=[pltpu.SemaphoreType.DMA((6,))],
    )(*outs)
    return (
        result,
        tokens_grad,
        gain.reshape(32),
        shift.reshape(32),
        qkv_grad,
        qv_b,
        out_grad.T,
        out_b.reshape(32),
        cent,
        ffn_g,
        ffn_s,
        up_grad,
        up_b,
        jnp.swapaxes(down_grad, 2, 3),
        down_b,
        rms.reshape(4),
    )


VMEM_LIMIT = 63 * 2**20


def solution(mesh):
    return jax.shard_map(
        local,
        mesh=mesh,
        in_specs=(
            P("dp", None),
            P("dp"),
            P("dp"),
            P("dp", None, None),
            P(),
            P(),
            P(None, None, "tensor"),
            P(None, "tensor"),
            P("tensor", None),
            P(),
            P(),
            P(),
            P(),
            P(None, None, None, "tensor"),
            P(None, None, "tensor"),
            P(None, None, "tensor", None),
            P(),
            P("dp", None),
        ),
        out_specs=(
            P("dp", None),
            P("dp", None),
            P("dp"),
            P("dp"),
            P(None, "dp", "tensor"),
            P(None, "tensor"),
            P("tensor", "dp"),
            P("dp"),
            P(None, "dp"),
            P(None, None, "dp"),
            P(None, None, "dp"),
            P(None, None, "dp", "tensor"),
            P(None, None, "tensor"),
            P(None, None, "tensor", "dp"),
            P(None, None, "dp"),
            P(),
        ),
        check_vma=False,
    )
```
